512 devices in a mesh: gx: 128 (over x, z, y_lo, core), gy: 4 (over y_hi).
Axes of the slice: x: 4, y: 8 (y_hi: 4, y_lo: 2; y = y_hi * 2 + y_lo), z: 8, core: 2. Of those that a mesh axis runs over, the one named last changes fastest.
Arguments:
- displacement: float32 [3, 3, 4096, 512], P(None, None, 'gx', 'gy'), may hold values from -6 to 6
- previous: float32 [3, 3, 4096, 512], P(None, None, 'gx', 'gy'), may hold values from -6 to 6
- moduli: float32 [2, 3, 4096, 512], P(None, None, 'gx', 'gy'), may hold values from 0.5 to 2
- density: float32 [3, 4096, 512], P(None, 'gx', 'gy'), may hold values from 0.5 to 2
- bins: float32 [2, 3, 2, 4096, 512], P(None, None, None, 'gx', 'gy'), may hold values from -6 to 6
- omega: float32 [2], replicated, may hold values from 0.1 to 1
- phase: float32 [2], replicated, may hold values from -3.140625 to 3.140625
Outputs:
- updated: float32 [3, 3, 4096, 512], P(None, None, 'gx', 'gy')
- middle: float32 [3, 3, 4096, 512], P(None, None, 'gx', 'gy')
- spectrum: float32 [2, 3, 2, 4096, 512], P(None, None, None, 'gx', 'gy')
The draws below stay inside these ranges and needn't reach their ends.
All inputs are finite; a program needn't handle non-finite values.
Results may differ from the reference program's by a relative error of at most 0.0001.
Values sent between devices are 32-bit elements; how exact they have to be, the bound alone decides.
No kernel may reach another device: no remote copies, remote signals or barrier semaphores. Data moves between devices by JAX's collectives and lax.ppermute only.
A program may use at most 64 MiB of HBM per device.

```python
import math
import jax
import jax.numpy as jnp
from jax import lax

CX = 16
BINS = 2
NXN = 4096
NYN = 512
NZN = 3
N_GX = 128


def block_scale(own_key, dims, cuts, least, high):
    def one(dim, blocks):
        heights = jax.random.uniform(jax.random.fold_in(jax.random.fold_in(own_key, 6), dim), (blocks,), jnp.float32, least / len(cuts), high / len(cuts))
        return jnp.repeat(jnp.exp(heights), dims[dim] // blocks).reshape((-1,) + (1,) * (len(dims) - dim - 1))

    factor_of = one(*cuts[0])
    for cut in cuts[1:]:
        factor_of = factor_of * one(*cut)
    return factor_of


def centred(own_key, shape, width, most, split=(), kind=jnp.bfloat16):
    gain = block_scale(own_key, shape, split, -0.22, 0.18) if split else 1.0
    result = jax.random.normal(own_key, shape, jnp.float32) * width * gain
    return jnp.minimum(jnp.maximum(result, -most), most).astype(kind)


def setup_inputs(seed: int = 0) -> dict:
    keys = jax.random.split(jax.random.key(seed), 8)
    displacement = centred(keys[0], (3, NZN, NXN, NYN), 1.0, 6.0, ((2, 128), (3, 4)), jnp.float32)
    previous = centred(keys[1], (3, NZN, NXN, NYN), 1.0, 6.0, ((2, 128), (3, 4)), jnp.float32)
    moduli = jnp.clip(jnp.exp(math.log(2.0) - 1.3862944 * jax.random.uniform(keys[2], (2, NZN, NXN, NYN), jnp.float32) ** block_scale(keys[2], (2, NZN, NXN, NYN), ((2, 128), (3, 4)), -0.2, 0.2)), 0.5, 2.0)
    density = jnp.clip(jnp.exp(math.log(2.0) - 1.3862944 * jax.random.uniform(keys[3], (NZN, NXN, NYN), jnp.float32) ** block_scale(keys[3], (NZN, NXN, NYN), ((1, 128), (2, 4)), -0.2, 0.2)), 0.5, 2.0)
    bins = centred(keys[4], (BINS, 3, 2, NXN, NYN), 1.0, 6.0, ((3, 128), (4, 4)), jnp.float32)
    omega = jnp.clip(jnp.exp(jax.random.uniform(keys[5], (BINS,), jnp.float32, math.log(0.1), math.log(1.0))), 0.1, 1.0)
    phase = jnp.clip(jax.random.uniform(keys[6], (BINS,), jnp.float32, -3.140625, 3.140625), -3.140625, 3.140625)
    return {"displacement": displacement, "previous": previous, "moduli": moduli, "density": density, "bins": bins, "omega": omega, "phase": phase}


derivative_table = ((-1.5, 2.0, -0.5), (-0.5, 0.0, 0.5), (0.5, -2.0, 1.5))
quadrature_weights = (1.0 / 3.0, 4.0 / 3.0, 1.0 / 3.0)
time_step = 0.03

def nodes_of_elements(values, along):
    length = (values.shape[along] - 1) // 2
    return jnp.stack([lax.slice_in_dim(values, local_node, local_node + 2 * length - 1, stride=2, axis=along) for local_node in range(3)], axis=0)

def assemble(local, along):
    leading = local[0]
    length = leading.shape[along]
    edge_shape = list(leading.shape)
    edge_shape[along] = 1
    zero_edge = jnp.zeros(edge_shape, leading.dtype)
    vertex_sum = jnp.concatenate([leading, zero_edge], along) + jnp.concatenate([zero_edge, local[2]], along)
    paired = jnp.stack([lax.slice_in_dim(vertex_sum, 0, length, axis=along), local[1]], axis=along + 1)
    merged_shape = list(leading.shape)
    merged_shape[along] = 2 * length
    merged = paired.reshape(merged_shape)
    return jnp.concatenate([merged, lax.slice_in_dim(vertex_sum, length, length + 1, axis=along)], along)

def to_elements(values):
    values = nodes_of_elements(values, 3)
    values = nodes_of_elements(values, 3)
    values = nodes_of_elements(values, 3)
    return values.reshape(values.shape[:5] + (values.shape[5] * values.shape[6],))

def stiffness_apply(field, moduli):
    shape_x = (field.shape[2] - 1) // 2
    shape_y = (field.shape[3] - 1) // 2
    shape_z = (field.shape[1] - 1) // 2
    nodal_values = to_elements(field)
    moduli_el = to_elements(moduli)
    lame_first = moduli_el[:, :, :, 0]
    shear_modulus = moduli_el[:, :, :, 1]
    derivative = jnp.array(derivative_table, jnp.float32)
    highest = lax.Precision.HIGHEST
    grad_x = 2.0 * jnp.einsum('pq,kqbcel->kpbcel', derivative, nodal_values, precision=highest)
    grad_y = 2.0 * jnp.einsum('pq,kaqcel->kapcel', derivative, nodal_values, precision=highest)
    grad_z = 2.0 * jnp.einsum('pq,qabcel->pabcel', derivative, nodal_values, precision=highest)
    gradients = (grad_x, grad_y, grad_z)
    volume_strain = grad_x[:, :, :, 0] + grad_y[:, :, :, 1] + grad_z[:, :, :, 2]
    weight_line = jnp.array(quadrature_weights, jnp.float32)
    point_weights = (weight_line[:, None, None] * weight_line[None, :, None] * weight_line[None, None, :] / 8.0)[:, :, :, None, None]
    components = []
    for comp in range(3):
        total_force = None
        for direction in range(3):
            stress = shear_modulus * (gradients[direction][:, :, :, comp] + gradients[comp][:, :, :, direction])
            if comp == direction:
                stress = stress + lame_first * volume_strain
            weighted = point_weights * stress
            if direction == 0:
                term = jnp.einsum('pq,kpbel->kqbel', derivative, weighted, precision=highest)
            elif direction == 1:
                term = jnp.einsum('pq,kapel->kaqel', derivative, weighted, precision=highest)
            else:
                term = jnp.einsum('pq,pabel->qabel', derivative, weighted, precision=highest)
            total_force = term if total_force is None else total_force + term
        components.append(2.0 * total_force)
    forces = jnp.stack(components, axis=3)
    forces = forces.reshape((3, 3, 3, 3, shape_z, shape_x, shape_y))
    forces = assemble(forces, 3)
    forces = assemble(forces, 3)
    return assemble(forces, 3)

def line_weights(length, free_ends):
    position = jnp.arange(length)
    weights = jnp.where(position % 2 == 0, 2.0 / 3.0, 4.0 / 3.0)
    if free_ends:
        weights = jnp.where((position == 0) | (position == length - 1), 1.0 / 3.0, weights)
    return weights.astype(jnp.float32)

def node_weights(layers_z, nodes_x, nodes_y):
    return line_weights(layers_z, True)[:, None, None] * line_weights(nodes_x, False)[None, :, None] * line_weights(nodes_y, False)[None, None, :] / 8.0

def close_periodic(values):
    values = jnp.concatenate([values, values[:, :, :1]], axis=2)
    return jnp.concatenate([values, values[:, :, :, :1]], axis=3)

def global_stiffness(field, moduli):
    block_nodes = 2 * CX
    closed_field = close_periodic(field)
    closed_moduli = close_periodic(moduli)

    def one_block(carried, offset):
        field_piece = lax.dynamic_slice_in_dim(closed_field, offset, block_nodes + 1, axis=2)
        moduli_piece = lax.dynamic_slice_in_dim(closed_moduli, offset, block_nodes + 1, axis=2)
        forces = stiffness_apply(field_piece, moduli_piece)
        forces = jnp.concatenate([forces[..., :1] + forces[..., -1:], forces[..., 1:-1]], axis=3)
        interior = jnp.concatenate([forces[:, :, :1] + carried[:, :, None], forces[:, :, 1:block_nodes]], axis=2)
        return (forces[:, :, block_nodes], interior)
    carried = jnp.zeros((3, field.shape[1], field.shape[3]), jnp.float32)
    offsets = jnp.arange(N_GX).astype(jnp.int32) * (2 * CX)
    trailing, pieces = lax.scan(one_block, carried, offsets)
    assembled = pieces.transpose(1, 2, 0, 3, 4).reshape(field.shape)
    return jnp.concatenate([assembled[:, :, :1] + trailing[:, :, None], assembled[:, :, 1:]], axis=2)

def reference(displacement, previous, moduli, density, bins, omega, phase):
    layers_z, nodes_x, nodes_y = (displacement.shape[1], displacement.shape[2], displacement.shape[3])
    lumped_mass = density * node_weights(layers_z, nodes_x, nodes_y)
    middle = 2.0 * displacement - previous - time_step * time_step * global_stiffness(displacement, moduli) / lumped_mass
    updated = 2.0 * middle - displacement - time_step * time_step * global_stiffness(middle, moduli) / lumped_mass
    counter = jnp.arange(1, 3).astype(jnp.float32)
    angles = phase[None, :] + counter[:, None] * omega[None, :]
    cosines = jnp.cos(angles).reshape(2, -1, 1, 1, 1)
    sines = jnp.sin(angles).reshape(2, -1, 1, 1, 1)
    top_one = middle[:, layers_z - 1]
    top_two = updated[:, layers_z - 1]
    new_re = bins[:, :, 0] + cosines[0] * top_one[None] + cosines[1] * top_two[None]
    new_im = bins[:, :, 1] - sines[0] * top_one[None] - sines[1] * top_two[None]
    waves = jnp.fft.fft(new_re + 1j * new_im, axis=2) / math.sqrt(nodes_x)
    waves = waves.reshape(waves.shape[0], 3, 2 * CX, N_GX, nodes_y).transpose(0, 1, 3, 2, 4).reshape(waves.shape[0], 3, nodes_x, nodes_y)
    spectrum = jnp.stack([jnp.real(waves), jnp.imag(waves)], axis=2).astype(jnp.float32)
    return (updated, middle, spectrum)
```

```python
import functools

import jax
import jax.numpy as jnp
import numpy as np
from jax import lax
from jax.experimental import pallas as pl
from jax.experimental.pallas import tpu as pltpu
from jax.sharding import PartitionSpec as P

time_step = 0.03
HALO = 4
EDGE = 8
HIGHEST = lax.Precision.HIGHEST


def edge_columns(width):
    table = np.zeros((EDGE, width), np.float32)
    for h in range(HALO):
        table[h, h] = 1.0
        table[HALO + h, width - HALO + h] = 1.0
    return table


def fourier_tables(length):
    index = np.arange(length)
    angle = 2.0 * np.pi * (index[:, None] * index[None, :] % length) / length
    return np.cos(angle), np.sin(angle)


def pack_rows_kernel(disp, prev, moduli, density, select, up, down, main):
    start = 0
    for ref in (disp, prev, moduli, density):
        planes, rows, width = ref.shape
        for i in range(planes):
            at = (start + i) * HALO
            up[at : at + HALO, :] = ref[i, rows - HALO : rows, :]
            down[at : at + HALO, :] = ref[i, :HALO, :]
        flat = ref[...].reshape(planes * rows, width)
        packed = lax.dot_general(
            select[...], flat, (((1,), (1,)), ((), ())), precision=HIGHEST, preferred_element_type=jnp.float32
        )
        main[:, start * rows : (start + planes) * rows] = packed
        start += planes
    used = start * rows
    main[:, used:] = jnp.zeros((EDGE, main.shape[1] - used), jnp.float32)


def pack_columns_kernel(main, before, after, select, first, last):
    width = main.shape[1]
    lanes = select.shape[1]
    first[:, :width] = main[:HALO, :]
    last[:, :width] = main[HALO:, :]
    count = before.shape[0]
    fill = jnp.zeros((lanes - count, lanes), jnp.float32)
    for n, ref in enumerate((after, before)):
        rows = jnp.concatenate([ref[...], fill], axis=0)
        packed = lax.dot_general(
            select[...], rows, (((1,), (1,)), ((), ())), precision=HIGHEST, preferred_element_type=jnp.float32
        )
        at = width + n * lanes
        first[:, at : at + lanes] = packed[:HALO]
        last[:, at : at + lanes] = packed[HALO:]


def shift(value, amount, axis):
    return pltpu.roll(value, (-amount) % value.shape[axis], axis)


def slopes(value, axis, even):
    ahead, ahead2 = shift(value, 1, axis), shift(value, 2, axis)
    back, back2 = shift(value, -1, axis), shift(value, -2, axis)
    right = jnp.where(even, 4.0 * ahead - 3.0 * value - ahead2, ahead - back)
    left = 3.0 * value - 4.0 * back + back2
    return right, left, jnp.where(even, right + left, right)


def spread(right, left, axis, even):
    ahead = jnp.where(even, -4.0 * left, -right)
    back = jnp.where(even, 4.0 * right, right)
    ahead = ahead + shift(jnp.where(even, left, 0.0), 1, axis)
    back = back - shift(jnp.where(even, right, 0.0), -1, axis)
    own = jnp.where(even, 3.0 * (left - right), 0.0)
    return own + shift(ahead, 1, axis) + shift(back, -1, axis)


def slopes_z(layers):
    a, b, c = layers
    return 4.0 * b - 3.0 * a - c, c - a, a - 4.0 * b + 3.0 * c


def spread_z(layers):
    a, b, c = layers
    return c - b - 3.0 * a, 4.0 * (a - c), b - a + 3.0 * c


def step_kernel(
    omega, phase, disp, prev, moduli, density, bins, before, after, east, west, select,
    updated, middle, operand, field, coef, strip, mid,
):
    rows, width = disp.shape[1], disp.shape[2]
    tall, wide = rows + EDGE, 2 * width
    halo_at = east.shape[1] - 2 * width
    both = jnp.concatenate([east[...], west[...]], axis=0)
    strip[...] = lax.dot_general(
        both, select[...], (((0,), (0,)), ((), ())), precision=HIGHEST, preferred_element_type=jnp.float32
    )
    start = 0
    for ref in (disp, prev, moduli, density):
        for i in range(ref.shape[0]):
            n = start + i
            field[n, :rows, :width] = ref[i]
            field[n, rows : rows + HALO, :width] = after[n * HALO : (n + 1) * HALO, :]
            field[n, rows + HALO :, :width] = before[n * HALO : (n + 1) * HALO, :]
            field[n, :rows, width:] = strip[n * rows : (n + 1) * rows, :]
            field[n, rows : rows + HALO, width:] = strip[halo_at + n * HALO : halo_at + (n + 1) * HALO, :]
            field[n, rows + HALO :, width:] = strip[
                halo_at + width + n * HALO : halo_at + width + (n + 1) * HALO, :
            ]
        start += ref.shape[0]

    row = lax.broadcasted_iota(jnp.int32, (tall, wide), 0)
    lane = lax.broadcasted_iota(jnp.int32, (tall, wide), 1)
    even_x = row % 2 == 0
    even_y = lane % 2 == 0
    two_x = jnp.where(even_x, 2.0, 1.0)
    two_y = jnp.where(even_y, 2.0, 1.0)
    weight = jnp.where(even_x, 1.0 / 3.0, 4.0 / 3.0) * jnp.where(even_y, 1.0 / 3.0, 4.0 / 3.0) / 8.0
    unused = (lane >= width + HALO) & (lane < wide - HALO)
    for layer in range(3):
        weight_z = 4.0 / 3.0 if layer == 1 else 1.0 / 3.0
        here = weight * weight_z
        lam = field[18 + layer] * here
        mu = field[21 + layer] * here
        mu_x, mu_y = mu * two_x, mu * two_y
        mu_xy = mu_x * two_y
        lam_x, lam_y = lam * two_x, lam * two_y
        mass = jnp.where(unused, 1.0, field[24 + layer]) * (here * two_x * two_y)
        for n, value in enumerate(
            (lam, lam_x, lam_y, lam_x + 2.0 * mu_x, lam_y + 2.0 * mu_y, lam_x * two_y + 2.0 * mu_xy,
             mu, mu_x, mu_y, mu_xy, time_step * time_step / mass)
        ):
            coef[layer, n] = value

    def advance(source, older, store):
        forces = [[None] * 3 for _ in range(3)]
        z_terms = [[None] * 3 for _ in range(3)]
        for layer in range(3):
            value = [source(c * 3 + layer) for c in range(3)]
            grad_z = []
            for c in range(3):
                a, b, d = (source(c * 3 + n) for n in range(3))
                if layer == 0:
                    grad_z.append(4.0 * b - 3.0 * a - d)
                elif layer == 1:
                    grad_z.append(d - a)
                else:
                    grad_z.append(a - 4.0 * b + 3.0 * d)
            lam, lam_x, lam_y, stiff_x, stiff_y, stiff_z, mu, mu_x, mu_y, mu_xy = (
                coef[layer, n] for n in range(10)
            )
            rx, lx, sx = zip(*(slopes(v, 0, even_x) for v in value))
            ry, ly, sy = zip(*(slopes(v, 1, even_y) for v in value))
            common = lam_y * grad_z[2] + lam * sy[1]
            force_x = spread(stiff_y * rx[0] + common, stiff_y * lx[0] + common, 0, even_x)
            common = mu * sx[1]
            force_x += spread(mu_x * ry[0] + common, mu_x * ly[0] + common, 1, even_y)
            common = mu * sy[0]
            force_y = spread(mu_y * rx[1] + common, mu_y * lx[1] + common, 0, even_x)
            common = lam_x * grad_z[2] + lam * sx[0]
            force_y += spread(stiff_x * ry[1] + common, stiff_x * ly[1] + common, 1, even_y)
            force_z = spread(mu_y * (rx[2] + grad_z[0]), mu_y * (lx[2] + grad_z[0]), 0, even_x)
            force_z += spread(mu_x * (ry[2] + grad_z[1]), mu_x * (ly[2] + grad_z[1]), 1, even_y)
            for c, value in enumerate((force_x, force_y, force_z)):
                forces[c][layer] = value
            z_terms[0][layer] = mu_xy * grad_z[0] + mu_y * sx[2]
            z_terms[1][layer] = mu_xy * grad_z[1] + mu_x * sy[2]
            z_terms[2][layer] = lam_y * sx[0] + lam_x * sy[1] + stiff_z * grad_z[2]
        for c in range(3):
            along_z = spread_z(z_terms[c])
            for layer in range(3):
                n = c * 3 + layer
                total = (forces[c][layer] + along_z[layer]) * coef[layer, 10]
                store(n, 2.0 * source(n) - older(n) - total)

    def keep_middle(n, value):
        mid[n] = value
        middle[n] = value[:rows, :width]

    def keep_updated(n, value):
        updated[n] = value[:rows, :width]

    advance(lambda n: field[n], lambda n: field[9 + n], keep_middle)
    advance(lambda n: mid[n], lambda n: field[n], keep_updated)

    slot = lax.broadcasted_iota(jnp.int32, (8, width), 0)
    angles = jnp.zeros((8, width), jnp.float32)
    for s in range(2):
        for b in range(2):
            angles = jnp.where(slot == 2 * s + b, phase[b] + (s + 1.0) * omega[b], angles)
    cosines, sines = jnp.cos(angles), jnp.sin(angles)
    low = lax.broadcasted_iota(jnp.int32, (rows, width), 1) < width // 2
    half = width // 2
    for b in range(2):
        for c in range(3):
            one, two = middle[c * 3 + 2], updated[c * 3 + 2]
            item = b * 3 + c
            real = bins[2 * item] + cosines[b : b + 1] * one + cosines[2 + b : 3 + b] * two
            imag = bins[2 * item + 1] - sines[b : b + 1] * one - sines[2 + b : 3 + b] * two
            if item < 4:
                operand[pl.ds(3 * item * rows, rows, stride=3), :] = real
                operand[pl.ds(3 * item * rows + 1, rows, stride=3), :] = imag
            else:
                at = 3 * (item - 4) * rows + 2
                operand[pl.ds(at, rows, stride=3), :] = jnp.where(low, real, pltpu.roll(imag, half, 1))
                operand[pl.ds(at + 6 * rows, rows, stride=3), :] = jnp.where(
                    low, pltpu.roll(real, half, 1), imag
                )


def first_transform_kernel(received, cosine, sine, out):
    count = cosine.shape[0]
    width = received.shape[1]
    parts = [received[pl.ds(n, count, stride=3), :] for n in range(3)]
    joined = jnp.concatenate(parts, axis=1)
    by_cos = jnp.dot(cosine[...], joined, precision=HIGHEST, preferred_element_type=jnp.float32)
    by_sin = jnp.dot(sine[...], joined, precision=HIGHEST, preferred_element_type=jnp.float32)
    out[pl.ds(0, count, stride=3), :] = by_cos[:, :width] + by_sin[:, width : 2 * width]
    out[pl.ds(1, count, stride=3), :] = by_cos[:, width : 2 * width] - by_sin[:, :width]
    turned = pltpu.roll(by_sin[:, 2 * width :], width // 2, 1)
    low = lax.broadcasted_iota(jnp.int32, turned.shape, 1) < width // 2
    out[pl.ds(2, count, stride=3), :] = by_cos[:, 2 * width :] + jnp.where(low, turned, -turned)


def second_transform_kernel(position, received, straight, turned, out):
    items, parts, rows, width = out.shape
    half = width // 2
    count = received.shape[0] // 3
    low = lax.broadcasted_iota(jnp.int32, (rows, width), 1) < half
    real, imag = [], []
    for item in range(items):
        if item < 4:
            real.append(received[pl.ds(3 * item * rows, rows, stride=3), :])
            imag.append(received[pl.ds(3 * item * rows + 1, rows, stride=3), :])
        else:
            at = 3 * (item - 4) * rows + 2
            one = received[pl.ds(at, rows, stride=3), :]
            two = received[pl.ds(at + 6 * rows, rows, stride=3), :]
            real.append(jnp.where(low, one, pltpu.roll(two, half, 1)))
            imag.append(jnp.where(low, pltpu.roll(one, half, 1), two))
    joined = jnp.concatenate([jnp.concatenate(real, axis=1), jnp.concatenate(imag, axis=1)], axis=0)
    node = lax.broadcasted_iota(jnp.int32, straight.shape, 1) % rows
    angle = (node * position[0]).astype(jnp.float32) * (2.0 * np.pi / (rows * count))
    matrix = straight[...] * jnp.cos(angle) + turned[...] * jnp.sin(angle)
    waves = jnp.dot(matrix, joined, precision=HIGHEST, preferred_element_type=jnp.float32)
    for item in range(items):
        for part in range(parts):
            out[item, part] = waves[part * rows : (part + 1) * rows, item * width : (item + 1) * width]


def exchange(value):
    peers = lax.axis_size("gx")
    rows, width = value.shape
    shaped = value.reshape(peers, 1, rows // peers * width)
    return lax.all_to_all(shaped, "gx", split_axis=0, concat_axis=0, tiled=True).reshape(rows, width)


def both_ways(forward, backward, axis):
    peers = lax.axis_size(axis)
    up = [(i, (i + 1) % peers) for i in range(peers)]
    down = [(j, i) for i, j in up]
    return lax.ppermute(forward, axis, up), lax.ppermute(backward, axis, down)


def f32(*shape):
    return jax.ShapeDtypeStruct(shape, jnp.float32)


def on_device(displacement, previous, moduli, density, bins, omega, phase):
    groups = lax.axis_size("gx")
    rows, width = density.shape[1:]
    items = bins.shape[0] * bins.shape[1]
    block = (rows, width)
    arrays = [a.reshape((-1,) + block) for a in (displacement, previous, moduli, density)]
    planes = sum(a.shape[0] for a in arrays)
    packed = -(-planes * rows // width) * width
    total = packed + 2 * width
    select = jnp.asarray(edge_columns(width))
    vmem = pl.BlockSpec(memory_space=pltpu.VMEM)
    smem = pl.BlockSpec(memory_space=pltpu.SMEM)
    params = pltpu.CompilerParams(vmem_limit_bytes=48 * 1024 * 1024)

    up, down, main = pl.pallas_call(
        pack_rows_kernel,
        out_shape=(f32(planes * HALO, width), f32(planes * HALO, width), f32(EDGE, packed)),
        in_specs=[vmem] * 5,
        out_specs=(vmem,) * 3,
        compiler_params=params,
    )(*arrays, select)
    before, after = both_ways(up, down, "gx")
    first, last = pl.pallas_call(
        pack_columns_kernel,
        out_shape=(f32(HALO, total), f32(HALO, total)),
        in_specs=[vmem] * 4,
        out_specs=(vmem,) * 2,
        compiler_params=params,
    )(main, before, after, select)
    west, east = both_ways(last, first, "gy")
    tall, wide = rows + EDGE, 2 * width
    updated, middle, operand = pl.pallas_call(
        step_kernel,
        out_shape=(f32(9, *block), f32(9, *block), f32(3 * groups, width)),
        in_specs=[smem] * 2 + [vmem] * 10,
        out_specs=(vmem,) * 3,
        scratch_shapes=[
            pltpu.VMEM((planes, tall, wide), jnp.float32),
            pltpu.VMEM((3, 11, tall, wide), jnp.float32),
            pltpu.VMEM((total, width), jnp.float32),
            pltpu.VMEM((9, tall, wide), jnp.float32),
        ],
        compiler_params=params,
    )(omega, phase, *arrays, bins.reshape((-1,) + block), before, after, east, west, select)

    cosine, sine = (jnp.asarray(t, jnp.float32) for t in fourier_tables(groups))
    sections = pl.pallas_call(
        first_transform_kernel,
        out_shape=f32(3 * groups, width),
        in_specs=[vmem] * 3,
        out_specs=vmem,
        compiler_params=params,
    )(exchange(operand), cosine, sine)
    scale = (groups * rows) ** -0.5
    c, s = (t * scale for t in fourier_tables(rows))
    straight = jnp.asarray(np.block([[c, s], [-s, c]]), jnp.float32)
    turned = jnp.asarray(np.block([[-s, c], [-c, -s]]), jnp.float32)
    position = lax.axis_index("gx").astype(jnp.int32).reshape(1)
    spectrum = pl.pallas_call(
        second_transform_kernel,
        out_shape=f32(items, 2, *block),
        in_specs=[smem] + [vmem] * 3,
        out_specs=vmem,
        compiler_params=params,
    )(position, exchange(sections), straight, turned)
    return (
        updated.reshape(displacement.shape),
        middle.reshape(displacement.shape),
        spectrum.reshape(bins.shape),
    )


def solution(mesh):
    placed = (
        P(None, None, "gx", "gy"),
        P(None, None, "gx", "gy"),
        P(None, None, "gx", "gy"),
        P(None, "gx", "gy"),
        P(None, None, None, "gx", "gy"),
        P(),
        P(),
    )
    return jax.shard_map(
        on_device,
        mesh=mesh,
        in_specs=placed,
        out_specs=(
            P(None, None, "gx", "gy"),
            P(None, None, "gx", "gy"),
            P(None, None, None, "gx", "gy"),
        ),
        check_vma=False,
    )
```

```python
import jax
import jax.numpy as jnp
import ml_dtypes
import numpy as np
from jax import lax
from jax.experimental import pallas as pl
from jax.experimental.pallas import tpu as pltpu
from jax.sharding import PartitionSpec as P

time_step = 0.03
HALO = 4
EDGE = 8


def edge_columns(width):
    table = np.zeros((EDGE, width), np.float32)
    for h in range(HALO):
        table[h, h] = 1.0
        table[HALO + h, width - HALO + h] = 1.0
    return table


def fourier_tables(length):
    index = np.arange(length)
    angle = 2.0 * np.pi * (index[:, None] * index[None, :] % length) / length
    return np.cos(angle), np.sin(angle)


def halves(value):
    high = value.astype(jnp.bfloat16)
    return high, (value - high.astype(jnp.float32)).astype(jnp.bfloat16)


def pick_columns(select, rows):
    chosen = select[...].astype(jnp.bfloat16)
    return lax.dot_general(
        jnp.concatenate([chosen, chosen], axis=1),
        jnp.concatenate(halves(rows), axis=1),
        (((1,), (1,)), ((), ())),
        preferred_element_type=jnp.float32,
    )


def pack_rows_kernel(disp, prev, moduli, density, up, down, low, high, sems):
    copies = []
    start = 0
    for n, ref in enumerate((disp, prev, moduli, density)):
        planes, rows, _ = ref.shape
        here = pl.ds(start, planes)
        copies.append(pltpu.make_async_copy(ref.at[:, pl.ds(0, 8), :], low.at[here], sems.at[2 * n]))
        copies.append(pltpu.make_async_copy(ref.at[:, pl.ds(rows - 8, 8), :], high.at[here], sems.at[2 * n + 1]))
        start += planes
    for copy in copies:
        copy.start()
    for copy in copies:
        copy.wait()
    for i in range(start):
        at = i * HALO
        up[at : at + HALO, :] = high[i, 8 - HALO :, :]
        down[at : at + HALO, :] = low[i, :HALO, :]


def pack_main_kernel(disp, prev, moduli, density, select, main):
    width = select.shape[1]
    whole = jnp.concatenate([ref[...].reshape(-1, width) for ref in (disp, prev, moduli, density)], axis=0)
    used = whole.shape[0]
    main[:, :used] = pick_columns(select, whole)
    main[:, used:] = jnp.zeros((EDGE, main.shape[1] - used), jnp.float32)


def pack_columns_kernel(main, before, after, select, first, last):
    width = main.shape[1]
    lanes = select.shape[1]
    first[:, :width] = main[:HALO, :]
    last[:, :width] = main[HALO:, :]
    fill = jnp.zeros((lanes - before.shape[0], lanes), jnp.float32)
    packed = pick_columns(select, jnp.concatenate([after[...], fill, before[...], fill], axis=0))
    first[:, width:] = packed[:HALO]
    last[:, width:] = packed[HALO:]


def shift(value, amount, axis):
    return pltpu.roll(value, (-amount) % value.shape[axis], axis)


def slopes(value, axis, even):
    ahead, ahead2 = shift(value, 1, axis), shift(value, 2, axis)
    back, back2 = shift(value, -1, axis), shift(value, -2, axis)
    right = jnp.where(even, 4.0 * ahead - 3.0 * value - ahead2, ahead - back)
    left = 3.0 * value - 4.0 * back + back2
    return right, left, jnp.where(even, right + left, right)


def spread(right, left, axis, even):
    ahead = jnp.where(even, -4.0 * left, -right)
    back = jnp.where(even, 4.0 * right, right)
    ahead = ahead + shift(jnp.where(even, left, 0.0), 1, axis)
    back = back - shift(jnp.where(even, right, 0.0), -1, axis)
    own = jnp.where(even, 3.0 * (left - right), 0.0)
    return own + shift(ahead, 1, axis) + shift(back, -1, axis)


def slopes_z(layers):
    a, b, c = layers
    return 4.0 * b - 3.0 * a - c, c - a, a - 4.0 * b + 3.0 * c


def spread_z(layers):
    a, b, c = layers
    return c - b - 3.0 * a, 4.0 * (a - c), b - a + 3.0 * c


def step_kernel(
    omega, phase, disp, prev, moduli, density, bins, before, after, east, west, select,
    updated, middle, operand, field, coef, strip, mid,
):
    rows, width = disp.shape[1], disp.shape[2]
    tall, wide = rows + EDGE, 2 * width
    halo_at = east.shape[1] - 2 * width
    both = jnp.concatenate([east[...], west[...]], axis=0)
    chosen = select[...].astype(jnp.bfloat16)
    strip[...] = lax.dot_general(
        jnp.concatenate(halves(both), axis=0),
        jnp.concatenate([chosen, chosen], axis=0),
        (((0,), (0,)), ((), ())),
        preferred_element_type=jnp.float32,
    )
    start = 0
    for ref in (disp, prev, moduli, density):
        for i in range(ref.shape[0]):
            n = start + i
            field[n, :rows, :width] = ref[i]
            field[n, rows : rows + HALO, :width] = after[n * HALO : (n + 1) * HALO, :]
            field[n, rows + HALO :, :width] = before[n * HALO : (n + 1) * HALO, :]
            field[n, :rows, width:] = strip[n * rows : (n + 1) * rows, :]
            field[n, rows : rows + HALO, width:] = strip[halo_at + n * HALO : halo_at + (n + 1) * HALO, :]
            field[n, rows + HALO :, width:] = strip[
                halo_at + width + n * HALO : halo_at + width + (n + 1) * HALO, :
            ]
        start += ref.shape[0]

    def tiled(tile, shape=(tall, wide)):
        line = jnp.concatenate([tile] * (shape[1] // tile.shape[1]), axis=1)
        return jnp.concatenate([line] * (shape[0] // tile.shape[0]), axis=0)

    tile_x, tile_y = (lax.broadcasted_iota(jnp.int32, (8, 128), axis) % 2 for axis in range(2))
    near_x, near_y = tiled(tile_x), tiled(tile_y)
    two_x, two_y = 2.0 - near_x.astype(jnp.float32), 2.0 - near_y.astype(jnp.float32)
    weight = (1.0 / 3.0 + near_x.astype(jnp.float32)) * (1.0 / 3.0 + near_y.astype(jnp.float32)) / 8.0
    lane = lax.broadcasted_iota(jnp.int32, (tall, wide), 1)
    unused = (lane >= width + HALO) & (lane < wide - HALO)
    for layer in range(3):
        weight_z = 4.0 / 3.0 if layer == 1 else 1.0 / 3.0
        here = weight * weight_z
        lam = field[18 + layer] * here
        mu = field[21 + layer] * here
        mu_x, mu_y = mu * two_x, mu * two_y
        mu_xy = mu_x * two_y
        lam_x, lam_y = lam * two_x, lam * two_y
        mass = jnp.where(unused, 1.0, field[24 + layer]) * (here * two_x * two_y)
        for n, value in enumerate(
            (lam, lam_x, lam_y, lam_x + 2.0 * mu_x, lam_y + 2.0 * mu_y, lam_x * two_y + 2.0 * mu_xy,
             mu, mu_x, mu_y, mu_xy, time_step * time_step / mass)
        ):
            coef[layer, n] = value

    def advance(source, older, store, own):
        out_rows, out_width = (rows, width) if own else (tall, wide)
        even_x, even_y = near_x == 0, near_y == 0
        even_xs, even_ys = even_x[:, :out_width], even_y[:out_rows, :]

        def for_x(value):
            return value[:, :out_width]

        def for_y(value):
            return value[:out_rows, :]

        def for_z(value):
            return value[:out_rows, :out_width]

        def along_x(right, left):
            return spread(right, left, 0, even_xs)[:out_rows]

        def along_y(right, left):
            return spread(right, left, 1, even_ys)[:, :out_width]

        forces = [[None] * 3 for _ in range(3)]
        z_terms = [[None] * 3 for _ in range(3)]
        for layer in range(3):
            value = [source(c * 3 + layer) for c in range(3)]
            grad_z = []
            for c in range(3):
                a, b, d = (source(c * 3 + n) for n in range(3))
                if layer == 0:
                    grad_z.append(4.0 * b - 3.0 * a - d)
                elif layer == 1:
                    grad_z.append(d - a)
                else:
                    grad_z.append(a - 4.0 * b + 3.0 * d)
            lam, lam_x, lam_y, stiff_x, stiff_y, stiff_z, mu, mu_x, mu_y, mu_xy = (
                coef[layer, n] for n in range(10)
            )
            rx, lx, sx = zip(*(slopes(v, 0, even_x) for v in value))
            ry, ly, sy = zip(*(slopes(v, 1, even_y) for v in value))
            common = for_x(lam_y * grad_z[2] + lam * sy[1])
            scale = for_x(stiff_y)
            force_x = along_x(scale * for_x(rx[0]) + common, scale * for_x(lx[0]) + common)
            common = for_x(mu * sy[0])
            scale = for_x(mu_y)
            force_y = along_x(scale * for_x(rx[1]) + common, scale * for_x(lx[1]) + common)
            common = for_x(grad_z[0])
            force_z = along_x(scale * (for_x(rx[2]) + common), scale * (for_x(lx[2]) + common))
            common = for_y(lam_x * grad_z[2] + lam * sx[0])
            scale = for_y(stiff_x)
            force_y += along_y(scale * for_y(ry[1]) + common, scale * for_y(ly[1]) + common)
            common = for_y(mu * sx[1])
            scale = for_y(mu_x)
            force_x += along_y(scale * for_y(ry[0]) + common, scale * for_y(ly[0]) + common)
            common = for_y(grad_z[1])
            force_z += along_y(scale * (for_y(ry[2]) + common), scale * (for_y(ly[2]) + common))
            for c, value in enumerate((force_x, force_y, force_z)):
                forces[c][layer] = value
            z_terms[0][layer] = for_z(mu_xy * grad_z[0] + mu_y * sx[2])
            z_terms[1][layer] = for_z(mu_xy * grad_z[1] + mu_x * sy[2])
            z_terms[2][layer] = for_z(lam_y * sx[0] + lam_x * sy[1] + stiff_z * grad_z[2])
        for c in range(3):
            along_z = spread_z(z_terms[c])
            for layer in range(3):
                n = c * 3 + layer
                total = (forces[c][layer] + along_z[layer]) * for_z(coef[layer, 10])
                store(n, 2.0 * for_z(source(n)) - for_z(older(n)) - total)

    def keep_middle(n, value):
        mid[n] = value
        middle[n] = value[:rows, :width]

    def keep_updated(n, value):
        updated[n] = value

    advance(lambda n: field[n], lambda n: field[9 + n], keep_middle, False)
    advance(lambda n: mid[n], lambda n: field[n], keep_updated, True)

    slot = lax.broadcasted_iota(jnp.int32, (8, width), 0)
    angles = jnp.zeros((8, width), jnp.float32)
    for s in range(2):
        for b in range(2):
            angles = jnp.where(slot == 2 * s + b, phase[b] + (s + 1.0) * omega[b], angles)
    cosines, sines = jnp.cos(angles), jnp.sin(angles)
    low = lax.broadcasted_iota(jnp.int32, (rows, width), 1) < width // 2
    half = width // 2
    for b in range(2):
        for c in range(3):
            one, two = middle[c * 3 + 2], updated[c * 3 + 2]
            item = b * 3 + c
            real = bins[2 * item] + cosines[b : b + 1] * one + cosines[2 + b : 3 + b] * two
            imag = bins[2 * item + 1] - sines[b : b + 1] * one - sines[2 + b : 3 + b] * two
            if item < 4:
                operand[pl.ds(3 * item * rows, rows, stride=3), :] = real
                operand[pl.ds(3 * item * rows + 1, rows, stride=3), :] = imag
            else:
                at = 3 * (item - 4) * rows + 2
                operand[pl.ds(at, rows, stride=3), :] = jnp.where(low, real, pltpu.roll(imag, half, 1))
                operand[pl.ds(at + 6 * rows, rows, stride=3), :] = jnp.where(
                    low, pltpu.roll(real, half, 1), imag
                )


def first_transform_kernel(received, table, out):
    count, width = received.shape[0] // 3, received.shape[1]
    joined = jnp.concatenate([received[pl.ds(n, count, stride=3), :] for n in range(3)], axis=1)
    high, rest = halves(joined)
    both = jnp.dot(
        table[...], jnp.concatenate([high, rest, high], axis=0), preferred_element_type=jnp.float32
    )
    by_cos, by_sin = both[:count], both[count:]
    out[pl.ds(0, count, stride=3), :] = by_cos[:, :width] + by_sin[:, width : 2 * width]
    out[pl.ds(1, count, stride=3), :] = by_cos[:, width : 2 * width] - by_sin[:, :width]
    turned = pltpu.roll(by_sin[:, 2 * width :], width // 2, 1)
    low = lax.broadcasted_iota(jnp.int32, turned.shape, 1) < width // 2
    out[pl.ds(2, count, stride=3), :] = by_cos[:, 2 * width :] + jnp.where(low, turned, -turned)


def second_transform_kernel(position, received, straight, turned, out):
    items, parts, rows, width = out.shape
    half = width // 2
    count = received.shape[0] // 3
    low = lax.broadcasted_iota(jnp.int32, (rows, width), 1) < half
    real, imag = [], []
    for item in range(items):
        if item < 4:
            real.append(received[pl.ds(3 * item * rows, rows, stride=3), :])
            imag.append(received[pl.ds(3 * item * rows + 1, rows, stride=3), :])
        else:
            at = 3 * (item - 4) * rows + 2
            one = received[pl.ds(at, rows, stride=3), :]
            two = received[pl.ds(at + 6 * rows, rows, stride=3), :]
            real.append(jnp.where(low, one, pltpu.roll(two, half, 1)))
            imag.append(jnp.where(low, pltpu.roll(one, half, 1), two))
    joined = jnp.concatenate([jnp.concatenate(real, axis=1), jnp.concatenate(imag, axis=1)], axis=0)
    node = lax.broadcasted_iota(jnp.int32, straight.shape, 1) % rows
    angle = (node * position[0]).astype(jnp.float32) * (2.0 * np.pi / (rows * count))
    matrix = straight[...] * jnp.cos(angle) + turned[...] * jnp.sin(angle)
    left, left_rest = halves(matrix)
    high, rest = halves(joined)
    waves = jnp.dot(
        jnp.concatenate([left, left, left_rest], axis=1),
        jnp.concatenate([high, rest, high], axis=0),
        preferred_element_type=jnp.float32,
    )
    for item in range(items):
        for part in range(parts):
            out[item, part] = waves[part * rows : (part + 1) * rows, item * width : (item + 1) * width]


def exchange(value):
    peers = lax.axis_size("gx")
    rows, width = value.shape
    shaped = value.reshape(peers, 1, rows // peers * width)
    return lax.all_to_all(shaped, "gx", split_axis=0, concat_axis=0, tiled=True).reshape(rows, width)


def both_ways(forward, backward, axis):
    peers = lax.axis_size(axis)
    up = [(i, (i + 1) % peers) for i in range(peers)]
    down = [(j, i) for i, j in up]
    return lax.ppermute(forward, axis, up), lax.ppermute(backward, axis, down)


def f32(*shape):
    return jax.ShapeDtypeStruct(shape, jnp.float32)


def on_device(displacement, previous, moduli, density, bins, omega, phase):
    groups = lax.axis_size("gx")
    rows, width = density.shape[1:]
    items = bins.shape[0] * bins.shape[1]
    block = (rows, width)
    arrays = [a.reshape((-1,) + block) for a in (displacement, previous, moduli, density)]
    planes = sum(a.shape[0] for a in arrays)
    packed = -(-planes * rows // width) * width
    total = packed + 2 * width
    select = jnp.asarray(edge_columns(width))
    vmem = pl.BlockSpec(memory_space=pltpu.VMEM)
    smem = pl.BlockSpec(memory_space=pltpu.SMEM)
    params = pltpu.CompilerParams(vmem_limit_bytes=48 * 1024 * 1024)

    hbm = pl.BlockSpec(memory_space=pltpu.HBM)
    up, down = pl.pallas_call(
        pack_rows_kernel,
        out_shape=(f32(planes * HALO, width), f32(planes * HALO, width)),
        in_specs=[hbm] * 4,
        out_specs=(vmem,) * 2,
        scratch_shapes=[
            pltpu.VMEM((planes, 8, width), jnp.float32),
            pltpu.VMEM((planes, 8, width), jnp.float32),
            pltpu.SemaphoreType.DMA((8,)),
        ],
        compiler_params=pltpu.CompilerParams(vmem_limit_bytes=62 * 1024 * 1024),
    )(*arrays)
    main = pl.pallas_call(
        pack_main_kernel,
        out_shape=f32(EDGE, packed),
        in_specs=[vmem] * 5,
        out_specs=vmem,
        compiler_params=params,
        cost_estimate=pl.CostEstimate(flops=50_000_000, bytes_accessed=2_000_000, transcendentals=0),
    )(*arrays, select)
    before, after = both_ways(up, down, "gx")
    first, last = pl.pallas_call(
        pack_columns_kernel,
        out_shape=(f32(HALO, total), f32(HALO, total)),
        in_specs=[vmem] * 4,
        out_specs=(vmem,) * 2,
        compiler_params=params,
    )(main, before, after, select)
    west, east = both_ways(last, first, "gy")
    tall, wide = rows + EDGE, 2 * width
    updated, middle, operand = pl.pallas_call(
        step_kernel,
        out_shape=(f32(9, *block), f32(9, *block), f32(3 * groups, width)),
        in_specs=[smem] * 2 + [vmem] * 10,
        out_specs=(vmem,) * 3,
        scratch_shapes=[
            pltpu.VMEM((planes, tall, wide), jnp.float32),
            pltpu.VMEM((3, 11, tall, wide), jnp.float32),
            pltpu.VMEM((total, width), jnp.float32),
            pltpu.VMEM((9, tall, wide), jnp.float32),
        ],
        compiler_params=params,
    )(omega, phase, *arrays, bins.reshape((-1,) + block), before, after, east, west, select)

    stacked = np.concatenate(fourier_tables(groups), axis=0)
    high = stacked.astype(ml_dtypes.bfloat16)
    rest = (stacked - high.astype(np.float64)).astype(ml_dtypes.bfloat16)
    table = jnp.asarray(np.concatenate([high, high, rest], axis=1))
    sections = pl.pallas_call(
        first_transform_kernel,
        out_shape=f32(3 * groups, width),
        in_specs=[vmem] * 2,
        out_specs=vmem,
        compiler_params=params,
    )(exchange(operand), table)
    scale = (groups * rows) ** -0.5
    c, s = (t * scale for t in fourier_tables(rows))
    straight = jnp.asarray(np.block([[c, s], [-s, c]]), jnp.float32)
    turned = jnp.asarray(np.block([[-s, c], [-c, -s]]), jnp.float32)
    position = lax.axis_index("gx").astype(jnp.int32).reshape(1)
    spectrum = pl.pallas_call(
        second_transform_kernel,
        out_shape=f32(items, 2, *block),
        in_specs=[smem] + [vmem] * 3,
        out_specs=vmem,
        compiler_params=params,
    )(position, exchange(sections), straight, turned)
    return (
        updated.reshape(displacement.shape),
        middle.reshape(displacement.shape),
        spectrum.reshape(bins.shape),
    )


def solution(mesh):
    placed = (
        P(None, None, "gx", "gy"),
        P(None, None, "gx", "gy"),
        P(None, None, "gx", "gy"),
        P(None, "gx", "gy"),
        P(None, None, None, "gx", "gy"),
        P(),
        P(),
    )
    return jax.shard_map(
        on_device,
        mesh=mesh,
        in_specs=placed,
        out_specs=(
            P(None, None, "gx", "gy"),
            P(None, None, "gx", "gy"),
            P(None, None, None, "gx", "gy"),
        ),
        check_vma=False,
    )
```

```python
import jax
import jax.numpy as jnp
import ml_dtypes
import numpy as np
from jax import lax
from jax.experimental import pallas as pl
from jax.experimental.pallas import tpu as pltpu
from jax.sharding import PartitionSpec as P

time_step = 0.03
HALO = 4
EDGE = 8
BINS = 12


def edge_columns(width):
    table = np.zeros((EDGE, width), np.float32)
    for h in range(HALO):
        table[h, h] = 1.0
        table[HALO + h, width - HALO + h] = 1.0
    return table


def fourier_tables(length):
    index = np.arange(length)
    angle = 2.0 * np.pi * (index[:, None] * index[None, :] % length) / length
    return np.cos(angle), np.sin(angle)


def halves(value):
    high = value.astype(jnp.bfloat16)
    return high, (value - high.astype(jnp.float32)).astype(jnp.bfloat16)


def pick_columns(select, rows):
    chosen = select[...].astype(jnp.bfloat16)
    return lax.dot_general(
        jnp.concatenate([chosen, chosen], axis=1),
        jnp.concatenate(halves(rows), axis=1),
        (((1,), (1,)), ((), ())),
        preferred_element_type=jnp.float32,
    )


def pack_rows_kernel(disp, prev, moduli, density, bins, out, sems):
    copies = []
    start = 0
    for n, ref in enumerate((disp, prev, moduli, density, bins)):
        planes = ref.shape[0]
        copies.append(
            pltpu.make_async_copy(ref.at[:, pl.ds(0, EDGE), :], out.at[pl.ds(start, planes)], sems.at[n])
        )
        start += planes
    for copy in copies:
        copy.start()
    for copy in copies:
        copy.wait()


def pack_main_kernel(disp, prev, moduli, density, select, main):
    width = select.shape[1]
    whole = jnp.concatenate([ref[...].reshape(-1, width) for ref in (disp, prev, moduli, density)], axis=0)
    used = whole.shape[0]
    main[:, :used] = pick_columns(select, whole)
    main[:, used:] = jnp.zeros((EDGE, main.shape[1] - used), jnp.float32)


def pack_columns_kernel(position, main, ahead, select, out):
    peers, _, total = out.shape
    width = main.shape[1]
    planes = ahead.shape[0] - BINS
    rows = ahead[:planes].reshape(planes * EDGE, select.shape[1])
    fill = jnp.zeros((total - width - rows.shape[0], rows.shape[1]), jnp.float32)
    packed = pick_columns(select, jnp.concatenate([rows, fill], axis=0))
    me = position[1]
    for step in range(peers):
        slot = lax.rem(me + step, peers)
        if step in (1, peers - 1):
            at = HALO if step == 1 else 0
            out[slot, :, :width] = main[at : at + HALO, :]
            out[slot, :, width:] = packed[at : at + HALO]
        else:
            out[slot] = jnp.zeros((HALO, total), jnp.float32)


def shift(value, amount, axis):
    return pltpu.roll(value, (-amount) % value.shape[axis], axis)


def slopes(value, axis, even):
    ahead, ahead2 = shift(value, 1, axis), shift(value, 2, axis)
    back, back2 = shift(value, -1, axis), shift(value, -2, axis)
    right = jnp.where(even, 4.0 * ahead - 3.0 * value - ahead2, ahead - back)
    left = 3.0 * value - 4.0 * back + back2
    return right, left, jnp.where(even, right + left, right)


def spread(right, left, axis, even):
    ahead = jnp.where(even, -4.0 * left, -right)
    back = jnp.where(even, 4.0 * right, right)
    ahead = ahead + shift(jnp.where(even, left, 0.0), 1, axis)
    back = back - shift(jnp.where(even, right, 0.0), -1, axis)
    own = jnp.where(even, 3.0 * (left - right), 0.0)
    return own + shift(ahead, 1, axis) + shift(back, -1, axis)


def slopes_z(layers):
    a, b, c = layers
    return 4.0 * b - 3.0 * a - c, c - a, a - 4.0 * b + 3.0 * c


def spread_z(layers):
    a, b, c = layers
    return c - b - 3.0 * a, 4.0 * (a - c), b - a + 3.0 * c


def step_kernel(
    position, omega, phase, disp, prev, moduli, density, bins, ahead, beside, select,
    updated, middle, tail, operand, field, coef, strip, mid,
):
    rows, width = disp.shape[1], disp.shape[2]
    tall, wide = rows + EDGE, 2 * width
    peers = beside.shape[0]
    halo_at = beside.shape[2] - 2 * width
    me = position[1]
    both = jnp.concatenate([beside[lax.rem(me + 1, peers)], beside[lax.rem(me + peers - 1, peers)]], axis=0)
    chosen = select[...].astype(jnp.bfloat16)
    strip[...] = lax.dot_general(
        jnp.concatenate(halves(both), axis=0),
        jnp.concatenate([chosen, chosen], axis=0),
        (((0,), (0,)), ((), ())),
        preferred_element_type=jnp.float32,
    )
    start = 0
    for ref in (disp, prev, moduli, density):
        for i in range(ref.shape[0]):
            n = start + i
            field[n, :rows, :width] = ref[i]
            field[n, rows:, :width] = ahead[n]
            field[n, :rows, width:] = strip[n * rows : (n + 1) * rows, :]
            field[n, rows:, width:] = strip[halo_at + n * EDGE : halo_at + (n + 1) * EDGE, :]
        start += ref.shape[0]

    def tiled(tile, shape=(tall, wide)):
        line = jnp.concatenate([tile] * (shape[1] // tile.shape[1]), axis=1)
        return jnp.concatenate([line] * (shape[0] // tile.shape[0]), axis=0)

    tile_x, tile_y = (lax.broadcasted_iota(jnp.int32, (8, 128), axis) % 2 for axis in range(2))
    near_x, near_y = tiled(tile_x), tiled(tile_y)
    two_x, two_y = 2.0 - near_x.astype(jnp.float32), 2.0 - near_y.astype(jnp.float32)
    weight = (1.0 / 3.0 + near_x.astype(jnp.float32)) * (1.0 / 3.0 + near_y.astype(jnp.float32)) / 8.0
    lane = lax.broadcasted_iota(jnp.int32, (tall, wide), 1)
    unused = (lane >= width + HALO) & (lane < wide - HALO)
    for layer in range(3):
        weight_z = 4.0 / 3.0 if layer == 1 else 1.0 / 3.0
        here = weight * weight_z
        lam = field[18 + layer] * here
        mu = field[21 + layer] * here
        mu_x, mu_y = mu * two_x, mu * two_y
        mu_xy = mu_x * two_y
        lam_x, lam_y = lam * two_x, lam * two_y
        mass = jnp.where(unused, 1.0, field[24 + layer]) * (here * two_x * two_y)
        for n, value in enumerate(
            (lam, lam_x, lam_y, lam_x + 2.0 * mu_x, lam_y + 2.0 * mu_y, lam_x * two_y + 2.0 * mu_xy,
             mu, mu_x, mu_y, mu_xy, time_step * time_step / mass)
        ):
            coef[layer, n] = value

    def advance(source, older, store, own):
        out_width = width if own else wide
        even_x, even_y = near_x == 0, near_y == 0
        even_xs = even_x[:, :out_width]

        def for_x(value):
            return value[:, :out_width]

        def along_x(right, left):
            return spread(right, left, 0, even_xs)

        def along_y(right, left):
            return spread(right, left, 1, even_y)[:, :out_width]

        forces = [[None] * 3 for _ in range(3)]
        z_terms = [[None] * 3 for _ in range(3)]
        for layer in range(3):
            value = [source(c * 3 + layer) for c in range(3)]
            grad_z = []
            for c in range(3):
                a, b, d = (source(c * 3 + n) for n in range(3))
                if layer == 0:
                    grad_z.append(4.0 * b - 3.0 * a - d)
                elif layer == 1:
                    grad_z.append(d - a)
                else:
                    grad_z.append(a - 4.0 * b + 3.0 * d)
            lam, lam_x, lam_y, stiff_x, stiff_y, stiff_z, mu, mu_x, mu_y, mu_xy = (
                coef[layer, n] for n in range(10)
            )
            rx, lx, sx = zip(*(slopes(v, 0, even_x) for v in value))
            ry, ly, sy = zip(*(slopes(v, 1, even_y) for v in value))
            common = for_x(lam_y * grad_z[2] + lam * sy[1])
            scale = for_x(stiff_y)
            force_x = along_x(scale * for_x(rx[0]) + common, scale * for_x(lx[0]) + common)
            common = for_x(mu * sy[0])
            scale = for_x(mu_y)
            force_y = along_x(scale * for_x(rx[1]) + common, scale * for_x(lx[1]) + common)
            common = for_x(grad_z[0])
            force_z = along_x(scale * (for_x(rx[2]) + common), scale * (for_x(lx[2]) + common))
            common = (lam_x * grad_z[2] + lam * sx[0])
            scale = (stiff_x)
            force_y += along_y(scale * (ry[1]) + common, scale * (ly[1]) + common)
            common = (mu * sx[1])
            scale = (mu_x)
            force_x += along_y(scale * (ry[0]) + common, scale * (ly[0]) + common)
            common = (grad_z[1])
            force_z += along_y(scale * ((ry[2]) + common), scale * ((ly[2]) + common))
            for c, value in enumerate((force_x, force_y, force_z)):
                forces[c][layer] = value
            z_terms[0][layer] = for_x(mu_xy * grad_z[0] + mu_y * sx[2])
            z_terms[1][layer] = for_x(mu_xy * grad_z[1] + mu_x * sy[2])
            z_terms[2][layer] = for_x(lam_y * sx[0] + lam_x * sy[1] + stiff_z * grad_z[2])
        for c in range(3):
            along_z = spread_z(z_terms[c])
            for layer in range(3):
                n = c * 3 + layer
                total = (forces[c][layer] + along_z[layer]) * for_x(coef[layer, 10])
                store(n, 2.0 * for_x(source(n)) - for_x(older(n)) - total)

    is_tail = lax.broadcasted_iota(jnp.int32, (EDGE, width), 0) < HALO
    tops = {}

    def keep(ref, n, value):
        ref[n] = value[:rows]
        if n % 3 == 2:
            first = jnp.where(is_tail, value[rows:], value[:EDGE])
            tops.setdefault(n // 3, []).append(jnp.concatenate([first, value[EDGE:rows]], axis=0))

    def keep_middle(n, value):
        mid[n] = value
        tail[(9 + n) * HALO : (10 + n) * HALO, :] = value[rows : rows + HALO, :width]
        keep(middle, n, value[:, :width])

    def keep_updated(n, value):
        tail[n * HALO : (n + 1) * HALO, :] = value[rows : rows + HALO]
        keep(updated, n, value)

    advance(lambda n: field[n], lambda n: field[9 + n], keep_middle, False)
    advance(lambda n: mid[n], lambda n: field[n], keep_updated, True)

    slot = lax.broadcasted_iota(jnp.int32, (8, width), 0)
    angles = jnp.zeros((8, width), jnp.float32)
    for s in range(2):
        for b in range(2):
            angles = jnp.where(slot == 2 * s + b, phase[b] + (s + 1.0) * omega[b], angles)
    cosines, sines = jnp.cos(angles), jnp.sin(angles)
    low = lax.broadcasted_iota(jnp.int32, (rows, width), 1) < width // 2
    half = width // 2
    for b in range(2):
        for c in range(3):
            one, two = tops[c]
            item = b * 3 + c
            old = []
            for n in (2 * item, 2 * item + 1):
                first = jnp.where(is_tail, ahead[start + n], bins[n, :EDGE])
                old.append(jnp.concatenate([first, bins[n, EDGE:]], axis=0))
            real = old[0] + cosines[b : b + 1] * one + cosines[2 + b : 3 + b] * two
            imag = old[1] - sines[b : b + 1] * one - sines[2 + b : 3 + b] * two
            if item < 4:
                operand[pl.ds(3 * item * rows, rows, stride=3), :] = real
                operand[pl.ds(3 * item * rows + 1, rows, stride=3), :] = imag
            else:
                at = 3 * (item - 4) * rows + 2
                operand[pl.ds(at, rows, stride=3), :] = jnp.where(low, real, pltpu.roll(imag, half, 1))
                operand[pl.ds(at + 6 * rows, rows, stride=3), :] = jnp.where(
                    low, pltpu.roll(real, half, 1), imag
                )


def first_transform_kernel(received, table, tail, out, tail_out):
    tail_out[...] = tail[...]
    count, width = received.shape[0] // 3, received.shape[1]
    joined = jnp.concatenate([received[pl.ds(n, count, stride=3), :] for n in range(3)], axis=1)
    high, rest = halves(joined)
    both = jnp.dot(
        table[...], jnp.concatenate([high, rest, high], axis=0), preferred_element_type=jnp.float32
    )
    by_cos, by_sin = both[:count], both[count:]
    out[pl.ds(0, count, stride=3), :] = by_cos[:, :width] + by_sin[:, width : 2 * width]
    out[pl.ds(1, count, stride=3), :] = by_cos[:, width : 2 * width] - by_sin[:, :width]
    turned = pltpu.roll(by_sin[:, 2 * width :], width // 2, 1)
    low = lax.broadcasted_iota(jnp.int32, turned.shape, 1) < width // 2
    out[pl.ds(2, count, stride=3), :] = by_cos[:, 2 * width :] + jnp.where(low, turned, -turned)


def second_transform_kernel(position, received, straight, turned, out):
    items, parts, rows, width = out.shape
    half = width // 2
    count = received.shape[0] // 3
    low = lax.broadcasted_iota(jnp.int32, (rows, width), 1) < half
    real, imag = [], []
    for item in range(items):
        if item < 4:
            real.append(received[pl.ds(3 * item * rows, rows, stride=3), :])
            imag.append(received[pl.ds(3 * item * rows + 1, rows, stride=3), :])
        else:
            at = 3 * (item - 4) * rows + 2
            one = received[pl.ds(at, rows, stride=3), :]
            two = received[pl.ds(at + 6 * rows, rows, stride=3), :]
            real.append(jnp.where(low, one, pltpu.roll(two, half, 1)))
            imag.append(jnp.where(low, pltpu.roll(one, half, 1), two))
    joined = jnp.concatenate([jnp.concatenate(real, axis=1), jnp.concatenate(imag, axis=1)], axis=0)
    slot = lax.broadcasted_iota(jnp.int32, straight.shape, 1) % rows
    node = jnp.where(slot < HALO, slot + rows, slot)
    angle = (node * position[0] % (rows * count)).astype(jnp.float32) * (2.0 * np.pi / (rows * count))
    matrix = straight[...] * jnp.cos(angle) + turned[...] * jnp.sin(angle)
    left, left_rest = halves(matrix)
    high, rest = halves(joined)
    waves = jnp.dot(
        jnp.concatenate([left, left, left_rest], axis=1),
        jnp.concatenate([high, rest, high], axis=0),
        preferred_element_type=jnp.float32,
    )
    for item in range(items):
        for part in range(parts):
            out[item, part] = waves[part * rows : (part + 1) * rows, item * width : (item + 1) * width]


def set_in_kernel(updated, middle, tail, updated_out, middle_out):
    for k, (ref, out) in enumerate(((updated, updated_out), (middle, middle_out))):
        for n in range(ref.shape[0]):
            out[n] = ref[n]
            out[n, :HALO, :] = tail[(k * ref.shape[0] + n) * HALO : (k * ref.shape[0] + n + 1) * HALO, :]


def exchange(value):
    peers = lax.axis_size("gx")
    rows, width = value.shape
    shaped = value.reshape(peers, 1, rows // peers * width)
    return lax.all_to_all(shaped, "gx", split_axis=0, concat_axis=0, tiled=True).reshape(rows, width)


def exchange_gy(value):
    return lax.all_to_all(value, "gy", split_axis=0, concat_axis=0, tiled=True)


def pass_on(value, axis, step):
    peers = lax.axis_size(axis)
    return lax.ppermute(value, axis, [(i, (i + step) % peers) for i in range(peers)])


def f32(*shape):
    return jax.ShapeDtypeStruct(shape, jnp.float32)


def on_device(displacement, previous, moduli, density, bins, omega, phase):
    groups = lax.axis_size("gx")
    rows, width = density.shape[1:]
    items = bins.shape[0] * bins.shape[1]
    block = (rows, width)
    arrays = [a.reshape((-1,) + block) for a in (displacement, previous, moduli, density, bins)]
    planes = sum(a.shape[0] for a in arrays) - BINS
    packed = -(-planes * rows // width) * width
    total = packed + 2 * width
    select = jnp.asarray(edge_columns(width))
    position = jnp.stack([lax.axis_index("gx"), lax.axis_index("gy")]).astype(jnp.int32)
    vmem = pl.BlockSpec(memory_space=pltpu.VMEM)
    smem = pl.BlockSpec(memory_space=pltpu.SMEM)
    hbm = pl.BlockSpec(memory_space=pltpu.HBM)
    params = pltpu.CompilerParams(vmem_limit_bytes=48 * 1024 * 1024)

    edge = pl.pallas_call(
        pack_rows_kernel,
        out_shape=f32(planes + BINS, EDGE, width),
        in_specs=[hbm] * 5,
        out_specs=hbm,
        scratch_shapes=[pltpu.SemaphoreType.DMA((5,))],
        compiler_params=pltpu.CompilerParams(vmem_limit_bytes=62 * 1024 * 1024),
    )(*arrays)
    main = pl.pallas_call(
        pack_main_kernel,
        out_shape=f32(EDGE, packed),
        in_specs=[vmem] * 5,
        out_specs=vmem,
        compiler_params=params,
        cost_estimate=pl.CostEstimate(flops=50_000_000, bytes_accessed=2_000_000, transcendentals=0),
    )(*arrays[:4], select)
    ahead = pass_on(edge, "gx", -1)
    sides = pl.pallas_call(
        pack_columns_kernel,
        out_shape=f32(lax.axis_size("gy"), HALO, total),
        in_specs=[smem] + [vmem] * 3,
        out_specs=vmem,
        compiler_params=params,
    )(position, main, ahead, select)
    tall, wide = rows + EDGE, 2 * width
    updated, middle, tail, operand = pl.pallas_call(
        step_kernel,
        out_shape=(f32(9, *block), f32(9, *block), f32(18 * HALO, width), f32(3 * groups, width)),
        in_specs=[smem] * 3 + [vmem] * 8,
        out_specs=(vmem,) * 4,
        scratch_shapes=[
            pltpu.VMEM((planes, tall, wide), jnp.float32),
            pltpu.VMEM((3, 11, tall, wide), jnp.float32),
            pltpu.VMEM((total, width), jnp.float32),
            pltpu.VMEM((9, tall, wide), jnp.float32),
        ],
        compiler_params=params,
    )(position, omega, phase, *arrays, ahead, exchange_gy(sides), select)

    stacked = np.concatenate(fourier_tables(groups), axis=0)
    high = stacked.astype(ml_dtypes.bfloat16)
    rest = (stacked - high.astype(np.float64)).astype(ml_dtypes.bfloat16)
    table = jnp.asarray(np.concatenate([high, high, rest], axis=1))
    sections, tail = pl.pallas_call(
        first_transform_kernel,
        out_shape=(f32(3 * groups, width), f32(*tail.shape)),
        in_specs=[vmem] * 3,
        out_specs=(vmem,) * 2,
        compiler_params=params,
    )(exchange(operand), table, tail)
    updated, middle = pl.pallas_call(
        set_in_kernel,
        out_shape=(f32(9, *block), f32(9, *block)),
        in_specs=[vmem] * 3,
        out_specs=(vmem,) * 2,
        compiler_params=params,
        cost_estimate=pl.CostEstimate(flops=1_000_000, bytes_accessed=1_200_000, transcendentals=0),
    )(updated, middle, pass_on(tail, "gx", 1))
    scale = (groups * rows) ** -0.5
    c, s = (t * scale for t in fourier_tables(rows))
    straight = jnp.asarray(np.block([[c, s], [-s, c]]), jnp.float32)
    turned = jnp.asarray(np.block([[-s, c], [-c, -s]]), jnp.float32)
    spectrum = pl.pallas_call(
        second_transform_kernel,
        out_shape=f32(items, 2, *block),
        in_specs=[smem] + [vmem] * 3,
        out_specs=vmem,
        compiler_params=params,
    )(position, exchange(sections), straight, turned)
    return (
        updated.reshape(displacement.shape),
        middle.reshape(displacement.shape),
        spectrum.reshape(bins.shape),
    )


def solution(mesh):
    placed = (
        P(None, None, "gx", "gy"),
        P(None, None, "gx", "gy"),
        P(None, None, "gx", "gy"),
        P(None, "gx", "gy"),
        P(None, None, None, "gx", "gy"),
        P(),
        P(),
    )
    return jax.shard_map(
        on_device,
        mesh=mesh,
        in_specs=placed,
        out_specs=(
            P(None, None, "gx", "gy"),
            P(None, None, "gx", "gy"),
            P(None, None, None, "gx", "gy"),
        ),
        check_vma=False,
    )
```

```python
import jax
import jax.numpy as jnp
import ml_dtypes
import numpy as np
from jax import lax
from jax.experimental import pallas as pl
from jax.experimental.pallas import tpu as pltpu
from jax.sharding import PartitionSpec as P

time_step = 0.03
HALO = 4
EDGE = 8
BINS = 12


def edge_columns(width):
    table = np.zeros((EDGE, width), np.float32)
    for h in range(HALO):
        table[h, h] = 1.0
        table[HALO + h, width - HALO + h] = 1.0
    return table


def fourier_tables(length):
    index = np.arange(length)
    angle = 2.0 * np.pi * (index[:, None] * index[None, :] % length) / length
    return np.cos(angle), np.sin(angle)


def halves(value):
    high = value.astype(jnp.bfloat16)
    return high, (value - high.astype(jnp.float32)).astype(jnp.bfloat16)


def pick_columns(select, rows):
    chosen = select[...].astype(jnp.bfloat16)
    return lax.dot_general(
        jnp.concatenate([chosen, chosen], axis=1),
        jnp.concatenate(halves(rows), axis=1),
        (((1,), (1,)), ((), ())),
        preferred_element_type=jnp.float32,
    )


def pack_rows_kernel(disp, prev, moduli, density, bins, out, sems):
    copies = []
    start = 0
    for n, ref in enumerate((disp, prev, moduli, density, bins)):
        planes = ref.shape[0]
        copies.append(
            pltpu.make_async_copy(ref.at[:, pl.ds(0, EDGE), :], out.at[pl.ds(start, planes)], sems.at[n])
        )
        start += planes
    for copy in copies:
        copy.start()
    for copy in copies:
        copy.wait()


def pack_main_kernel(disp, prev, moduli, density, select, main):
    width = select.shape[1]
    whole = jnp.concatenate([ref[...].reshape(-1, width) for ref in (disp, prev, moduli, density)], axis=0)
    used = whole.shape[0]
    main[:, :used] = pick_columns(select, whole)
    main[:, used:] = jnp.zeros((EDGE, main.shape[1] - used), jnp.float32)


def pack_columns_kernel(facts, main, ahead, select, out):
    peers, _, total = out.shape
    width = main.shape[1]
    planes = ahead.shape[0] - BINS
    rows = ahead[:planes].reshape(planes * EDGE, select.shape[1])
    fill = jnp.zeros((total - width - rows.shape[0], rows.shape[1]), jnp.float32)
    packed = pick_columns(select, jnp.concatenate([rows, fill], axis=0))
    for slot in range(peers):
        after, before = (facts[n : n + 1, :1] > 0.5 for n in (slot, peers + slot))
        for source, at in ((main[...], 0), (packed, width)):
            chosen = jnp.where(after, source[HALO:], jnp.where(before, source[:HALO], 0.0))
            out[slot, :, at : at + source.shape[1]] = chosen


def shift(value, amount, axis):
    return pltpu.roll(value, (-amount) % value.shape[axis], axis)


def slopes(value, axis, even):
    step = shift(value, 1, axis) - value
    before = shift(step, -1, axis)
    right = jnp.where(even, 3.0 * step - shift(step, 1, axis), step + before)
    left = shift(3.0 * step - before, -1, axis)
    return right, left, jnp.where(even, right + left, right)


def spread(right, left, axis, even):
    left = shift(left, 1, axis)
    step = jnp.where(
        even,
        3.0 * right + shift(right - left, 1, axis),
        right + 3.0 * left - shift(right, -1, axis),
    )
    return shift(step, -1, axis) - step


def spread_z(layers):
    a, b, c = layers
    return c - b - 3.0 * a, 4.0 * (a - c), b - a + 3.0 * c


def step_kernel(
    facts, disp, prev, moduli, density, bins, ahead, beside, select,
    updated, middle, tail, operand, field, coef, strip, mid,
):
    rows, width = disp.shape[1], disp.shape[2]
    tall, wide = rows + EDGE, 2 * width
    peers = beside.shape[0]
    halo_at = beside.shape[2] - 2 * width
    east = west = beside[0]
    for slot in range(1, peers):
        east = jnp.where(facts[slot : slot + 1, :1] > 0.5, beside[slot], east)
        west = jnp.where(facts[peers + slot : peers + slot + 1, :1] > 0.5, beside[slot], west)
    both = jnp.concatenate([east, west], axis=0)
    chosen = select[...].astype(jnp.bfloat16)
    strip[...] = lax.dot_general(
        jnp.concatenate(halves(both), axis=0),
        jnp.concatenate([chosen, chosen], axis=0),
        (((0,), (0,)), ((), ())),
        preferred_element_type=jnp.float32,
    )
    start = 0
    for ref in (disp, prev, moduli, density):
        for i in range(ref.shape[0]):
            n = start + i
            field[n, :rows, :width] = ref[i]
            field[n, rows:, :width] = ahead[n]
            field[n, :rows, width:] = strip[n * rows : (n + 1) * rows, :]
            field[n, rows:, width:] = strip[halo_at + n * EDGE : halo_at + (n + 1) * EDGE, :]
        start += ref.shape[0]

    def tiled(tile, shape=(tall, wide)):
        line = jnp.concatenate([tile] * (shape[1] // tile.shape[1]), axis=1)
        return jnp.concatenate([line] * (shape[0] // tile.shape[0]), axis=0)

    tile_x, tile_y = (lax.broadcasted_iota(jnp.int32, (8, 128), axis) % 2 for axis in range(2))
    near_x, near_y = tiled(tile_x), tiled(tile_y)
    two_x, two_y = 2.0 - near_x.astype(jnp.float32), 2.0 - near_y.astype(jnp.float32)
    weight = (1.0 / 3.0 + near_x.astype(jnp.float32)) * (1.0 / 3.0 + near_y.astype(jnp.float32)) / 8.0
    lane = lax.broadcasted_iota(jnp.int32, (tall, wide), 1)
    unused = (lane >= width + HALO) & (lane < wide - HALO)
    for layer in range(3):
        weight_z = 4.0 / 3.0 if layer == 1 else 1.0 / 3.0
        here = weight * weight_z
        lam = field[18 + layer] * here
        mu = field[21 + layer] * here
        mu_x, mu_y = mu * two_x, mu * two_y
        mu_xy = mu_x * two_y
        lam_x, lam_y = lam * two_x, lam * two_y
        mass = jnp.where(unused, 1.0, field[24 + layer]) * (here * two_x * two_y)
        for n, value in enumerate(
            (lam, lam_x, lam_y, lam_x + 2.0 * mu_x, lam_y + 2.0 * mu_y, lam_x * two_y + 2.0 * mu_xy,
             mu, mu_x, mu_y, mu_xy, time_step * time_step / mass)
        ):
            coef[layer, n] = value

    def advance(source, older, store, own):
        out_width = width if own else wide
        even_x, even_y = near_x == 0, near_y == 0
        even_xs = even_x[:, :out_width]

        def for_x(value):
            return value[:, :out_width]

        def along_x(right, left):
            return spread(right, left, 0, even_xs)

        def along_y(right, left):
            return spread(right, left, 1, even_y)[:, :out_width]

        forces = [[None] * 3 for _ in range(3)]
        z_terms = [[None] * 3 for _ in range(3)]
        for layer in range(3):
            value = [source(c * 3 + layer) for c in range(3)]
            grad_z = []
            for c in range(3):
                a, b, d = (source(c * 3 + n) for n in range(3))
                if layer == 0:
                    grad_z.append(4.0 * b - 3.0 * a - d)
                elif layer == 1:
                    grad_z.append(d - a)
                else:
                    grad_z.append(a - 4.0 * b + 3.0 * d)
            lam, lam_x, lam_y, stiff_x, stiff_y, stiff_z, mu, mu_x, mu_y, mu_xy = (
                coef[layer, n] for n in range(10)
            )
            rx, lx, sx = zip(*(slopes(v, 0, even_x) for v in value))
            ry, ly, sy = zip(*(slopes(v, 1, even_y) for v in value))
            common = for_x(lam_y * grad_z[2] + lam * sy[1])
            scale = for_x(stiff_y)
            force_x = along_x(scale * for_x(rx[0]) + common, scale * for_x(lx[0]) + common)
            common = for_x(mu * sy[0])
            scale = for_x(mu_y)
            force_y = along_x(scale * for_x(rx[1]) + common, scale * for_x(lx[1]) + common)
            common = for_x(grad_z[0])
            force_z = along_x(scale * (for_x(rx[2]) + common), scale * (for_x(lx[2]) + common))
            common = (lam_x * grad_z[2] + lam * sx[0])
            scale = (stiff_x)
            force_y += along_y(scale * (ry[1]) + common, scale * (ly[1]) + common)
            common = (mu * sx[1])
            scale = (mu_x)
            force_x += along_y(scale * (ry[0]) + common, scale * (ly[0]) + common)
            common = (grad_z[1])
            force_z += along_y(scale * ((ry[2]) + common), scale * ((ly[2]) + common))
            for c, value in enumerate((force_x, force_y, force_z)):
                forces[c][layer] = value
            z_terms[0][layer] = for_x(mu_xy * grad_z[0] + mu_y * sx[2])
            z_terms[1][layer] = for_x(mu_xy * grad_z[1] + mu_x * sy[2])
            z_terms[2][layer] = for_x(lam_y * sx[0] + lam_x * sy[1] + stiff_z * grad_z[2])
        for c in range(3):
            along_z = spread_z(z_terms[c])
            for layer in range(3):
                n = c * 3 + layer
                total = (forces[c][layer] + along_z[layer]) * for_x(coef[layer, 10])
                store(n, 2.0 * for_x(source(n)) - for_x(older(n)) - total)

    is_tail = lax.broadcasted_iota(jnp.int32, (EDGE, width), 0) < HALO
    tops = {}

    def keep(ref, n, value):
        ref[n] = value[:rows]
        if n % 3 == 2:
            first = jnp.where(is_tail, value[rows:], value[:EDGE])
            tops.setdefault(n // 3, []).append(jnp.concatenate([first, value[EDGE:rows]], axis=0))

    def keep_middle(n, value):
        mid[n] = value
        tail[(9 + n) * HALO : (10 + n) * HALO, :] = value[rows : rows + HALO, :width]
        keep(middle, n, value[:, :width])

    def keep_updated(n, value):
        tail[n * HALO : (n + 1) * HALO, :] = value[rows : rows + HALO]
        keep(updated, n, value)

    advance(lambda n: field[n], lambda n: field[9 + n], keep_middle, False)
    advance(lambda n: mid[n], lambda n: field[n], keep_updated, True)

    angles = facts[2 * peers : 2 * peers + 8]
    cosines, sines = jnp.cos(angles), jnp.sin(angles)
    low = lax.broadcasted_iota(jnp.int32, (rows, width), 1) < width // 2
    half = width // 2
    for b in range(2):
        for c in range(3):
            one, two = tops[c]
            item = b * 3 + c
            old = []
            for n in (2 * item, 2 * item + 1):
                first = jnp.where(is_tail, ahead[start + n], bins[n, :EDGE])
                old.append(jnp.concatenate([first, bins[n, EDGE:]], axis=0))
            real = old[0] + cosines[b : b + 1] * one + cosines[2 + b : 3 + b] * two
            imag = old[1] - sines[b : b + 1] * one - sines[2 + b : 3 + b] * two
            if item < 4:
                operand[pl.ds(3 * item * rows, rows, stride=3), :] = real
                operand[pl.ds(3 * item * rows + 1, rows, stride=3), :] = imag
            else:
                at = 3 * (item - 4) * rows + 2
                operand[pl.ds(at, rows, stride=3), :] = jnp.where(low, real, pltpu.roll(imag, half, 1))
                operand[pl.ds(at + 6 * rows, rows, stride=3), :] = jnp.where(
                    low, pltpu.roll(real, half, 1), imag
                )


def first_transform_kernel(received, table, tail, out, tail_out):
    tail_out[...] = tail[...]
    count, width = received.shape[0] // 3, received.shape[1]
    joined = jnp.concatenate([received[pl.ds(n, count, stride=3), :] for n in range(3)], axis=1)
    high, rest = halves(joined)
    both = jnp.dot(
        table[...], jnp.concatenate([high, rest, high], axis=0), preferred_element_type=jnp.float32
    )
    by_cos, by_sin = both[:count], both[count:]
    out[pl.ds(0, count, stride=3), :] = by_cos[:, :width] + by_sin[:, width : 2 * width]
    out[pl.ds(1, count, stride=3), :] = by_cos[:, width : 2 * width] - by_sin[:, :width]
    turned = pltpu.roll(by_sin[:, 2 * width :], width // 2, 1)
    low = lax.broadcasted_iota(jnp.int32, turned.shape, 1) < width // 2
    out[pl.ds(2, count, stride=3), :] = by_cos[:, 2 * width :] + jnp.where(low, turned, -turned)


def second_transform_kernel(facts, received, straight, turned, out):
    items, parts, rows, width = out.shape
    half = width // 2
    count = received.shape[0] // 3
    low = lax.broadcasted_iota(jnp.int32, (rows, width), 1) < half
    real, imag = [], []
    for item in range(items):
        if item < 4:
            real.append(received[pl.ds(3 * item * rows, rows, stride=3), :])
            imag.append(received[pl.ds(3 * item * rows + 1, rows, stride=3), :])
        else:
            at = 3 * (item - 4) * rows + 2
            one = received[pl.ds(at, rows, stride=3), :]
            two = received[pl.ds(at + 6 * rows, rows, stride=3), :]
            real.append(jnp.where(low, one, pltpu.roll(two, half, 1)))
            imag.append(jnp.where(low, pltpu.roll(one, half, 1), two))
    joined = jnp.concatenate([jnp.concatenate(real, axis=1), jnp.concatenate(imag, axis=1)], axis=0)
    slot = lax.broadcasted_iota(jnp.int32, straight.shape, 1) % rows
    node = jnp.where(slot < HALO, slot + rows, slot).astype(jnp.float32)
    place = facts[facts.shape[0] - 1 :, : slot.shape[1]]
    angle = node * place * (2.0 * np.pi / (rows * count))
    matrix = straight[...] * jnp.cos(angle) + turned[...] * jnp.sin(angle)
    left, left_rest = halves(matrix)
    high, rest = halves(joined)
    waves = jnp.dot(
        jnp.concatenate([left, left, left_rest], axis=1),
        jnp.concatenate([high, rest, high], axis=0),
        preferred_element_type=jnp.float32,
    )
    for item in range(items):
        for part in range(parts):
            out[item, part] = waves[part * rows : (part + 1) * rows, item * width : (item + 1) * width]


def set_in_kernel(updated, middle, tail, updated_out, middle_out):
    for k, (ref, out) in enumerate(((updated, updated_out), (middle, middle_out))):
        for n in range(ref.shape[0]):
            out[n] = ref[n]
            out[n, :HALO, :] = tail[(k * ref.shape[0] + n) * HALO : (k * ref.shape[0] + n + 1) * HALO, :]


def exchange(value):
    peers = lax.axis_size("gx")
    rows, width = value.shape
    shaped = value.reshape(peers, 1, rows // peers * width)
    return lax.all_to_all(shaped, "gx", split_axis=0, concat_axis=0, tiled=True).reshape(rows, width)


def exchange_gy(value):
    return lax.all_to_all(value, "gy", split_axis=0, concat_axis=0, tiled=True)


def pass_on(value, axis, step):
    peers = lax.axis_size(axis)
    return lax.ppermute(value, axis, [(i, (i + step) % peers) for i in range(peers)])


def f32(*shape):
    return jax.ShapeDtypeStruct(shape, jnp.float32)


def on_device(displacement, previous, moduli, density, bins, omega, phase):
    groups = lax.axis_size("gx")
    rows, width = density.shape[1:]
    items = bins.shape[0] * bins.shape[1]
    block = (rows, width)
    arrays = [a.reshape((-1,) + block) for a in (displacement, previous, moduli, density, bins)]
    planes = sum(a.shape[0] for a in arrays) - BINS
    packed = -(-planes * rows // width) * width
    total = packed + 2 * width
    select = jnp.asarray(edge_columns(width))
    peers = lax.axis_size("gy")
    distance = jnp.arange(peers) - lax.axis_index("gy")
    steps = jnp.arange(1, 3).astype(jnp.float32)
    facts = jnp.concatenate(
        [
            (distance == 1) | (distance == 1 - peers),
            (distance == -1) | (distance == peers - 1),
            (phase[None, :] + steps[:, None] * omega[None, :]).reshape(-1),
            jnp.full((4,), lax.axis_index("gx")),
        ],
        dtype=jnp.float32,
    )
    facts = jnp.broadcast_to(facts[:, None], (facts.shape[0], width))
    vmem = pl.BlockSpec(memory_space=pltpu.VMEM)
    hbm = pl.BlockSpec(memory_space=pltpu.HBM)
    params = pltpu.CompilerParams(vmem_limit_bytes=48 * 1024 * 1024)

    edge = pl.pallas_call(
        pack_rows_kernel,
        out_shape=f32(planes + BINS, EDGE, width),
        in_specs=[hbm] * 5,
        out_specs=vmem,
        scratch_shapes=[pltpu.SemaphoreType.DMA((5,))],
        compiler_params=pltpu.CompilerParams(vmem_limit_bytes=62 * 1024 * 1024),
    )(*arrays)
    main = pl.pallas_call(
        pack_main_kernel,
        out_shape=f32(EDGE, packed),
        in_specs=[vmem] * 5,
        out_specs=vmem,
        compiler_params=params,
        cost_estimate=pl.CostEstimate(flops=50_000_000, bytes_accessed=2_000_000, transcendentals=0),
    )(*arrays[:4], select)
    ahead = pass_on(edge, "gx", -1)
    sides = pl.pallas_call(
        pack_columns_kernel,
        out_shape=f32(peers, HALO, total),
        in_specs=[vmem] * 4,
        out_specs=vmem,
        compiler_params=params,
    )(facts, main, ahead, select)
    tall, wide = rows + EDGE, 2 * width
    updated, middle, tail, operand = pl.pallas_call(
        step_kernel,
        out_shape=(f32(9, *block), f32(9, *block), f32(18 * HALO, width), f32(3 * groups, width)),
        in_specs=[vmem] * 9,
        out_specs=(vmem,) * 4,
        scratch_shapes=[
            pltpu.VMEM((planes, tall, wide), jnp.float32),
            pltpu.VMEM((3, 11, tall, wide), jnp.float32),
            pltpu.VMEM((total, width), jnp.float32),
            pltpu.VMEM((9, tall, wide), jnp.float32),
        ],
        compiler_params=params,
    )(facts, *arrays, ahead, exchange_gy(sides), select)

    stacked = np.concatenate(fourier_tables(groups), axis=0)
    high = stacked.astype(ml_dtypes.bfloat16)
    rest = (stacked - high.astype(np.float64)).astype(ml_dtypes.bfloat16)
    table = jnp.asarray(np.concatenate([high, high, rest], axis=1))
    sections, tail = pl.pallas_call(
        first_transform_kernel,
        out_shape=(f32(3 * groups, width), f32(*tail.shape)),
        in_specs=[vmem] * 3,
        out_specs=(vmem,) * 2,
        compiler_params=params,
    )(exchange(operand), table, tail)
    updated, middle = pl.pallas_call(
        set_in_kernel,
        out_shape=(f32(9, *block), f32(9, *block)),
        in_specs=[vmem] * 3,
        out_specs=(vmem,) * 2,
        compiler_params=params,
        cost_estimate=pl.CostEstimate(flops=1_000_000, bytes_accessed=1_200_000, transcendentals=0),
    )(updated, middle, pass_on(tail, "gx", 1))
    scale = (groups * rows) ** -0.5
    c, s = (t * scale for t in fourier_tables(rows))
    straight = jnp.asarray(np.block([[c, s], [-s, c]]), jnp.float32)
    turned = jnp.asarray(np.block([[-s, c], [-c, -s]]), jnp.float32)
    spectrum = pl.pallas_call(
        second_transform_kernel,
        out_shape=f32(items, 2, *block),
        in_specs=[vmem] * 4,
        out_specs=vmem,
        compiler_params=params,
    )(facts, exchange(sections), straight, turned)
    return (
        updated.reshape(displacement.shape),
        middle.reshape(displacement.shape),
        spectrum.reshape(bins.shape),
    )


def solution(mesh):
    placed = (
        P(None, None, "gx", "gy"),
        P(None, None, "gx", "gy"),
        P(None, None, "gx", "gy"),
        P(None, "gx", "gy"),
        P(None, None, None, "gx", "gy"),
        P(),
        P(),
    )
    return jax.shard_map(
        on_device,
        mesh=mesh,
        in_specs=placed,
        out_specs=(
            P(None, None, "gx", "gy"),
            P(None, None, "gx", "gy"),
            P(None, None, None, "gx", "gy"),
        ),
        check_vma=False,
    )
```

```python
import jax
import jax.numpy as jnp
import ml_dtypes
import numpy as np
from jax import lax
from jax.experimental import pallas as pl
from jax.experimental.pallas import tpu as pltpu
from jax.sharding import PartitionSpec as P

time_step = 0.03
HALO = 4
EDGE = 8
BINS = 12


def edge_columns(width):
    table = np.zeros((EDGE, width), np.float32)
    for h in range(HALO):
        table[h, h] = 1.0
        table[HALO + h, width - HALO + h] = 1.0
    return table


def fourier_tables(length):
    index = np.arange(length)
    angle = 2.0 * np.pi * (index[:, None] * index[None, :] % length) / length
    return np.cos(angle), np.sin(angle)


def halves(value):
    high = value.astype(jnp.bfloat16)
    return high, (value - high.astype(jnp.float32)).astype(jnp.bfloat16)


def pick_columns(select, rows):
    chosen = select[...].astype(jnp.bfloat16)
    return lax.dot_general(
        jnp.concatenate([chosen, chosen], axis=1),
        jnp.concatenate(halves(rows), axis=1),
        (((1,), (1,)), ((), ())),
        preferred_element_type=jnp.float32,
    )


def pack_rows_kernel(disp, prev, moduli, density, bins, out, last, sems):
    copies = []
    start = 0
    for n, ref in enumerate((disp, prev, moduli, density, bins)):
        planes, rows, _ = ref.shape
        here = out.at[pl.ds(start, planes)] if n < 4 else last
        copies.append(pltpu.make_async_copy(ref.at[:, pl.ds(rows - EDGE, EDGE), :], here, sems.at[n]))
        start += planes if n < 4 else 0
    for copy in copies:
        copy.start()
    for copy in copies:
        copy.wait()
    for n in range(last.shape[0]):
        at = n % 2 * HALO
        out[start + n // 2, at : at + HALO, :] = last[n, EDGE - HALO :, :]


def pack_main_kernel(disp, prev, moduli, density, select, main):
    width = select.shape[1]
    whole = jnp.concatenate([ref[...].reshape(-1, width) for ref in (disp, prev, moduli, density)], axis=0)
    used = whole.shape[0]
    main[:, :used] = pick_columns(select, whole)
    main[:, used:] = jnp.zeros((EDGE, main.shape[1] - used), jnp.float32)


def pack_columns_kernel(facts, main, behind, select, out):
    peers, _, total = out.shape
    width = main.shape[1]
    planes = behind.shape[0] - BINS // 2
    rows = behind[:planes].reshape(planes * EDGE, select.shape[1])
    fill = jnp.zeros((total - width - rows.shape[0], rows.shape[1]), jnp.float32)
    packed = pick_columns(select, jnp.concatenate([rows, fill], axis=0))
    for slot in range(peers):
        after, before = (facts[n : n + 1, :1] > 0.5 for n in (slot, peers + slot))
        for source, at in ((main[...], 0), (packed, width)):
            chosen = jnp.where(after, source[HALO:], jnp.where(before, source[:HALO], 0.0))
            out[slot, :, at : at + source.shape[1]] = chosen


def shift(value, amount, axis):
    return pltpu.roll(value, (-amount) % value.shape[axis], axis)


def slopes(value, axis, even):
    ahead, ahead2 = shift(value, 1, axis), shift(value, 2, axis)
    back, back2 = shift(value, -1, axis), shift(value, -2, axis)
    right = jnp.where(even, 4.0 * ahead - 3.0 * value - ahead2, ahead - back)
    left = 3.0 * value - 4.0 * back + back2
    return right, left, jnp.where(even, right + left, right)


def spread(right, left, axis, even):
    ahead = jnp.where(even, -4.0 * left, -right)
    back = jnp.where(even, 4.0 * right, right)
    ahead = ahead + shift(jnp.where(even, left, 0.0), 1, axis)
    back = back - shift(jnp.where(even, right, 0.0), -1, axis)
    own = jnp.where(even, 3.0 * (left - right), 0.0)
    return own + shift(ahead, 1, axis) + shift(back, -1, axis)


def spread_z(layers):
    a, b, c = layers
    return c - b - 3.0 * a, 4.0 * (a - c), b - a + 3.0 * c


def step_kernel(
    facts, disp, prev, moduli, density, bins, behind, beside, select,
    updated, middle, tail, operand, field, coef, strip, mid,
):
    rows, width = disp.shape[1], disp.shape[2]
    tall, wide = rows + EDGE, 2 * width
    peers = beside.shape[0]
    halo_at = beside.shape[2] - 2 * width
    east = west = beside[0]
    for slot in range(1, peers):
        east = jnp.where(facts[slot : slot + 1, :1] > 0.5, beside[slot], east)
        west = jnp.where(facts[peers + slot : peers + slot + 1, :1] > 0.5, beside[slot], west)
    both = jnp.concatenate([east, west], axis=0)
    chosen = select[...].astype(jnp.bfloat16)
    strip[...] = lax.dot_general(
        jnp.concatenate(halves(both), axis=0),
        jnp.concatenate([chosen, chosen], axis=0),
        (((0,), (0,)), ((), ())),
        preferred_element_type=jnp.float32,
    )
    start = 0
    for ref in (disp, prev, moduli, density):
        for i in range(ref.shape[0]):
            n = start + i
            field[n, :rows, :width] = ref[i]
            field[n, rows:, :width] = behind[n]
            field[n, :rows, width:] = strip[n * rows : (n + 1) * rows, :]
            field[n, rows:, width:] = strip[halo_at + n * EDGE : halo_at + (n + 1) * EDGE, :]
        start += ref.shape[0]

    def tiled(tile, shape=(tall, wide)):
        line = jnp.concatenate([tile] * (shape[1] // tile.shape[1]), axis=1)
        return jnp.concatenate([line] * (shape[0] // tile.shape[0]), axis=0)

    tile_x, tile_y = (lax.broadcasted_iota(jnp.int32, (8, 128), axis) % 2 for axis in range(2))
    near_x, near_y = tiled(tile_x), tiled(tile_y)
    two_x, two_y = 2.0 - near_x.astype(jnp.float32), 2.0 - near_y.astype(jnp.float32)
    weight = (1.0 / 3.0 + near_x.astype(jnp.float32)) * (1.0 / 3.0 + near_y.astype(jnp.float32)) / 8.0
    lane = lax.broadcasted_iota(jnp.int32, (tall, wide), 1)
    unused = (lane >= width + HALO) & (lane < wide - HALO)
    for layer in range(3):
        weight_z = 4.0 / 3.0 if layer == 1 else 1.0 / 3.0
        here = weight * weight_z
        lam = field[18 + layer] * here
        mu = field[21 + layer] * here
        mu_x, mu_y = mu * two_x, mu * two_y
        mu_xy = mu_x * two_y
        lam_x, lam_y = lam * two_x, lam * two_y
        mass = jnp.where(unused, 1.0, field[24 + layer]) * (here * two_x * two_y)
        for n, value in enumerate(
            (lam, lam_x, lam_y, lam_x + 2.0 * mu_x, lam_y + 2.0 * mu_y, lam_x * two_y + 2.0 * mu_xy,
             mu, mu_x, mu_y, mu_xy, time_step * time_step / mass)
        ):
            coef[layer, n] = value

    def advance(source, older, store, own):
        out_width = width if own else wide
        even_x, even_y = near_x == 0, near_y == 0
        even_xs = even_x[:, :out_width]

        def for_x(value):
            return value[:, :out_width]

        def along_x(right, left):
            return spread(right, left, 0, even_xs)

        def along_y(right, left):
            return spread(right, left, 1, even_y)[:, :out_width]

        forces = [[None] * 3 for _ in range(3)]
        z_terms = [[None] * 3 for _ in range(3)]
        for layer in range(3):
            value = [source(c * 3 + layer) for c in range(3)]
            grad_z = []
            for c in range(3):
                a, b, d = (source(c * 3 + n) for n in range(3))
                if layer == 0:
                    grad_z.append(4.0 * b - 3.0 * a - d)
                elif layer == 1:
                    grad_z.append(d - a)
                else:
                    grad_z.append(a - 4.0 * b + 3.0 * d)
            lam, lam_x, lam_y, stiff_x, stiff_y, stiff_z, mu, mu_x, mu_y, mu_xy = (
                coef[layer, n] for n in range(10)
            )
            rx, lx, sx = zip(*(slopes(v, 0, even_x) for v in value))
            ry, ly, sy = zip(*(slopes(v, 1, even_y) for v in value))
            common = for_x(lam_y * grad_z[2] + lam * sy[1])
            scale = for_x(stiff_y)
            force_x = along_x(scale * for_x(rx[0]) + common, scale * for_x(lx[0]) + common)
            common = for_x(mu * sy[0])
            scale = for_x(mu_y)
            force_y = along_x(scale * for_x(rx[1]) + common, scale * for_x(lx[1]) + common)
            common = for_x(grad_z[0])
            force_z = along_x(scale * (for_x(rx[2]) + common), scale * (for_x(lx[2]) + common))
            common = (lam_x * grad_z[2] + lam * sx[0])
            scale = (stiff_x)
            force_y += along_y(scale * (ry[1]) + common, scale * (ly[1]) + common)
            common = (mu * sx[1])
            scale = (mu_x)
            force_x += along_y(scale * (ry[0]) + common, scale * (ly[0]) + common)
            common = (grad_z[1])
            force_z += along_y(scale * ((ry[2]) + common), scale * ((ly[2]) + common))
            for c, value in enumerate((force_x, force_y, force_z)):
                forces[c][layer] = value
            z_terms[0][layer] = for_x(mu_xy * grad_z[0] + mu_y * sx[2])
            z_terms[1][layer] = for_x(mu_xy * grad_z[1] + mu_x * sy[2])
            z_terms[2][layer] = for_x(lam_y * sx[0] + lam_x * sy[1] + stiff_z * grad_z[2])
        for c in range(3):
            along_z = spread_z(z_terms[c])
            for layer in range(3):
                n = c * 3 + layer
                total = (forces[c][layer] + along_z[layer]) * for_x(coef[layer, 10])
                store(n, 2.0 * for_x(source(n)) - for_x(older(n)) - total)

    is_tail = lax.broadcasted_iota(jnp.int32, (EDGE, width), 0) >= HALO
    tops = {}

    def keep(ref, n, value):
        ref[n] = value[:rows]
        if n % 3 == 2:
            last = jnp.where(is_tail, value[rows:], value[rows - EDGE : rows])
            tops.setdefault(n // 3, []).append(jnp.concatenate([value[: rows - EDGE], last], axis=0))

    def keep_middle(n, value):
        mid[n] = value
        tail[(9 + n) * HALO : (10 + n) * HALO, :] = value[rows + HALO :, :width]
        keep(middle, n, value[:, :width])

    def keep_updated(n, value):
        tail[n * HALO : (n + 1) * HALO, :] = value[rows + HALO :]
        keep(updated, n, value)

    advance(lambda n: field[n], lambda n: field[9 + n], keep_middle, False)
    advance(lambda n: mid[n], lambda n: field[n], keep_updated, True)

    angles = facts[2 * peers : 2 * peers + 8]
    cosines, sines = jnp.cos(angles), jnp.sin(angles)
    low = lax.broadcasted_iota(jnp.int32, (rows, width), 1) < width // 2
    half = width // 2
    for b in range(2):
        for c in range(3):
            one, two = tops[c]
            item = b * 3 + c
            old = []
            rest = behind[start + item]
            for n, other in ((2 * item, pltpu.roll(rest, HALO, 0)), (2 * item + 1, rest)):
                last = jnp.where(is_tail, other, bins[n, rows - EDGE :])
                old.append(jnp.concatenate([bins[n, : rows - EDGE], last], axis=0))
            real = old[0] + cosines[b : b + 1] * one + cosines[2 + b : 3 + b] * two
            imag = old[1] - sines[b : b + 1] * one - sines[2 + b : 3 + b] * two
            if item < 4:
                operand[pl.ds(3 * item * rows, rows, stride=3), :] = real
                operand[pl.ds(3 * item * rows + 1, rows, stride=3), :] = imag
            else:
                at = 3 * (item - 4) * rows + 2
                operand[pl.ds(at, rows, stride=3), :] = jnp.where(low, real, pltpu.roll(imag, half, 1))
                operand[pl.ds(at + 6 * rows, rows, stride=3), :] = jnp.where(
                    low, pltpu.roll(real, half, 1), imag
                )


def first_transform_kernel(received, table, tail, out, tail_out):
    tail_out[...] = tail[...]
    count, width = received.shape[0] // 3, received.shape[1]
    joined = jnp.concatenate([received[pl.ds(n, count, stride=3), :] for n in range(3)], axis=1)
    high, rest = halves(joined)
    both = jnp.dot(
        table[...], jnp.concatenate([high, rest, high], axis=0), preferred_element_type=jnp.float32
    )
    by_cos, by_sin = both[:count], both[count:]
    out[pl.ds(0, count, stride=3), :] = by_cos[:, :width] + by_sin[:, width : 2 * width]
    out[pl.ds(1, count, stride=3), :] = by_cos[:, width : 2 * width] - by_sin[:, :width]
    turned = pltpu.roll(by_sin[:, 2 * width :], width // 2, 1)
    low = lax.broadcasted_iota(jnp.int32, turned.shape, 1) < width // 2
    out[pl.ds(2, count, stride=3), :] = by_cos[:, 2 * width :] + jnp.where(low, turned, -turned)


def second_transform_kernel(facts, received, straight, turned, out):
    items, parts, rows, width = out.shape
    half = width // 2
    count = received.shape[0] // 3
    low = lax.broadcasted_iota(jnp.int32, (rows, width), 1) < half
    real, imag = [], []
    for item in range(items):
        if item < 4:
            real.append(received[pl.ds(3 * item * rows, rows, stride=3), :])
            imag.append(received[pl.ds(3 * item * rows + 1, rows, stride=3), :])
        else:
            at = 3 * (item - 4) * rows + 2
            one = received[pl.ds(at, rows, stride=3), :]
            two = received[pl.ds(at + 6 * rows, rows, stride=3), :]
            real.append(jnp.where(low, one, pltpu.roll(two, half, 1)))
            imag.append(jnp.where(low, pltpu.roll(one, half, 1), two))
    joined = jnp.concatenate([jnp.concatenate(real, axis=1), jnp.concatenate(imag, axis=1)], axis=0)
    slot = lax.broadcasted_iota(jnp.int32, straight.shape, 1) % rows
    node = jnp.where(slot < rows - HALO, slot, slot - rows).astype(jnp.float32)
    place = facts[facts.shape[0] - 1 :, : slot.shape[1]]
    angle = node * place * (2.0 * np.pi / (rows * count))
    matrix = straight[...] * jnp.cos(angle) + turned[...] * jnp.sin(angle)
    left, left_rest = halves(matrix)
    high, rest = halves(joined)
    waves = jnp.dot(
        jnp.concatenate([left, left, left_rest], axis=1),
        jnp.concatenate([high, rest, high], axis=0),
        preferred_element_type=jnp.float32,
    )
    for item in range(items):
        for part in range(parts):
            out[item, part] = waves[part * rows : (part + 1) * rows, item * width : (item + 1) * width]


def set_in_kernel(updated, middle, tail, updated_out, middle_out):
    for k, (ref, out) in enumerate(((updated, updated_out), (middle, middle_out))):
        for n in range(ref.shape[0]):
            out[n] = ref[n]
            out[n, -HALO:, :] = tail[(k * ref.shape[0] + n) * HALO : (k * ref.shape[0] + n + 1) * HALO, :]


def exchange(value):
    peers = lax.axis_size("gx")
    rows, width = value.shape
    shaped = value.reshape(peers, 1, rows // peers * width)
    return lax.all_to_all(shaped, "gx", split_axis=0, concat_axis=0, tiled=True).reshape(rows, width)


def exchange_gy(value):
    return lax.all_to_all(value, "gy", split_axis=0, concat_axis=0, tiled=True)


def pass_on(value, axis, step):
    peers = lax.axis_size(axis)
    return lax.ppermute(value, axis, [(i, (i + step) % peers) for i in range(peers)])


def f32(*shape):
    return jax.ShapeDtypeStruct(shape, jnp.float32)


def on_device(displacement, previous, moduli, density, bins, omega, phase):
    groups = lax.axis_size("gx")
    rows, width = density.shape[1:]
    items = bins.shape[0] * bins.shape[1]
    block = (rows, width)
    arrays = [a.reshape((-1,) + block) for a in (displacement, previous, moduli, density, bins)]
    planes = sum(a.shape[0] for a in arrays) - BINS
    packed = -(-planes * rows // width) * width
    total = packed + 2 * width
    select = jnp.asarray(edge_columns(width))
    peers = lax.axis_size("gy")
    distance = jnp.arange(peers) - lax.axis_index("gy")
    steps = jnp.arange(1, 3).astype(jnp.float32)
    facts = jnp.concatenate(
        [
            (distance == 1) | (distance == 1 - peers),
            (distance == -1) | (distance == peers - 1),
            (phase[None, :] + steps[:, None] * omega[None, :]).reshape(-1),
            jnp.full((4,), lax.axis_index("gx")),
        ],
        dtype=jnp.float32,
    )
    facts = jnp.broadcast_to(facts[:, None], (facts.shape[0], width))
    vmem = pl.BlockSpec(memory_space=pltpu.VMEM)
    hbm = pl.BlockSpec(memory_space=pltpu.HBM)
    params = pltpu.CompilerParams(vmem_limit_bytes=48 * 1024 * 1024)

    edge = pl.pallas_call(
        pack_rows_kernel,
        out_shape=f32(planes + BINS // 2, EDGE, width),
        in_specs=[hbm] * 5,
        out_specs=vmem,
        scratch_shapes=[pltpu.VMEM((BINS, EDGE, width), jnp.float32), pltpu.SemaphoreType.DMA((5,))],
        compiler_params=pltpu.CompilerParams(vmem_limit_bytes=62 * 1024 * 1024),
    )(*arrays)
    main = pl.pallas_call(
        pack_main_kernel,
        out_shape=f32(EDGE, packed),
        in_specs=[vmem] * 5,
        out_specs=vmem,
        compiler_params=params,
        cost_estimate=pl.CostEstimate(flops=50_000_000, bytes_accessed=2_000_000, transcendentals=0),
    )(*arrays[:4], select)
    behind = pass_on(edge, "gx", 1)
    sides = pl.pallas_call(
        pack_columns_kernel,
        out_shape=f32(peers, HALO, total),
        in_specs=[vmem] * 4,
        out_specs=vmem,
        compiler_params=params,
    )(facts, main, behind, select)
    tall, wide = rows + EDGE, 2 * width
    updated, middle, tail, operand = pl.pallas_call(
        step_kernel,
        out_shape=(f32(9, *block), f32(9, *block), f32(18 * HALO, width), f32(3 * groups, width)),
        in_specs=[vmem] * 9,
        out_specs=(vmem,) * 4,
        scratch_shapes=[
            pltpu.VMEM((planes, tall, wide), jnp.float32),
            pltpu.VMEM((3, 11, tall, wide), jnp.float32),
            pltpu.VMEM((total, width), jnp.float32),
            pltpu.VMEM((9, tall, wide), jnp.float32),
        ],
        compiler_params=params,
    )(facts, *arrays, behind, exchange_gy(sides), select)

    stacked = np.concatenate(fourier_tables(groups), axis=0)
    high = stacked.astype(ml_dtypes.bfloat16)
    rest = (stacked - high.astype(np.float64)).astype(ml_dtypes.bfloat16)
    table = jnp.asarray(np.concatenate([high, high, rest], axis=1))
    sections, tail = pl.pallas_call(
        first_transform_kernel,
        out_shape=(f32(3 * groups, width), f32(*tail.shape)),
        in_specs=[vmem] * 3,
        out_specs=(vmem,) * 2,
        compiler_params=params,
    )(exchange(operand), table, tail)
    updated, middle = pl.pallas_call(
        set_in_kernel,
        out_shape=(f32(9, *block), f32(9, *block)),
        in_specs=[vmem] * 3,
        out_specs=(vmem,) * 2,
        compiler_params=params,
        cost_estimate=pl.CostEstimate(flops=1_000_000, bytes_accessed=1_200_000, transcendentals=0),
    )(updated, middle, pass_on(tail, "gx", -1))
    scale = (groups * rows) ** -0.5
    c, s = (t * scale for t in fourier_tables(rows))
    straight = jnp.asarray(np.block([[c, s], [-s, c]]), jnp.float32)
    turned = jnp.asarray(np.block([[-s, c], [-c, -s]]), jnp.float32)
    spectrum = pl.pallas_call(
        second_transform_kernel,
        out_shape=f32(items, 2, *block),
        in_specs=[vmem] * 4,
        out_specs=vmem,
        compiler_params=params,
    )(facts, exchange(sections), straight, turned)
    return (
        updated.reshape(displacement.shape),
        middle.reshape(displacement.shape),
        spectrum.reshape(bins.shape),
    )


def solution(mesh):
    placed = (
        P(None, None, "gx", "gy"),
        P(None, None, "gx", "gy"),
        P(None, None, "gx", "gy"),
        P(None, "gx", "gy"),
        P(None, None, None, "gx", "gy"),
        P(),
        P(),
    )
    return jax.shard_map(
        on_device,
        mesh=mesh,
        in_specs=placed,
        out_specs=(
            P(None, None, "gx", "gy"),
            P(None, None, "gx", "gy"),
            P(None, None, None, "gx", "gy"),
        ),
        check_vma=False,
    )
```

```python
import jax
import jax.numpy as jnp
import ml_dtypes
import numpy as np
from jax import lax
from jax.experimental import pallas as pl
from jax.experimental.pallas import tpu as pltpu
from jax.sharding import PartitionSpec as P

time_step = 0.03
HALO = 4
EDGE = 8
BINS = 12


def edge_columns(width):
    table = np.zeros((EDGE, width), np.float32)
    for h in range(HALO):
        table[h, h] = 1.0
        table[HALO + h, width - HALO + h] = 1.0
    return table


def fourier_tables(length):
    index = np.arange(length)
    angle = 2.0 * np.pi * (index[:, None] * index[None, :] % length) / length
    return np.cos(angle), np.sin(angle)


def halves(value):
    high = value.astype(jnp.bfloat16)
    return high, (value - high.astype(jnp.float32)).astype(jnp.bfloat16)


def pick_columns(select, rows):
    chosen = select[...].astype(jnp.bfloat16)
    return lax.dot_general(
        jnp.concatenate([chosen, chosen], axis=1),
        jnp.concatenate(halves(rows), axis=1),
        (((1,), (1,)), ((), ())),
        preferred_element_type=jnp.float32,
    )


def pack_rows_kernel(disp, prev, moduli, density, bins, out, last, sems):
    copies = []
    start = 0
    for n, ref in enumerate((disp, prev, moduli, density, bins)):
        planes, rows, _ = ref.shape
        here = out.at[pl.ds(start, planes)] if n < 4 else last
        copies.append(pltpu.make_async_copy(ref.at[:, pl.ds(rows - EDGE, EDGE), :], here, sems.at[n]))
        start += planes if n < 4 else 0
    for copy in copies:
        copy.start()
    for copy in copies:
        copy.wait()
    for n in range(last.shape[0]):
        at = n % 2 * HALO
        out[start + n // 2, at : at + HALO, :] = last[n, EDGE - HALO :, :]


def pack_main_kernel(disp, prev, moduli, density, select, main):
    width = select.shape[1]
    whole = jnp.concatenate([ref[...].reshape(-1, width) for ref in (disp, prev, moduli, density)], axis=0)
    used = whole.shape[0]
    main[:, :used] = pick_columns(select, whole)
    main[:, used:] = jnp.zeros((EDGE, main.shape[1] - used), jnp.float32)


def pack_columns_kernel(facts, main, behind, select, out):
    peers, _, total = out.shape
    width = main.shape[1]
    planes = behind.shape[0] - BINS // 2
    rows = behind[:planes].reshape(planes * EDGE, select.shape[1])
    fill = jnp.zeros((total - width - rows.shape[0], rows.shape[1]), jnp.float32)
    packed = pick_columns(select, jnp.concatenate([rows, fill], axis=0))
    for slot in range(peers):
        after, before = (facts[n : n + 1, :1] > 0.5 for n in (slot, peers + slot))
        for source, at in ((main[...], 0), (packed, width)):
            chosen = jnp.where(after, source[HALO:], jnp.where(before, source[:HALO], 0.0))
            out[slot, :, at : at + source.shape[1]] = chosen


def shift(value, amount, axis):
    return pltpu.roll(value, (-amount) % value.shape[axis], axis)


def slopes(value, axis, even):
    ahead, ahead2 = shift(value, 1, axis), shift(value, 2, axis)
    back, back2 = shift(value, -1, axis), shift(value, -2, axis)
    right = jnp.where(even, 4.0 * ahead - 3.0 * value - ahead2, ahead - back)
    left = 3.0 * value - 4.0 * back + back2
    return right, left, jnp.where(even, right + left, right)


def spread(right, left, axis, even):
    ahead = jnp.where(even, -4.0 * left, -right)
    back = jnp.where(even, 4.0 * right, right)
    ahead = ahead + shift(jnp.where(even, left, 0.0), 1, axis)
    back = back - shift(jnp.where(even, right, 0.0), -1, axis)
    own = jnp.where(even, 3.0 * (left - right), 0.0)
    return own + shift(ahead, 1, axis) + shift(back, -1, axis)


def spread_z(layers):
    a, b, c = layers
    return c - b - 3.0 * a, 4.0 * (a - c), b - a + 3.0 * c


def step_kernel(
    facts, disp, prev, moduli, density, bins, behind, beside, select,
    updated, middle, tail, operand, field, coef, strip, mid,
):
    rows, width = disp.shape[1], disp.shape[2]
    tall, wide = rows + EDGE, 2 * width
    peers = beside.shape[0]
    halo_at = beside.shape[2] - 2 * width
    east = west = beside[0]
    for slot in range(1, peers):
        east = jnp.where(facts[slot : slot + 1, :1] > 0.5, beside[slot], east)
        west = jnp.where(facts[peers + slot : peers + slot + 1, :1] > 0.5, beside[slot], west)
    both = jnp.concatenate([east, west], axis=0)
    chosen = select[...].astype(jnp.bfloat16)
    strip[...] = lax.dot_general(
        jnp.concatenate(halves(both), axis=0),
        jnp.concatenate([chosen, chosen], axis=0),
        (((0,), (0,)), ((), ())),
        preferred_element_type=jnp.float32,
    )
    start = 0
    for ref in (disp, prev, moduli, density):
        for i in range(ref.shape[0]):
            n = start + i
            field[n, :rows, :width] = ref[i]
            field[n, rows:, :width] = behind[n]
            field[n, :rows, width:] = strip[n * rows : (n + 1) * rows, :]
            field[n, rows:, width:] = strip[halo_at + n * EDGE : halo_at + (n + 1) * EDGE, :]
        start += ref.shape[0]

    def tiled(tile, shape=(tall, wide)):
        line = jnp.concatenate([tile] * (shape[1] // tile.shape[1]), axis=1)
        return jnp.concatenate([line] * (shape[0] // tile.shape[0]), axis=0)

    tile_x, tile_y = (lax.broadcasted_iota(jnp.int32, (8, 128), axis) % 2 for axis in range(2))
    near_x, near_y = tiled(tile_x), tiled(tile_y)
    two_x, two_y = 2.0 - near_x.astype(jnp.float32), 2.0 - near_y.astype(jnp.float32)
    weight = (1.0 / 3.0 + near_x.astype(jnp.float32)) * (1.0 / 3.0 + near_y.astype(jnp.float32)) / 8.0
    lane = lax.broadcasted_iota(jnp.int32, (tall, wide), 1)
    unused = (lane >= width + HALO) & (lane < wide - HALO)
    for layer in range(3):
        weight_z = 4.0 / 3.0 if layer == 1 else 1.0 / 3.0
        here = weight * weight_z
        lam = field[18 + layer] * here
        mu = field[21 + layer] * here
        mu_x, mu_y = mu * two_x, mu * two_y
        mu_xy = mu_x * two_y
        lam_x, lam_y = lam * two_x, lam * two_y
        mass = jnp.where(unused, 1.0, field[24 + layer]) * (here * two_x * two_y)
        for n, value in enumerate(
            (lam, lam_x, lam_y, lam_x + 2.0 * mu_x, lam_y + 2.0 * mu_y, lam_x * two_y + 2.0 * mu_xy,
             mu, mu_x, mu_y, mu_xy, time_step * time_step / mass)
        ):
            coef[layer, n] = value

    def advance(source, older, store, own):
        out_width = width if own else wide
        even_x, even_y = near_x == 0, near_y == 0
        even_xs = even_x[:, :out_width]

        def for_x(value):
            return value[:, :out_width]

        def along_x(right, left):
            return spread(right, left, 0, even_xs)

        def along_y(right, left):
            return spread(right, left, 1, even_y)[:, :out_width]

        forces = [[None] * 3 for _ in range(3)]
        z_terms = [[None] * 3 for _ in range(3)]
        for layer in range(3):
            value = [source(c * 3 + layer) for c in range(3)]
            grad_z = []
            for c in range(3):
                a, b, d = (source(c * 3 + n) for n in range(3))
                if layer == 0:
                    grad_z.append(4.0 * b - 3.0 * a - d)
                elif layer == 1:
                    grad_z.append(d - a)
                else:
                    grad_z.append(a - 4.0 * b + 3.0 * d)
            lam, lam_x, lam_y, stiff_x, stiff_y, stiff_z, mu, mu_x, mu_y, mu_xy = (
                coef[layer, n] for n in range(10)
            )
            rx, lx, sx = zip(*(slopes(v, 0, even_x) for v in value))
            ry, ly, sy = zip(*(slopes(v, 1, even_y) for v in value))
            common = for_x(lam_y * grad_z[2] + lam * sy[1])
            scale = for_x(stiff_y)
            force_x = along_x(scale * for_x(rx[0]) + common, scale * for_x(lx[0]) + common)
            common = for_x(mu * sy[0])
            scale = for_x(mu_y)
            force_y = along_x(scale * for_x(rx[1]) + common, scale * for_x(lx[1]) + common)
            common = for_x(grad_z[0])
            force_z = along_x(scale * (for_x(rx[2]) + common), scale * (for_x(lx[2]) + common))
            common = (lam_x * grad_z[2] + lam * sx[0])
            scale = (stiff_x)
            force_y += along_y(scale * (ry[1]) + common, scale * (ly[1]) + common)
            common = (mu * sx[1])
            scale = (mu_x)
            force_x += along_y(scale * (ry[0]) + common, scale * (ly[0]) + common)
            common = (grad_z[1])
            force_z += along_y(scale * ((ry[2]) + common), scale * ((ly[2]) + common))
            for c, value in enumerate((force_x, force_y, force_z)):
                forces[c][layer] = value
            z_terms[0][layer] = for_x(mu_xy * grad_z[0] + mu_y * sx[2])
            z_terms[1][layer] = for_x(mu_xy * grad_z[1] + mu_x * sy[2])
            z_terms[2][layer] = for_x(lam_y * sx[0] + lam_x * sy[1] + stiff_z * grad_z[2])
        for c in range(3):
            along_z = spread_z(z_terms[c])
            for layer in range(3):
                n = c * 3 + layer
                total = (forces[c][layer] + along_z[layer]) * for_x(coef[layer, 10])
                store(n, 2.0 * for_x(source(n)) - for_x(older(n)) - total)

    is_tail = lax.broadcasted_iota(jnp.int32, (EDGE, width), 0) >= HALO
    tops = {}

    def keep(ref, n, value):
        ref[n] = value[:rows]
        if n % 3 == 2:
            last = jnp.where(is_tail, value[rows:], value[rows - EDGE : rows])
            tops.setdefault(n // 3, []).append(jnp.concatenate([value[: rows - EDGE], last], axis=0))

    def keep_middle(n, value):
        mid[n] = value
        tail[(9 + n) * HALO : (10 + n) * HALO, :] = value[rows + HALO :, :width]
        keep(middle, n, value[:, :width])

    def keep_updated(n, value):
        tail[n * HALO : (n + 1) * HALO, :] = value[rows + HALO :]
        keep(updated, n, value)

    advance(lambda n: field[n], lambda n: field[9 + n], keep_middle, False)
    advance(lambda n: mid[n], lambda n: field[n], keep_updated, True)

    angles = facts[2 * peers : 2 * peers + 8]
    cosines, sines = jnp.cos(angles), jnp.sin(angles)
    low = lax.broadcasted_iota(jnp.int32, (rows, width), 1) < width // 2
    half = width // 2
    for b in range(2):
        for c in range(3):
            one, two = tops[c]
            item = b * 3 + c
            old = []
            rest = behind[start + item]
            for n, other in ((2 * item, pltpu.roll(rest, HALO, 0)), (2 * item + 1, rest)):
                last = jnp.where(is_tail, other, bins[n, rows - EDGE :])
                old.append(jnp.concatenate([bins[n, : rows - EDGE], last], axis=0))
            real = old[0] + cosines[b : b + 1] * one + cosines[2 + b : 3 + b] * two
            imag = old[1] - sines[b : b + 1] * one - sines[2 + b : 3 + b] * two
            if item < 4:
                operand[pl.ds(3 * item * rows, rows, stride=3), :] = real
                operand[pl.ds(3 * item * rows + 1, rows, stride=3), :] = imag
            else:
                at = 3 * (item - 4) * rows + 2
                operand[pl.ds(at, rows, stride=3), :] = jnp.where(low, real, pltpu.roll(imag, half, 1))
                operand[pl.ds(at + 6 * rows, rows, stride=3), :] = jnp.where(
                    low, pltpu.roll(real, half, 1), imag
                )


def first_transform_kernel(received, table, tail, out, tail_out):
    tail_out[...] = tail[...]
    count, width = received.shape[0] // 3, received.shape[1]
    joined = jnp.concatenate([received[pl.ds(n, count, stride=3), :] for n in range(3)], axis=1)
    high, rest = halves(joined)
    both = jnp.dot(
        table[...], jnp.concatenate([high, rest, high], axis=0), preferred_element_type=jnp.float32
    )
    by_cos, by_sin = both[:count], both[count:]
    out[pl.ds(0, count, stride=3), :] = by_cos[:, :width] + by_sin[:, width : 2 * width]
    out[pl.ds(1, count, stride=3), :] = by_cos[:, width : 2 * width] - by_sin[:, :width]
    turned = pltpu.roll(by_sin[:, 2 * width :], width // 2, 1)
    low = lax.broadcasted_iota(jnp.int32, turned.shape, 1) < width // 2
    out[pl.ds(2, count, stride=3), :] = by_cos[:, 2 * width :] + jnp.where(low, turned, -turned)


def second_transform_kernel(facts, received, straight, turned, out):
    items, parts, rows, width = out.shape
    half = width // 2
    count = received.shape[0] // 3
    low = lax.broadcasted_iota(jnp.int32, (rows, width), 1) < half
    real, imag = [], []
    for item in range(items):
        if item < 4:
            real.append(received[pl.ds(3 * item * rows, rows, stride=3), :])
            imag.append(received[pl.ds(3 * item * rows + 1, rows, stride=3), :])
        else:
            at = 3 * (item - 4) * rows + 2
            one = received[pl.ds(at, rows, stride=3), :]
            two = received[pl.ds(at + 6 * rows, rows, stride=3), :]
            real.append(jnp.where(low, one, pltpu.roll(two, half, 1)))
            imag.append(jnp.where(low, pltpu.roll(one, half, 1), two))
    joined = jnp.concatenate([jnp.concatenate(real, axis=1), jnp.concatenate(imag, axis=1)], axis=0)
    slot = lax.broadcasted_iota(jnp.int32, straight.shape, 1) % rows
    node = jnp.where(slot < rows - HALO, slot, slot - rows).astype(jnp.float32)
    place = facts[facts.shape[0] - 1 :, : slot.shape[1]]
    angle = node * place * (2.0 * np.pi / (rows * count))
    matrix = straight[...] * jnp.cos(angle) + turned[...] * jnp.sin(angle)
    left, left_rest = halves(matrix)
    high, rest = halves(joined)
    waves = jnp.dot(
        jnp.concatenate([left, left, left_rest], axis=1),
        jnp.concatenate([high, rest, high], axis=0),
        preferred_element_type=jnp.float32,
    )
    for item in range(items):
        for part in range(parts):
            out[item, part] = waves[part * rows : (part + 1) * rows, item * width : (item + 1) * width]


def set_in_kernel(updated, middle, tail, updated_out, middle_out):
    for k, (ref, out) in enumerate(((updated, updated_out), (middle, middle_out))):
        for n in range(ref.shape[0]):
            out[n] = ref[n]
            out[n, -HALO:, :] = tail[(k * ref.shape[0] + n) * HALO : (k * ref.shape[0] + n + 1) * HALO, :]


def exchange(value):
    peers = lax.axis_size("gx")
    rows, width = value.shape
    shaped = value.reshape(peers, 1, rows // peers * width)
    return lax.all_to_all(shaped, "gx", split_axis=0, concat_axis=0, tiled=True).reshape(rows, width)


def exchange_gy(value):
    return lax.all_to_all(value, "gy", split_axis=0, concat_axis=0, tiled=True)


def pass_on(value, axis, step):
    peers = lax.axis_size(axis)
    return lax.ppermute(value, axis, [(i, (i + step) % peers) for i in range(peers)])


def f32(*shape):
    return jax.ShapeDtypeStruct(shape, jnp.float32)


def on_device(displacement, previous, moduli, density, bins, omega, phase):
    groups = lax.axis_size("gx")
    rows, width = density.shape[1:]
    items = bins.shape[0] * bins.shape[1]
    block = (rows, width)
    arrays = [a.reshape((-1,) + block) for a in (displacement, previous, moduli, density, bins)]
    planes = sum(a.shape[0] for a in arrays) - BINS
    packed = -(-planes * rows // width) * width
    total = packed + 2 * width
    select = jnp.asarray(edge_columns(width))
    peers = lax.axis_size("gy")
    distance = jnp.arange(peers) - lax.axis_index("gy")
    steps = jnp.arange(1, 3).astype(jnp.float32)
    facts = jnp.concatenate(
        [
            (distance == 1) | (distance == 1 - peers),
            (distance == -1) | (distance == peers - 1),
            (phase[None, :] + steps[:, None] * omega[None, :]).reshape(-1),
            jnp.full((4,), lax.axis_index("gx")),
        ],
        dtype=jnp.float32,
    )
    facts = jnp.broadcast_to(facts[:, None], (facts.shape[0], width))
    vmem = pl.BlockSpec(memory_space=pltpu.VMEM)
    hbm = pl.BlockSpec(memory_space=pltpu.HBM)
    params = pltpu.CompilerParams(vmem_limit_bytes=48 * 1024 * 1024)

    edge = pl.pallas_call(
        pack_rows_kernel,
        out_shape=pltpu.VMEM((planes + BINS // 2, EDGE, width), jnp.float32),
        in_specs=[hbm] * 5,
        out_specs=vmem,
        scratch_shapes=[pltpu.VMEM((BINS, EDGE, width), jnp.float32), pltpu.SemaphoreType.DMA((5,))],
        compiler_params=pltpu.CompilerParams(vmem_limit_bytes=60 * 1024 * 1024),
    )(*arrays)
    main = pl.pallas_call(
        pack_main_kernel,
        out_shape=f32(EDGE, packed),
        in_specs=[vmem] * 5,
        out_specs=vmem,
        compiler_params=params,
        cost_estimate=pl.CostEstimate(flops=50_000_000, bytes_accessed=2_000_000, transcendentals=0),
    )(*arrays[:4], select)
    behind = pass_on(edge, "gx", 1)
    sides = pl.pallas_call(
        pack_columns_kernel,
        out_shape=f32(peers, HALO, total),
        in_specs=[vmem] * 4,
        out_specs=vmem,
        compiler_params=params,
    )(facts, main, behind, select)
    tall, wide = rows + EDGE, 2 * width
    updated, middle, tail, operand = pl.pallas_call(
        step_kernel,
        out_shape=(f32(9, *block), f32(9, *block), f32(18 * HALO, width), f32(3 * groups, width)),
        in_specs=[vmem] * 9,
        out_specs=(vmem,) * 4,
        scratch_shapes=[
            pltpu.VMEM((planes, tall, wide), jnp.float32),
            pltpu.VMEM((3, 11, tall, wide), jnp.float32),
            pltpu.VMEM((total, width), jnp.float32),
            pltpu.VMEM((9, tall, wide), jnp.float32),
        ],
        compiler_params=params,
    )(facts, *arrays, behind, exchange_gy(sides), select)

    stacked = np.concatenate(fourier_tables(groups), axis=0)
    high = stacked.astype(ml_dtypes.bfloat16)
    rest = (stacked - high.astype(np.float64)).astype(ml_dtypes.bfloat16)
    table = jnp.asarray(np.concatenate([high, high, rest], axis=1))
    sections, tail = pl.pallas_call(
        first_transform_kernel,
        out_shape=(f32(3 * groups, width), f32(*tail.shape)),
        in_specs=[vmem] * 3,
        out_specs=(vmem,) * 2,
        compiler_params=params,
    )(exchange(operand), table, tail)
    updated, middle = pl.pallas_call(
        set_in_kernel,
        out_shape=(f32(9, *block), f32(9, *block)),
        in_specs=[vmem] * 3,
        out_specs=(vmem,) * 2,
        compiler_params=params,
        cost_estimate=pl.CostEstimate(flops=1_000_000, bytes_accessed=1_200_000, transcendentals=0),
    )(updated, middle, pass_on(tail, "gx", -1))
    scale = (groups * rows) ** -0.5
    c, s = (t * scale for t in fourier_tables(rows))
    straight = jnp.asarray(np.block([[c, s], [-s, c]]), jnp.float32)
    turned = jnp.asarray(np.block([[-s, c], [-c, -s]]), jnp.float32)
    spectrum = pl.pallas_call(
        second_transform_kernel,
        out_shape=f32(items, 2, *block),
        in_specs=[vmem] * 4,
        out_specs=vmem,
        compiler_params=params,
    )(facts, exchange(sections), straight, turned)
    return (
        updated.reshape(displacement.shape),
        middle.reshape(displacement.shape),
        spectrum.reshape(bins.shape),
    )


def solution(mesh):
    placed = (
        P(None, None, "gx", "gy"),
        P(None, None, "gx", "gy"),
        P(None, None, "gx", "gy"),
        P(None, "gx", "gy"),
        P(None, None, None, "gx", "gy"),
        P(),
        P(),
    )
    return jax.shard_map(
        on_device,
        mesh=mesh,
        in_specs=placed,
        out_specs=(
            P(None, None, "gx", "gy"),
            P(None, None, "gx", "gy"),
            P(None, None, None, "gx", "gy"),
        ),
        check_vma=False,
    )
```

```python
import jax
import jax.numpy as jnp
import ml_dtypes
import numpy as np
from jax import lax
from jax.experimental import pallas as pl
from jax.experimental.pallas import tpu as pltpu
from jax.sharding import PartitionSpec as P

time_step = 0.03
HALO = 4
EDGE = 8
BINS = 12


def edge_columns(width):
    table = np.zeros((EDGE, width), np.float32)
    for h in range(HALO):
        table[h, h] = 1.0
        table[HALO + h, width - HALO + h] = 1.0
    return table


def fourier_tables(length):
    index = np.arange(length)
    angle = 2.0 * np.pi * (index[:, None] * index[None, :] % length) / length
    return np.cos(angle), np.sin(angle)


def halves(value):
    high = value.astype(jnp.bfloat16)
    return high, (value - high.astype(jnp.float32)).astype(jnp.bfloat16)


def pick_columns(select, rows):
    chosen = select[...].astype(jnp.bfloat16)
    return lax.dot_general(
        jnp.concatenate([chosen, chosen], axis=1),
        jnp.concatenate(halves(rows), axis=1),
        (((1,), (1,)), ((), ())),
        preferred_element_type=jnp.float32,
    )


def row_tiles(whole):
    planes, rows, width = whole.shape
    return jnp.concatenate(
        [whole[:, at : at + EDGE].reshape(planes * EDGE, width) for at in range(0, rows, EDGE)], axis=0
    )


def pack_columns_kernel(disp, prev, moduli, density, masks, select, out, whole, sems):
    copies = []
    start = 0
    for n, ref in enumerate((disp, prev, moduli, density)):
        copies.append(pltpu.make_async_copy(ref, whole.at[pl.ds(start, ref.shape[0])], sems.at[n]))
        start += ref.shape[0]
    for copy in copies:
        copy.start()
    for copy in copies:
        copy.wait()
    peers, _, total = out.shape
    rows = row_tiles(whole[...])
    fill = jnp.zeros((total - rows.shape[0], rows.shape[1]), jnp.float32)
    packed = pick_columns(select, jnp.concatenate([rows, fill], axis=0))
    for slot in range(peers):
        after, before = (masks[n : n + 1, :1] > 0.5 for n in (slot, peers + slot))
        out[slot] = jnp.where(after, packed[HALO:], jnp.where(before, packed[:HALO], 0.0))


def both_sides(masks, beside):
    peers = beside.shape[0]
    east = west = beside[0]
    for slot in range(1, peers):
        east = jnp.where(masks[slot : slot + 1, :1] > 0.5, beside[slot], east)
        west = jnp.where(masks[peers + slot : peers + slot + 1, :1] > 0.5, beside[slot], west)
    return jnp.concatenate([east, west], axis=0)


def place_columns(both, select):
    chosen = select[...].astype(jnp.bfloat16)
    return lax.dot_general(
        jnp.concatenate(halves(both), axis=0),
        jnp.concatenate([chosen, chosen], axis=0),
        (((0,), (0,)), ((), ())),
        preferred_element_type=jnp.float32,
    )


def pack_rows_kernel(disp, prev, moduli, density, bins, masks, beside, out):
    start = 0
    for ref in (disp, prev, moduli, density):
        for i in range(ref.shape[0]):
            out[start + i] = ref[i, -EDGE:, :]
        start += ref.shape[0]
    for n in range(BINS):
        at = n % 2 * HALO
        out[start + n // 2, at : at + HALO, :] = bins[n, -HALO:, :]
    width = out.shape[2]
    both = both_sides(masks, beside)
    first = start * (disp.shape[1] - EDGE)
    base = first // width * width
    corner = pltpu.roll(both[:, base : base + 2 * width], 2 * width - (first - base), 1)
    out[start + BINS // 2] = corner[:, :width]
    out[start + BINS // 2 + 1] = corner[:, width:]


def shift(value, amount, axis):
    return pltpu.roll(value, (-amount) % value.shape[axis], axis)


def slopes(value, axis, even):
    ahead, ahead2 = shift(value, 1, axis), shift(value, 2, axis)
    back, back2 = shift(value, -1, axis), shift(value, -2, axis)
    right = jnp.where(even, 4.0 * ahead - 3.0 * value - ahead2, ahead - back)
    left = 3.0 * value - 4.0 * back + back2
    return right, left, jnp.where(even, right + left, right)


def spread(right, left, axis, even):
    ahead = jnp.where(even, -4.0 * left, -right)
    back = jnp.where(even, 4.0 * right, right)
    ahead = ahead + shift(jnp.where(even, left, 0.0), 1, axis)
    back = back - shift(jnp.where(even, right, 0.0), -1, axis)
    own = jnp.where(even, 3.0 * (left - right), 0.0)
    return own + shift(ahead, 1, axis) + shift(back, -1, axis)


def spread_z(layers):
    a, b, c = layers
    return c - b - 3.0 * a, 4.0 * (a - c), b - a + 3.0 * c


def two_steps(field, coef, mid, keep_middle, keep_updated):
    _, tall, wide = field.shape
    width = wide // 2

    def tiled(tile, shape=(tall, wide)):
        line = jnp.concatenate([tile] * (shape[1] // tile.shape[1]), axis=1)
        return jnp.concatenate([line] * (shape[0] // tile.shape[0]), axis=0)

    tile_x, tile_y = (lax.broadcasted_iota(jnp.int32, (8, 128), axis) % 2 for axis in range(2))
    near_x, near_y = tiled(tile_x), tiled(tile_y)
    two_x, two_y = 2.0 - near_x.astype(jnp.float32), 2.0 - near_y.astype(jnp.float32)
    weight = (1.0 / 3.0 + near_x.astype(jnp.float32)) * (1.0 / 3.0 + near_y.astype(jnp.float32)) / 8.0
    lane = lax.broadcasted_iota(jnp.int32, (tall, wide), 1)
    unused = (lane >= width + HALO) & (lane < wide - HALO)
    for layer in range(3):
        weight_z = 4.0 / 3.0 if layer == 1 else 1.0 / 3.0
        here = weight * weight_z
        lam = field[18 + layer] * here
        mu = field[21 + layer] * here
        mu_x, mu_y = mu * two_x, mu * two_y
        mu_xy = mu_x * two_y
        lam_x, lam_y = lam * two_x, lam * two_y
        mass = jnp.where(unused, 1.0, field[24 + layer]) * (here * two_x * two_y)
        for n, value in enumerate(
            (lam, lam_x, lam_y, lam_x + 2.0 * mu_x, lam_y + 2.0 * mu_y, lam_x * two_y + 2.0 * mu_xy,
             mu, mu_x, mu_y, mu_xy, time_step * time_step / mass)
        ):
            coef[layer, n] = value

    def advance(source, older, store, own):
        out_width = width if own else wide
        even_x, even_y = near_x == 0, near_y == 0
        even_xs = even_x[:, :out_width]

        def for_x(value):
            return value[:, :out_width]

        def along_x(right, left):
            return spread(right, left, 0, even_xs)

        def along_y(right, left):
            return spread(right, left, 1, even_y)[:, :out_width]

        forces = [[None] * 3 for _ in range(3)]
        z_terms = [[None] * 3 for _ in range(3)]
        for layer in range(3):
            value = [source(c * 3 + layer) for c in range(3)]
            grad_z = []
            for c in range(3):
                a, b, d = (source(c * 3 + n) for n in range(3))
                if layer == 0:
                    grad_z.append(4.0 * b - 3.0 * a - d)
                elif layer == 1:
                    grad_z.append(d - a)
                else:
                    grad_z.append(a - 4.0 * b + 3.0 * d)
            lam, lam_x, lam_y, stiff_x, stiff_y, stiff_z, mu, mu_x, mu_y, mu_xy = (
                coef[layer, n] for n in range(10)
            )
            rx, lx, sx = zip(*(slopes(v, 0, even_x) for v in value))
            ry, ly, sy = zip(*(slopes(v, 1, even_y) for v in value))
            common = for_x(lam_y * grad_z[2] + lam * sy[1])
            scale = for_x(stiff_y)
            force_x = along_x(scale * for_x(rx[0]) + common, scale * for_x(lx[0]) + common)
            common = for_x(mu * sy[0])
            scale = for_x(mu_y)
            force_y = along_x(scale * for_x(rx[1]) + common, scale * for_x(lx[1]) + common)
            common = for_x(grad_z[0])
            force_z = along_x(scale * (for_x(rx[2]) + common), scale * (for_x(lx[2]) + common))
            common = (lam_x * grad_z[2] + lam * sx[0])
            scale = (stiff_x)
            force_y += along_y(scale * (ry[1]) + common, scale * (ly[1]) + common)
            common = (mu * sx[1])
            scale = (mu_x)
            force_x += along_y(scale * (ry[0]) + common, scale * (ly[0]) + common)
            common = (grad_z[1])
            force_z += along_y(scale * ((ry[2]) + common), scale * ((ly[2]) + common))
            for c, value in enumerate((force_x, force_y, force_z)):
                forces[c][layer] = value
            z_terms[0][layer] = for_x(mu_xy * grad_z[0] + mu_y * sx[2])
            z_terms[1][layer] = for_x(mu_xy * grad_z[1] + mu_x * sy[2])
            z_terms[2][layer] = for_x(lam_y * sx[0] + lam_x * sy[1] + stiff_z * grad_z[2])
        for c in range(3):
            along_z = spread_z(z_terms[c])
            for layer in range(3):
                n = c * 3 + layer
                total = (forces[c][layer] + along_z[layer]) * for_x(coef[layer, 10])
                store(n, 2.0 * for_x(source(n)) - for_x(older(n)) - total)

    advance(lambda n: field[n], lambda n: field[9 + n], keep_middle, False)
    advance(lambda n: mid[n], lambda n: field[n], keep_updated, True)


def own_rows_kernel(masks, disp, prev, moduli, density, beside, select, updated, middle, head, field, coef, strip, mid):
    rows, width = disp.shape[1], disp.shape[2]
    strip[...] = place_columns(both_sides(masks, beside), select)
    planes = field.shape[0]
    start = 0
    for ref in (disp, prev, moduli, density):
        for i in range(ref.shape[0]):
            n = start + i
            field[n, :, :width] = ref[i]
            for tile in range(rows // EDGE):
                at = (tile * planes + n) * EDGE
                field[n, tile * EDGE : (tile + 1) * EDGE, width:] = strip[at : at + EDGE, :]
            head[n] = field[n, :EDGE, :]
        start += ref.shape[0]

    def keep_middle(n, value):
        mid[n] = value
        middle[n] = value[:, :width]

    def keep_updated(n, value):
        updated[n] = value

    two_steps(field, coef, mid, keep_middle, keep_updated)


def joint_rows_kernel(
    facts, updated, middle, head, behind, bins, select, near, tail, operand, field, coef, mid,
):
    rows, width = updated.shape[1], updated.shape[2]
    planes = field.shape[0]
    corner = jnp.concatenate([behind[planes + BINS // 2], behind[planes + BINS // 2 + 1]], axis=1)
    strip = place_columns(corner, select)
    for n in range(planes):
        field[n, :EDGE, :] = head[n]
        field[n, EDGE:, :width] = behind[n]
        field[n, EDGE:, width:] = strip[n * EDGE : (n + 1) * EDGE]
    is_near = lax.broadcasted_iota(jnp.int32, (EDGE, width), 0) < HALO
    tops = {}

    def keep(k, whole, n, value):
        near[k * 9 + n] = value[:EDGE]
        at = (k * 9 + n) * HALO
        tail[at : at + HALO, :] = value[EDGE + HALO :]
        if n % 3 == 2:
            first = jnp.where(is_near, value[:EDGE], whole[n, :EDGE, :])
            last = jnp.where(is_near, whole[n, rows - EDGE :, :], value[EDGE:])
            tops.setdefault(n // 3, []).append(
                jnp.concatenate([first, whole[n, EDGE : rows - EDGE, :], last], axis=0)
            )

    def keep_middle(n, value):
        mid[n] = value
        keep(1, middle, n, value[:, :width])

    def keep_updated(n, value):
        keep(0, updated, n, value)

    two_steps(field, coef, mid, keep_middle, keep_updated)

    angles = facts[EDGE:]
    cosines, sines = jnp.cos(angles), jnp.sin(angles)
    low = lax.broadcasted_iota(jnp.int32, (rows, width), 1) < width // 2
    half = width // 2
    for b in range(2):
        for c in range(3):
            one, two = tops[c]
            item = b * 3 + c
            old = []
            rest = behind[planes + item]
            for n, other in ((2 * item, pltpu.roll(rest, HALO, 0)), (2 * item + 1, rest)):
                last = jnp.where(is_near, bins[n, rows - EDGE :], other)
                old.append(jnp.concatenate([bins[n, : rows - EDGE], last], axis=0))
            real = old[0] + cosines[b : b + 1] * one + cosines[2 + b : 3 + b] * two
            imag = old[1] - sines[b : b + 1] * one - sines[2 + b : 3 + b] * two
            if item < 4:
                operand[pl.ds(3 * item * rows, rows, stride=3), :] = real
                operand[pl.ds(3 * item * rows + 1, rows, stride=3), :] = imag
            else:
                at = 3 * (item - 4) * rows + 2
                operand[pl.ds(at, rows, stride=3), :] = jnp.where(low, real, pltpu.roll(imag, half, 1))
                operand[pl.ds(at + 6 * rows, rows, stride=3), :] = jnp.where(
                    low, pltpu.roll(real, half, 1), imag
                )


def first_transform_kernel(received, table, tail, out, tail_out):
    tail_out[...] = tail[...]
    count, width = received.shape[0] // 3, received.shape[1]
    joined = jnp.concatenate([received[pl.ds(n, count, stride=3), :] for n in range(3)], axis=1)
    high, rest = halves(joined)
    both = jnp.dot(
        table[...], jnp.concatenate([high, rest, high], axis=0), preferred_element_type=jnp.float32
    )
    by_cos, by_sin = both[:count], both[count:]
    out[pl.ds(0, count, stride=3), :] = by_cos[:, :width] + by_sin[:, width : 2 * width]
    out[pl.ds(1, count, stride=3), :] = by_cos[:, width : 2 * width] - by_sin[:, :width]
    turned = pltpu.roll(by_sin[:, 2 * width :], width // 2, 1)
    low = lax.broadcasted_iota(jnp.int32, turned.shape, 1) < width // 2
    out[pl.ds(2, count, stride=3), :] = by_cos[:, 2 * width :] + jnp.where(low, turned, -turned)


def second_transform_kernel(facts, received, straight, turned, out):
    items, parts, rows, width = out.shape
    half = width // 2
    count = received.shape[0] // 3
    low = lax.broadcasted_iota(jnp.int32, (rows, width), 1) < half
    real, imag = [], []
    for item in range(items):
        if item < 4:
            real.append(received[pl.ds(3 * item * rows, rows, stride=3), :])
            imag.append(received[pl.ds(3 * item * rows + 1, rows, stride=3), :])
        else:
            at = 3 * (item - 4) * rows + 2
            one = received[pl.ds(at, rows, stride=3), :]
            two = received[pl.ds(at + 6 * rows, rows, stride=3), :]
            real.append(jnp.where(low, one, pltpu.roll(two, half, 1)))
            imag.append(jnp.where(low, pltpu.roll(one, half, 1), two))
    joined = jnp.concatenate([jnp.concatenate(real, axis=1), jnp.concatenate(imag, axis=1)], axis=0)
    slot = lax.broadcasted_iota(jnp.int32, straight.shape, 1) % rows
    node = jnp.where(slot < rows - HALO, slot, slot - rows).astype(jnp.float32)
    place = facts[facts.shape[0] - 1 :, : slot.shape[1]]
    angle = node * place * (2.0 * np.pi / (rows * count))
    matrix = straight[...] * jnp.cos(angle) + turned[...] * jnp.sin(angle)
    left, left_rest = halves(matrix)
    high, rest = halves(joined)
    waves = jnp.dot(
        jnp.concatenate([left, left, left_rest], axis=1),
        jnp.concatenate([high, rest, high], axis=0),
        preferred_element_type=jnp.float32,
    )
    for item in range(items):
        for part in range(parts):
            out[item, part] = waves[part * rows : (part + 1) * rows, item * width : (item + 1) * width]


def set_in_kernel(updated, middle, near, tail, updated_out, middle_out):
    for k, (ref, out) in enumerate(((updated, updated_out), (middle, middle_out))):
        for n in range(ref.shape[0]):
            at = k * ref.shape[0] + n
            out[n, HALO:-HALO, :] = ref[n, HALO:-HALO, :]
            out[n, :HALO, :] = near[at, :HALO, :]
            out[n, -HALO:, :] = tail[at * HALO : (at + 1) * HALO, :]


def exchange(value):
    peers = lax.axis_size("gx")
    rows, width = value.shape
    shaped = value.reshape(peers, 1, rows // peers * width)
    return lax.all_to_all(shaped, "gx", split_axis=0, concat_axis=0, tiled=True).reshape(rows, width)


def exchange_gy(value):
    return lax.all_to_all(value, "gy", split_axis=0, concat_axis=0, tiled=True)


def pass_on(value, axis, step):
    peers = lax.axis_size(axis)
    return lax.ppermute(value, axis, [(i, (i + step) % peers) for i in range(peers)])


def f32(*shape):
    return jax.ShapeDtypeStruct(shape, jnp.float32)


def on_device(displacement, previous, moduli, density, bins, omega, phase):
    groups = lax.axis_size("gx")
    rows, width = density.shape[1:]
    items = bins.shape[0] * bins.shape[1]
    block = (rows, width)
    arrays = [a.reshape((-1,) + block) for a in (displacement, previous, moduli, density, bins)]
    planes = sum(a.shape[0] for a in arrays) - BINS
    packed = -(-planes * rows // width) * width
    select = jnp.asarray(edge_columns(width))
    peers = lax.axis_size("gy")
    distance = jnp.arange(peers) - lax.axis_index("gy")
    masks = jnp.concatenate(
        [(distance == 1) | (distance == 1 - peers), (distance == -1) | (distance == peers - 1)]
    )
    masks = masks.astype(jnp.float32)
    steps = jnp.arange(1, 3).astype(jnp.float32)
    angles = (phase[None, :] + steps[:, None] * omega[None, :]).reshape(-1)
    facts = jnp.concatenate([masks, angles, jnp.full((4,), lax.axis_index("gx"))], dtype=jnp.float32)
    facts = jnp.broadcast_to(facts[:, None], (facts.shape[0], width))
    masks = jnp.broadcast_to(masks[:, None], (2 * peers, width))
    vmem = pl.BlockSpec(memory_space=pltpu.VMEM)
    hbm = pl.BlockSpec(memory_space=pltpu.HBM)
    params = pltpu.CompilerParams(vmem_limit_bytes=48 * 1024 * 1024)
    wide = 2 * width

    sides = pl.pallas_call(
        pack_columns_kernel,
        out_shape=pltpu.VMEM((peers, HALO, packed), jnp.float32),
        in_specs=[hbm] * 4 + [vmem] * 2,
        out_specs=vmem,
        scratch_shapes=[pltpu.VMEM((planes,) + block, jnp.float32), pltpu.SemaphoreType.DMA((4,))],
        compiler_params=pltpu.CompilerParams(vmem_limit_bytes=60 * 1024 * 1024),
    )(*arrays[:4], masks, select)
    beside = exchange_gy(sides)
    edge = pl.pallas_call(
        pack_rows_kernel,
        out_shape=f32(planes + BINS // 2 + 2, EDGE, width),
        in_specs=[vmem] * 7,
        out_specs=vmem,
        compiler_params=params,
    )(*arrays, facts, beside)
    behind = pass_on(edge, "gx", 1)
    updated, middle, head = pl.pallas_call(
        own_rows_kernel,
        out_shape=(f32(9, *block), f32(9, *block), f32(planes, EDGE, wide)),
        in_specs=[vmem] * 7,
        out_specs=(vmem,) * 3,
        scratch_shapes=[
            pltpu.VMEM((planes, rows, wide), jnp.float32),
            pltpu.VMEM((3, 11, rows, wide), jnp.float32),
            pltpu.VMEM((packed, width), jnp.float32),
            pltpu.VMEM((9, rows, wide), jnp.float32),
        ],
        compiler_params=params,
        cost_estimate=pl.CostEstimate(flops=50_000_000, bytes_accessed=2_000_000, transcendentals=0),
    )(facts, *arrays[:4], beside, select)
    near, tail, operand = pl.pallas_call(
        joint_rows_kernel,
        out_shape=(f32(18, EDGE, width), f32(18 * HALO, width), f32(3 * groups, width)),
        in_specs=[vmem] * 7,
        out_specs=(vmem,) * 3,
        scratch_shapes=[
            pltpu.VMEM((planes, 2 * EDGE, wide), jnp.float32),
            pltpu.VMEM((3, 11, 2 * EDGE, wide), jnp.float32),
            pltpu.VMEM((9, 2 * EDGE, wide), jnp.float32),
        ],
        compiler_params=params,
    )(facts, updated, middle, head, behind, arrays[4], select)

    stacked = np.concatenate(fourier_tables(groups), axis=0)
    high = stacked.astype(ml_dtypes.bfloat16)
    rest = (stacked - high.astype(np.float64)).astype(ml_dtypes.bfloat16)
    table = jnp.asarray(np.concatenate([high, high, rest], axis=1))
    sections, tail = pl.pallas_call(
        first_transform_kernel,
        out_shape=(f32(3 * groups, width), f32(*tail.shape)),
        in_specs=[vmem] * 3,
        out_specs=(vmem,) * 2,
        compiler_params=params,
    )(exchange(operand), table, tail)
    updated, middle = pl.pallas_call(
        set_in_kernel,
        out_shape=(f32(9, *block), f32(9, *block)),
        in_specs=[vmem] * 4,
        out_specs=(vmem,) * 2,
        compiler_params=params,
        cost_estimate=pl.CostEstimate(flops=1_000_000, bytes_accessed=1_200_000, transcendentals=0),
    )(updated, middle, near, pass_on(tail, "gx", -1))
    scale = (groups * rows) ** -0.5
    c, s = (t * scale for t in fourier_tables(rows))
    straight = jnp.asarray(np.block([[c, s], [-s, c]]), jnp.float32)
    turned = jnp.asarray(np.block([[-s, c], [-c, -s]]), jnp.float32)
    spectrum = pl.pallas_call(
        second_transform_kernel,
        out_shape=f32(items, 2, *block),
        in_specs=[vmem] * 4,
        out_specs=vmem,
        compiler_params=params,
    )(facts, exchange(sections), straight, turned)
    return (
        updated.reshape(displacement.shape),
        middle.reshape(displacement.shape),
        spectrum.reshape(bins.shape),
    )


def solution(mesh):
    placed = (
        P(None, None, "gx", "gy"),
        P(None, None, "gx", "gy"),
        P(None, None, "gx", "gy"),
        P(None, "gx", "gy"),
        P(None, None, None, "gx", "gy"),
        P(),
        P(),
    )
    return jax.shard_map(
        on_device,
        mesh=mesh,
        in_specs=placed,
        out_specs=(
            P(None, None, "gx", "gy"),
            P(None, None, "gx", "gy"),
            P(None, None, None, "gx", "gy"),
        ),
        check_vma=False,
    )
```

```python
import jax
import jax.numpy as jnp
import ml_dtypes
import numpy as np
from jax import lax
from jax.experimental import pallas as pl
from jax.experimental.pallas import tpu as pltpu
from jax.sharding import PartitionSpec as P

time_step = 0.03
HALO = 4
EDGE = 8
BINS = 12


def edge_columns(width):
    side = lax.broadcasted_iota(jnp.int32, (EDGE, width), 0)
    lane = lax.broadcasted_iota(jnp.int32, (EDGE, width), 1)
    return (lane == jnp.where(side < HALO, side, side + width - EDGE)).astype(jnp.float32).astype(jnp.bfloat16)


def fourier_tables(length):
    index = np.arange(length)
    angle = 2.0 * np.pi * (index[:, None] * index[None, :] % length) / length
    return np.cos(angle), np.sin(angle)


def halves(value):
    high = value.astype(jnp.bfloat16)
    return high, (value - high.astype(jnp.float32)).astype(jnp.bfloat16)


def pick_columns(rows):
    chosen = edge_columns(rows.shape[1])
    return lax.dot_general(
        jnp.concatenate([chosen, chosen], axis=1),
        jnp.concatenate(halves(rows), axis=1),
        (((1,), (1,)), ((), ())),
        preferred_element_type=jnp.float32,
    )


def row_tiles(whole):
    planes, rows, width = whole.shape
    return jnp.concatenate(
        [whole[:, at : at + EDGE].reshape(planes * EDGE, width) for at in range(0, rows, EDGE)], axis=0
    )


def pack_columns_kernel(disp, prev, moduli, density, out, whole, sems):
    copies = []
    start = 0
    for n, ref in enumerate((disp, prev, moduli, density)):
        copies.append(pltpu.make_async_copy(ref, whole.at[pl.ds(start, ref.shape[0])], sems.at[n]))
        start += ref.shape[0]
    for copy in copies:
        copy.start()
    for copy in copies:
        copy.wait()
    peers, _, total = out.shape
    rows = row_tiles(whole[...])
    fill = jnp.zeros((total - rows.shape[0], rows.shape[1]), jnp.float32)
    packed = pick_columns(jnp.concatenate([rows, fill], axis=0))
    me = lax.axis_index("gy")
    for step in range(peers):
        slot = lax.rem(me + step, peers)
        if step in (1, peers - 1):
            out[slot] = packed[HALO:] if step == 1 else packed[:HALO]
        else:
            out[slot] = jnp.zeros(out.shape[1:], jnp.float32)


def both_sides(beside):
    peers = beside.shape[0]
    me = lax.axis_index("gy")
    return jnp.concatenate([beside[lax.rem(me + 1, peers)], beside[lax.rem(me + peers - 1, peers)]], axis=0)


def place_columns(both, width):
    chosen = edge_columns(width)
    return lax.dot_general(
        jnp.concatenate(halves(both), axis=0),
        jnp.concatenate([chosen, chosen], axis=0),
        (((0,), (0,)), ((), ())),
        preferred_element_type=jnp.float32,
    )


def pack_rows_kernel(whole, bins, beside, out):
    start, rows, width = whole.shape
    for n in range(start):
        out[n] = whole[n, -EDGE:, :]
    for n in range(BINS):
        at = n % 2 * HALO
        out[start + n // 2, at : at + HALO, :] = bins[n, -HALO:, :]
    both = both_sides(beside)
    first = start * (rows - EDGE)
    base = first // width * width
    corner = pltpu.roll(both[:, base : base + 2 * width], 2 * width - (first - base), 1)
    out[start + BINS // 2] = corner[:, :width]
    out[start + BINS // 2 + 1] = corner[:, width:]


def shift(value, amount, axis):
    return pltpu.roll(value, (-amount) % value.shape[axis], axis)


def slopes(value, axis, even):
    ahead, ahead2 = shift(value, 1, axis), shift(value, 2, axis)
    back, back2 = shift(value, -1, axis), shift(value, -2, axis)
    right = jnp.where(even, 4.0 * ahead - 3.0 * value - ahead2, ahead - back)
    left = 3.0 * value - 4.0 * back + back2
    return right, left, jnp.where(even, right + left, right)


def spread(right, left, axis, even):
    ahead = jnp.where(even, -4.0 * left, -right)
    back = jnp.where(even, 4.0 * right, right)
    ahead = ahead + shift(jnp.where(even, left, 0.0), 1, axis)
    back = back - shift(jnp.where(even, right, 0.0), -1, axis)
    own = jnp.where(even, 3.0 * (left - right), 0.0)
    return own + shift(ahead, 1, axis) + shift(back, -1, axis)


def spread_z(layers):
    a, b, c = layers
    return c - b - 3.0 * a, 4.0 * (a - c), b - a + 3.0 * c


def two_steps(field, coef, mid, keep_middle, keep_updated):
    _, tall, wide = field.shape
    width = wide // 2

    def tiled(tile, shape=(tall, wide)):
        line = jnp.concatenate([tile] * (shape[1] // tile.shape[1]), axis=1)
        return jnp.concatenate([line] * (shape[0] // tile.shape[0]), axis=0)

    tile_x, tile_y = (lax.broadcasted_iota(jnp.int32, (8, 128), axis) % 2 for axis in range(2))
    near_x, near_y = tiled(tile_x), tiled(tile_y)
    two_x, two_y = 2.0 - near_x.astype(jnp.float32), 2.0 - near_y.astype(jnp.float32)
    weight = (1.0 / 3.0 + near_x.astype(jnp.float32)) * (1.0 / 3.0 + near_y.astype(jnp.float32)) / 8.0
    lane = lax.broadcasted_iota(jnp.int32, (tall, wide), 1)
    unused = (lane >= width + HALO) & (lane < wide - HALO)
    for layer in range(3):
        weight_z = 4.0 / 3.0 if layer == 1 else 1.0 / 3.0
        here = weight * weight_z
        lam = field[18 + layer] * here
        mu = field[21 + layer] * here
        mu_x, mu_y = mu * two_x, mu * two_y
        mu_xy = mu_x * two_y
        lam_x, lam_y = lam * two_x, lam * two_y
        mass = jnp.where(unused, 1.0, field[24 + layer]) * (here * two_x * two_y)
        for n, value in enumerate(
            (lam, lam_x, lam_y, lam_x + 2.0 * mu_x, lam_y + 2.0 * mu_y, lam_x * two_y + 2.0 * mu_xy,
             mu, mu_x, mu_y, mu_xy, time_step * time_step / mass)
        ):
            coef[layer, n] = value

    def advance(source, older, store, own):
        out_width = width if own else wide
        even_x, even_y = near_x == 0, near_y == 0
        even_xs = even_x[:, :out_width]

        def for_x(value):
            return value[:, :out_width]

        def along_x(right, left):
            return spread(right, left, 0, even_xs)

        def along_y(right, left):
            return spread(right, left, 1, even_y)[:, :out_width]

        forces = [[None] * 3 for _ in range(3)]
        z_terms = [[None] * 3 for _ in range(3)]
        for layer in range(3):
            value = [source(c * 3 + layer) for c in range(3)]
            grad_z = []
            for c in range(3):
                a, b, d = (source(c * 3 + n) for n in range(3))
                if layer == 0:
                    grad_z.append(4.0 * b - 3.0 * a - d)
                elif layer == 1:
                    grad_z.append(d - a)
                else:
                    grad_z.append(a - 4.0 * b + 3.0 * d)
            lam, lam_x, lam_y, stiff_x, stiff_y, stiff_z, mu, mu_x, mu_y, mu_xy = (
                coef[layer, n] for n in range(10)
            )
            rx, lx, sx = zip(*(slopes(v, 0, even_x) for v in value))
            ry, ly, sy = zip(*(slopes(v, 1, even_y) for v in value))
            common = for_x(lam_y * grad_z[2] + lam * sy[1])
            scale = for_x(stiff_y)
            force_x = along_x(scale * for_x(rx[0]) + common, scale * for_x(lx[0]) + common)
            common = for_x(mu * sy[0])
            scale = for_x(mu_y)
            force_y = along_x(scale * for_x(rx[1]) + common, scale * for_x(lx[1]) + common)
            common = for_x(grad_z[0])
            force_z = along_x(scale * (for_x(rx[2]) + common), scale * (for_x(lx[2]) + common))
            common = (lam_x * grad_z[2] + lam * sx[0])
            scale = (stiff_x)
            force_y += along_y(scale * (ry[1]) + common, scale * (ly[1]) + common)
            common = (mu * sx[1])
            scale = (mu_x)
            force_x += along_y(scale * (ry[0]) + common, scale * (ly[0]) + common)
            common = (grad_z[1])
            force_z += along_y(scale * ((ry[2]) + common), scale * ((ly[2]) + common))
            for c, value in enumerate((force_x, force_y, force_z)):
                forces[c][layer] = value
            z_terms[0][layer] = for_x(mu_xy * grad_z[0] + mu_y * sx[2])
            z_terms[1][layer] = for_x(mu_xy * grad_z[1] + mu_x * sy[2])
            z_terms[2][layer] = for_x(lam_y * sx[0] + lam_x * sy[1] + stiff_z * grad_z[2])
        for c in range(3):
            along_z = spread_z(z_terms[c])
            for layer in range(3):
                n = c * 3 + layer
                total = (forces[c][layer] + along_z[layer]) * for_x(coef[layer, 10])
                store(n, 2.0 * for_x(source(n)) - for_x(older(n)) - total)

    advance(lambda n: field[n], lambda n: field[9 + n], keep_middle, False)
    advance(lambda n: mid[n], lambda n: field[n], keep_updated, True)


def own_rows_kernel(whole, beside, updated, middle, head, field, coef, strip, mid):
    planes, rows, width = whole.shape
    strip[...] = place_columns(both_sides(beside), width)
    for n in range(planes):
        field[n, :, :width] = whole[n]
        for tile in range(rows // EDGE):
            at = (tile * planes + n) * EDGE
            field[n, tile * EDGE : (tile + 1) * EDGE, width:] = strip[at : at + EDGE, :]
        head[n] = field[n, :EDGE, :]

    def keep_middle(n, value):
        mid[n] = value
        middle[n] = value[:, :width]

    def keep_updated(n, value):
        updated[n] = value

    two_steps(field, coef, mid, keep_middle, keep_updated)


def joint_rows_kernel(
    angles, updated, middle, head, behind, bins, near, tail, operand, field, coef, mid,
):
    rows, width = updated.shape[1], updated.shape[2]
    planes = field.shape[0]
    corner = jnp.concatenate([behind[planes + BINS // 2], behind[planes + BINS // 2 + 1]], axis=1)
    strip = place_columns(corner, width)
    for n in range(planes):
        field[n, :EDGE, :] = head[n]
        field[n, EDGE:, :width] = behind[n]
        field[n, EDGE:, width:] = strip[n * EDGE : (n + 1) * EDGE]
    is_near = lax.broadcasted_iota(jnp.int32, (EDGE, width), 0) < HALO
    tops = {}

    def keep(k, whole, n, value):
        near[k * 9 + n] = value[:EDGE]
        at = (k * 9 + n) * HALO
        tail[at : at + HALO, :] = value[EDGE + HALO :]
        if n % 3 == 2:
            first = jnp.where(is_near, value[:EDGE], whole[n, :EDGE, :])
            last = jnp.where(is_near, whole[n, rows - EDGE :, :], value[EDGE:])
            tops.setdefault(n // 3, []).append(
                jnp.concatenate([first, whole[n, EDGE : rows - EDGE, :], last], axis=0)
            )

    def keep_middle(n, value):
        mid[n] = value
        keep(1, middle, n, value[:, :width])

    def keep_updated(n, value):
        keep(0, updated, n, value)

    two_steps(field, coef, mid, keep_middle, keep_updated)

    cosines, sines = jnp.cos(angles[...]), jnp.sin(angles[...])
    low = lax.broadcasted_iota(jnp.int32, (rows, width), 1) < width // 2
    half = width // 2
    for b in range(2):
        for c in range(3):
            one, two = tops[c]
            item = b * 3 + c
            old = []
            rest = behind[planes + item]
            for n, other in ((2 * item, pltpu.roll(rest, HALO, 0)), (2 * item + 1, rest)):
                last = jnp.where(is_near, bins[n, rows - EDGE :], other)
                old.append(jnp.concatenate([bins[n, : rows - EDGE], last], axis=0))
            real = old[0] + cosines[b : b + 1] * one + cosines[2 + b : 3 + b] * two
            imag = old[1] - sines[b : b + 1] * one - sines[2 + b : 3 + b] * two
            if item < 4:
                operand[pl.ds(3 * item * rows, rows, stride=3), :] = real
                operand[pl.ds(3 * item * rows + 1, rows, stride=3), :] = imag
            else:
                at = 3 * (item - 4) * rows + 2
                operand[pl.ds(at, rows, stride=3), :] = jnp.where(low, real, pltpu.roll(imag, half, 1))
                operand[pl.ds(at + 6 * rows, rows, stride=3), :] = jnp.where(
                    low, pltpu.roll(real, half, 1), imag
                )


def first_transform_kernel(received, table, tail, out, tail_out):
    tail_out[...] = tail[...]
    count, width = received.shape[0] // 3, received.shape[1]
    joined = jnp.concatenate([received[pl.ds(n, count, stride=3), :] for n in range(3)], axis=1)
    high, rest = halves(joined)
    both = jnp.dot(
        table[...], jnp.concatenate([high, rest, high], axis=0), preferred_element_type=jnp.float32
    )
    by_cos, by_sin = both[:count], both[count:]
    out[pl.ds(0, count, stride=3), :] = by_cos[:, :width] + by_sin[:, width : 2 * width]
    out[pl.ds(1, count, stride=3), :] = by_cos[:, width : 2 * width] - by_sin[:, :width]
    turned = pltpu.roll(by_sin[:, 2 * width :], width // 2, 1)
    low = lax.broadcasted_iota(jnp.int32, turned.shape, 1) < width // 2
    out[pl.ds(2, count, stride=3), :] = by_cos[:, 2 * width :] + jnp.where(low, turned, -turned)


def second_transform_kernel(received, straight, turned, out):
    items, parts, rows, width = out.shape
    half = width // 2
    count = received.shape[0] // 3
    low = lax.broadcasted_iota(jnp.int32, (rows, width), 1) < half
    real, imag = [], []
    for item in range(items):
        if item < 4:
            real.append(received[pl.ds(3 * item * rows, rows, stride=3), :])
            imag.append(received[pl.ds(3 * item * rows + 1, rows, stride=3), :])
        else:
            at = 3 * (item - 4) * rows + 2
            one = received[pl.ds(at, rows, stride=3), :]
            two = received[pl.ds(at + 6 * rows, rows, stride=3), :]
            real.append(jnp.where(low, one, pltpu.roll(two, half, 1)))
            imag.append(jnp.where(low, pltpu.roll(one, half, 1), two))
    joined = jnp.concatenate([jnp.concatenate(real, axis=1), jnp.concatenate(imag, axis=1)], axis=0)
    slot = lax.broadcasted_iota(jnp.int32, straight.shape, 1) % rows
    node = jnp.where(slot < rows - HALO, slot, slot - rows).astype(jnp.float32)
    place = lax.axis_index("gx").astype(jnp.float32)
    angle = node * place * (2.0 * np.pi / (rows * count))
    matrix = straight[...] * jnp.cos(angle) + turned[...] * jnp.sin(angle)
    left, left_rest = halves(matrix)
    high, rest = halves(joined)
    waves = jnp.dot(
        jnp.concatenate([left, left, left_rest], axis=1),
        jnp.concatenate([high, rest, high], axis=0),
        preferred_element_type=jnp.float32,
    )
    for item in range(items):
        for part in range(parts):
            out[item, part] = waves[part * rows : (part + 1) * rows, item * width : (item + 1) * width]


def set_in_kernel(updated, middle, near, tail, updated_out, middle_out):
    for k, (ref, out) in enumerate(((updated, updated_out), (middle, middle_out))):
        for n in range(ref.shape[0]):
            at = k * ref.shape[0] + n
            out[n, HALO:-HALO, :] = ref[n, HALO:-HALO, :]
            out[n, :HALO, :] = near[at, :HALO, :]
            out[n, -HALO:, :] = tail[at * HALO : (at + 1) * HALO, :]


def exchange(value):
    peers = lax.axis_size("gx")
    rows, width = value.shape
    shaped = value.reshape(peers, 1, rows // peers * width)
    return lax.all_to_all(shaped, "gx", split_axis=0, concat_axis=0, tiled=True).reshape(rows, width)


def exchange_gy(value):
    return lax.all_to_all(value, "gy", split_axis=0, concat_axis=0, tiled=True)


def pass_on(value, axis, step):
    peers = lax.axis_size(axis)
    return lax.ppermute(value, axis, [(i, (i + step) % peers) for i in range(peers)])


def f32(*shape):
    return jax.ShapeDtypeStruct(shape, jnp.float32)


def on_device(displacement, previous, moduli, density, bins, omega, phase):
    groups = lax.axis_size("gx")
    rows, width = density.shape[1:]
    items = bins.shape[0] * bins.shape[1]
    block = (rows, width)
    arrays = [a.reshape((-1,) + block) for a in (displacement, previous, moduli, density, bins)]
    planes = sum(a.shape[0] for a in arrays) - BINS
    packed = -(-planes * rows // width) * width
    peers = lax.axis_size("gy")
    vmem = pl.BlockSpec(memory_space=pltpu.VMEM)
    hbm = pl.BlockSpec(memory_space=pltpu.HBM)
    params = pltpu.CompilerParams(vmem_limit_bytes=48 * 1024 * 1024)
    wide = 2 * width

    sides, whole = pl.pallas_call(
        pack_columns_kernel,
        out_shape=(
            pltpu.VMEM((peers, HALO, packed), jnp.float32),
            pltpu.VMEM((planes,) + block, jnp.float32),
        ),
        in_specs=[hbm] * 4,
        out_specs=(vmem,) * 2,
        scratch_shapes=[pltpu.SemaphoreType.DMA((4,))],
        compiler_params=pltpu.CompilerParams(vmem_limit_bytes=60 * 1024 * 1024),
    )(*arrays[:4])
    beside = exchange_gy(sides)
    edge = pl.pallas_call(
        pack_rows_kernel,
        out_shape=f32(planes + BINS // 2 + 2, EDGE, width),
        in_specs=[vmem] * 3,
        out_specs=vmem,
        compiler_params=params,
    )(whole, arrays[4], beside)
    edge, omega, phase = lax.optimization_barrier((edge, omega, phase))
    steps = np.arange(1, 3, dtype=np.float32)
    angles = (phase[None, :] + steps[:, None] * omega[None, :]).reshape(-1)
    angles = jnp.broadcast_to(angles[:, None], (angles.shape[0], width))
    behind = pass_on(edge, "gx", 1)
    updated, middle, head = pl.pallas_call(
        own_rows_kernel,
        out_shape=(f32(9, *block), f32(9, *block), f32(planes, EDGE, wide)),
        in_specs=[vmem] * 2,
        out_specs=(vmem,) * 3,
        scratch_shapes=[
            pltpu.VMEM((planes, rows, wide), jnp.float32),
            pltpu.VMEM((3, 11, rows, wide), jnp.float32),
            pltpu.VMEM((packed, width), jnp.float32),
            pltpu.VMEM((9, rows, wide), jnp.float32),
        ],
        compiler_params=params,
        cost_estimate=pl.CostEstimate(flops=50_000_000, bytes_accessed=2_000_000, transcendentals=0),
    )(whole, beside)
    near, tail, operand = pl.pallas_call(
        joint_rows_kernel,
        out_shape=(f32(18, EDGE, width), f32(18 * HALO, width), f32(3 * groups, width)),
        in_specs=[vmem] * 6,
        out_specs=(vmem,) * 3,
        scratch_shapes=[
            pltpu.VMEM((planes, 2 * EDGE, wide), jnp.float32),
            pltpu.VMEM((3, 11, 2 * EDGE, wide), jnp.float32),
            pltpu.VMEM((9, 2 * EDGE, wide), jnp.float32),
        ],
        compiler_params=params,
    )(angles, updated, middle, head, behind, arrays[4])

    stacked = np.concatenate(fourier_tables(groups), axis=0)
    high = stacked.astype(ml_dtypes.bfloat16)
    rest = (stacked - high.astype(np.float64)).astype(ml_dtypes.bfloat16)
    table = jnp.asarray(np.concatenate([high, high, rest], axis=1))
    sections, tail = pl.pallas_call(
        first_transform_kernel,
        out_shape=(f32(3 * groups, width), f32(*tail.shape)),
        in_specs=[vmem] * 3,
        out_specs=(vmem,) * 2,
        compiler_params=params,
    )(exchange(operand), table, tail)
    updated, middle = pl.pallas_call(
        set_in_kernel,
        out_shape=(f32(9, *block), f32(9, *block)),
        in_specs=[vmem] * 4,
        out_specs=(vmem,) * 2,
        compiler_params=params,
        cost_estimate=pl.CostEstimate(flops=1_000_000, bytes_accessed=1_200_000, transcendentals=0),
    )(updated, middle, near, pass_on(tail, "gx", -1))
    scale = (groups * rows) ** -0.5
    c, s = (t * scale for t in fourier_tables(rows))
    straight = jnp.asarray(np.block([[c, s], [-s, c]]), jnp.float32)
    turned = jnp.asarray(np.block([[-s, c], [-c, -s]]), jnp.float32)
    spectrum = pl.pallas_call(
        second_transform_kernel,
        out_shape=f32(items, 2, *block),
        in_specs=[vmem] * 3,
        out_specs=vmem,
        compiler_params=params,
    )(exchange(sections), straight, turned)
    return (
        updated.reshape(displacement.shape),
        middle.reshape(displacement.shape),
        spectrum.reshape(bins.shape),
    )


def solution(mesh):
    placed = (
        P(None, None, "gx", "gy"),
        P(None, None, "gx", "gy"),
        P(None, None, "gx", "gy"),
        P(None, "gx", "gy"),
        P(None, None, None, "gx", "gy"),
        P(),
        P(),
    )
    return jax.shard_map(
        on_device,
        mesh=mesh,
        in_specs=placed,
        out_specs=(
            P(None, None, "gx", "gy"),
            P(None, None, "gx", "gy"),
            P(None, None, None, "gx", "gy"),
        ),
        check_vma=False,
    )
```

```python
import functools

import jax
import jax.numpy as jnp
import ml_dtypes
import numpy as np
from jax import lax
from jax.experimental import pallas as pl
from jax.experimental.pallas import tpu as pltpu
from jax.sharding import PartitionSpec as P

time_step = 0.03
HALO = 4
EDGE = 8
BINS = 12


def edge_columns(width):
    side = lax.broadcasted_iota(jnp.int32, (EDGE, width), 0)
    lane = lax.broadcasted_iota(jnp.int32, (EDGE, width), 1)
    return (lane == jnp.where(side < HALO, side, side + width - EDGE)).astype(jnp.float32).astype(jnp.bfloat16)


def fourier_tables(length):
    index = np.arange(length)
    angle = 2.0 * np.pi * (index[:, None] * index[None, :] % length) / length
    return np.cos(angle), np.sin(angle)


def halves(value):
    high = value.astype(jnp.bfloat16)
    return high, (value - high.astype(jnp.float32)).astype(jnp.bfloat16)


def pick_columns(rows):
    width = rows.shape[1]
    turned = [rows[at : at + width].T for at in range(0, rows.shape[0], width)]
    return jnp.concatenate([jnp.concatenate([t[:HALO], t[-HALO:]], axis=0) for t in turned], axis=1)


def row_tiles(whole):
    planes, rows, width = whole.shape
    return jnp.concatenate(
        [whole[:, at : at + EDGE].reshape(planes * EDGE, width) for at in range(0, rows, EDGE)], axis=0
    )


def pack_columns_kernel(disp, prev, moduli, density, out, whole, sems):
    copies = []
    start = 0
    for n, ref in enumerate((disp, prev, moduli, density)):
        copies.append(pltpu.make_async_copy(ref, whole.at[pl.ds(start, ref.shape[0])], sems.at[n]))
        start += ref.shape[0]
    for copy in copies:
        copy.start()
    for copy in copies:
        copy.wait()
    peers, _, total = out.shape
    rows = row_tiles(whole[...])
    fill = jnp.zeros((total - rows.shape[0], rows.shape[1]), jnp.float32)
    packed = pick_columns(jnp.concatenate([rows, fill], axis=0))
    me = lax.axis_index("gy")
    for step in range(peers):
        slot = lax.rem(me + step, peers)
        if step in (1, peers - 1):
            out[slot] = packed[HALO:] if step == 1 else packed[:HALO]
        else:
            out[slot] = jnp.zeros(out.shape[1:], jnp.float32)


def both_sides(beside):
    peers = beside.shape[0]
    me = lax.axis_index("gy")
    return jnp.concatenate([beside[lax.rem(me + 1, peers)], beside[lax.rem(me + peers - 1, peers)]], axis=0)


def place_columns(both, width):
    chosen = edge_columns(width)
    return lax.dot_general(
        jnp.concatenate(halves(both), axis=0),
        jnp.concatenate([chosen, chosen], axis=0),
        (((0,), (0,)), ((), ())),
        preferred_element_type=jnp.float32,
    )


def pack_rows_kernel(whole, bins, beside, out):
    start, rows, width = whole.shape
    for n in range(start):
        out[n] = whole[n, -EDGE:, :]
    for n in range(BINS):
        at = n % 2 * HALO
        out[start + n // 2, at : at + HALO, :] = bins[n, -HALO:, :]
    both = both_sides(beside)
    first = start * (rows - EDGE)
    base = first // width * width
    corner = pltpu.roll(both[:, base : base + 2 * width], 2 * width - (first - base), 1)
    out[start + BINS // 2] = corner[:, :width]
    out[start + BINS // 2 + 1] = corner[:, width:]


def shift(value, amount, axis):
    return pltpu.roll(value, (-amount) % value.shape[axis], axis)


def slopes(value, axis, even):
    ahead, ahead2 = shift(value, 1, axis), shift(value, 2, axis)
    back, back2 = shift(value, -1, axis), shift(value, -2, axis)
    right = jnp.where(even, 4.0 * ahead - 3.0 * value - ahead2, ahead - back)
    left = 3.0 * value - 4.0 * back + back2
    return right, left, jnp.where(even, right + left, right)


def spread(right, left, axis, even):
    ahead = jnp.where(even, -4.0 * left, -right)
    back = jnp.where(even, 4.0 * right, right)
    ahead = ahead + shift(jnp.where(even, left, 0.0), 1, axis)
    back = back - shift(jnp.where(even, right, 0.0), -1, axis)
    own = jnp.where(even, 3.0 * (left - right), 0.0)
    return own + shift(ahead, 1, axis) + shift(back, -1, axis)


def spread_z(layers):
    a, b, c = layers
    return c - b - 3.0 * a, 4.0 * (a - c), b - a + 3.0 * c


def two_steps(field, coef, mid, keep_middle, keep_updated):
    _, tall, wide = field.shape
    width = wide // 2

    def tiled(tile, shape=(tall, wide)):
        line = jnp.concatenate([tile] * (shape[1] // tile.shape[1]), axis=1)
        return jnp.concatenate([line] * (shape[0] // tile.shape[0]), axis=0)

    tile_x, tile_y = (lax.broadcasted_iota(jnp.int32, (8, 128), axis) % 2 for axis in range(2))
    near_x, near_y = tiled(tile_x), tiled(tile_y)
    two_x, two_y = 2.0 - near_x.astype(jnp.float32), 2.0 - near_y.astype(jnp.float32)
    weight = (1.0 / 3.0 + near_x.astype(jnp.float32)) * (1.0 / 3.0 + near_y.astype(jnp.float32)) / 8.0
    lane = lax.broadcasted_iota(jnp.int32, (tall, wide), 1)
    unused = (lane >= width + HALO) & (lane < wide - HALO)
    for layer in range(3):
        weight_z = 4.0 / 3.0 if layer == 1 else 1.0 / 3.0
        here = weight * weight_z
        lam = field[18 + layer] * here
        mu = field[21 + layer] * here
        mu_x, mu_y = mu * two_x, mu * two_y
        mu_xy = mu_x * two_y
        lam_x, lam_y = lam * two_x, lam * two_y
        mass = jnp.where(unused, 1.0, field[24 + layer]) * (here * two_x * two_y)
        for n, value in enumerate(
            (lam, lam_x, lam_y, lam_x + 2.0 * mu_x, lam_y + 2.0 * mu_y, lam_x * two_y + 2.0 * mu_xy,
             mu, mu_x, mu_y, mu_xy, time_step * time_step / mass)
        ):
            coef[layer, n] = value

    def advance(source, older, store, own):
        out_width = width if own else wide
        even_x, even_y = near_x == 0, near_y == 0
        even_xs = even_x[:, :out_width]

        def for_x(value):
            return value[:, :out_width]

        def along_x(right, left):
            return spread(right, left, 0, even_xs)

        def along_y(right, left):
            return spread(right, left, 1, even_y)[:, :out_width]

        forces = [[None] * 3 for _ in range(3)]
        z_terms = [[None] * 3 for _ in range(3)]
        for layer in range(3):
            value = [source(c * 3 + layer) for c in range(3)]
            grad_z = []
            for c in range(3):
                a, b, d = (source(c * 3 + n) for n in range(3))
                if layer == 0:
                    grad_z.append(4.0 * b - 3.0 * a - d)
                elif layer == 1:
                    grad_z.append(d - a)
                else:
                    grad_z.append(a - 4.0 * b + 3.0 * d)
            lam, lam_x, lam_y, stiff_x, stiff_y, stiff_z, mu, mu_x, mu_y, mu_xy = (
                coef[layer, n] for n in range(10)
            )
            rx, lx, sx = zip(*(slopes(v, 0, even_x) for v in value))
            ry, ly, sy = zip(*(slopes(v, 1, even_y) for v in value))
            common = for_x(lam_y * grad_z[2] + lam * sy[1])
            scale = for_x(stiff_y)
            force_x = along_x(scale * for_x(rx[0]) + common, scale * for_x(lx[0]) + common)
            common = for_x(mu * sy[0])
            scale = for_x(mu_y)
            force_y = along_x(scale * for_x(rx[1]) + common, scale * for_x(lx[1]) + common)
            common = for_x(grad_z[0])
            force_z = along_x(scale * (for_x(rx[2]) + common), scale * (for_x(lx[2]) + common))
            common = (lam_x * grad_z[2] + lam * sx[0])
            scale = (stiff_x)
            force_y += along_y(scale * (ry[1]) + common, scale * (ly[1]) + common)
            common = (mu * sx[1])
            scale = (mu_x)
            force_x += along_y(scale * (ry[0]) + common, scale * (ly[0]) + common)
            common = (grad_z[1])
            force_z += along_y(scale * ((ry[2]) + common), scale * ((ly[2]) + common))
            for c, value in enumerate((force_x, force_y, force_z)):
                forces[c][layer] = value
            z_terms[0][layer] = for_x(mu_xy * grad_z[0] + mu_y * sx[2])
            z_terms[1][layer] = for_x(mu_xy * grad_z[1] + mu_x * sy[2])
            z_terms[2][layer] = for_x(lam_y * sx[0] + lam_x * sy[1] + stiff_z * grad_z[2])
        for c in range(3):
            along_z = spread_z(z_terms[c])
            for layer in range(3):
                n = c * 3 + layer
                total = (forces[c][layer] + along_z[layer]) * for_x(coef[layer, 10])
                store(n, 2.0 * for_x(source(n)) - for_x(older(n)) - total)

    advance(lambda n: field[n], lambda n: field[9 + n], keep_middle, False)
    advance(lambda n: mid[n], lambda n: field[n], keep_updated, True)


def own_rows_kernel(angles, whole, beside, updated, middle, head, waves, field, coef, strip, mid):
    planes, rows, width = whole.shape
    waves[: angles.shape[0], :] = jnp.cos(angles[...])
    waves[angles.shape[0] :, :] = jnp.sin(angles[...])
    strip[...] = place_columns(both_sides(beside), width)
    for n in range(planes):
        field[n, :, :width] = whole[n]
        for tile in range(rows // EDGE):
            at = (tile * planes + n) * EDGE
            field[n, tile * EDGE : (tile + 1) * EDGE, width:] = strip[at : at + EDGE, :]
        head[n] = field[n, :EDGE, :]

    def keep_middle(n, value):
        mid[n] = value
        middle[n] = value[:, :width]

    def keep_updated(n, value):
        updated[n] = value

    two_steps(field, coef, mid, keep_middle, keep_updated)


def joint_rows_kernel(
    waves, updated, middle, head, behind, bins, near, tail, operand, field, coef, mid,
):
    rows, width = updated.shape[1], updated.shape[2]
    planes = field.shape[0]
    corner = jnp.concatenate([behind[planes + BINS // 2], behind[planes + BINS // 2 + 1]], axis=1)
    strip = place_columns(corner, width)
    for n in range(planes):
        field[n, :EDGE, :] = head[n]
        field[n, EDGE:, :width] = behind[n]
        field[n, EDGE:, width:] = strip[n * EDGE : (n + 1) * EDGE]
    is_near = lax.broadcasted_iota(jnp.int32, (EDGE, width), 0) < HALO
    tops = {}

    def keep(k, whole, n, value):
        near[k * 9 + n] = value[:EDGE]
        at = (k * 9 + n) * HALO
        tail[at : at + HALO, :] = value[EDGE + HALO :]
        if n % 3 == 2:
            first = jnp.where(is_near, value[:EDGE], whole[n, :EDGE, :])
            last = jnp.where(is_near, whole[n, rows - EDGE :, :], value[EDGE:])
            tops.setdefault(n // 3, []).append(
                jnp.concatenate([first, whole[n, EDGE : rows - EDGE, :], last], axis=0)
            )

    def keep_middle(n, value):
        mid[n] = value
        keep(1, middle, n, value[:, :width])

    def keep_updated(n, value):
        keep(0, updated, n, value)

    two_steps(field, coef, mid, keep_middle, keep_updated)

    cosines, sines = waves[:HALO], waves[HALO:]
    low = lax.broadcasted_iota(jnp.int32, (rows, width), 1) < width // 2
    half = width // 2
    for b in range(2):
        for c in range(3):
            one, two = tops[c]
            item = b * 3 + c
            old = []
            rest = behind[planes + item]
            for n, other in ((2 * item, pltpu.roll(rest, HALO, 0)), (2 * item + 1, rest)):
                last = jnp.where(is_near, bins[n, rows - EDGE :], other)
                old.append(jnp.concatenate([bins[n, : rows - EDGE], last], axis=0))
            real = old[0] + cosines[b : b + 1] * one + cosines[2 + b : 3 + b] * two
            imag = old[1] - sines[b : b + 1] * one - sines[2 + b : 3 + b] * two
            if item < 4:
                operand[pl.ds(3 * item * rows, rows, stride=3), :] = real
                operand[pl.ds(3 * item * rows + 1, rows, stride=3), :] = imag
            else:
                at = 3 * (item - 4) * rows + 2
                operand[pl.ds(at, rows, stride=3), :] = jnp.where(low, real, pltpu.roll(imag, half, 1))
                operand[pl.ds(at + 6 * rows, rows, stride=3), :] = jnp.where(
                    low, pltpu.roll(real, half, 1), imag
                )


def first_transform_kernel(received, table, tail, out, tail_out):
    tail_out[...] = tail[...]
    count, width = received.shape[0] // 3, received.shape[1]
    joined = jnp.concatenate([received[pl.ds(n, count, stride=3), :] for n in range(3)], axis=1)
    high, rest = halves(joined)
    both = jnp.dot(
        table[...], jnp.concatenate([high, rest, high], axis=0), preferred_element_type=jnp.float32
    )
    by_cos, by_sin = both[:count], both[count:]
    out[pl.ds(0, count, stride=3), :] = by_cos[:, :width] + by_sin[:, width : 2 * width]
    out[pl.ds(1, count, stride=3), :] = by_cos[:, width : 2 * width] - by_sin[:, :width]
    turned = pltpu.roll(by_sin[:, 2 * width :], width // 2, 1)
    low = lax.broadcasted_iota(jnp.int32, turned.shape, 1) < width // 2
    out[pl.ds(2, count, stride=3), :] = by_cos[:, 2 * width :] + jnp.where(low, turned, -turned)


def second_transform_kernel(received, matrix, out):
    items, parts, rows, width = out.shape
    half = width // 2
    count = received.shape[0] // 3
    low = lax.broadcasted_iota(jnp.int32, (rows, width), 1) < half
    real, imag = [], []
    for item in range(items):
        if item < 4:
            real.append(received[pl.ds(3 * item * rows, rows, stride=3), :])
            imag.append(received[pl.ds(3 * item * rows + 1, rows, stride=3), :])
        else:
            at = 3 * (item - 4) * rows + 2
            one = received[pl.ds(at, rows, stride=3), :]
            two = received[pl.ds(at + 6 * rows, rows, stride=3), :]
            real.append(jnp.where(low, one, pltpu.roll(two, half, 1)))
            imag.append(jnp.where(low, pltpu.roll(one, half, 1), two))
    joined = jnp.concatenate([jnp.concatenate(real, axis=1), jnp.concatenate(imag, axis=1)], axis=0)
    left, left_rest = halves(matrix[...])
    high, rest = halves(joined)
    waves = jnp.dot(
        jnp.concatenate([left, left, left_rest], axis=1),
        jnp.concatenate([high, rest, high], axis=0),
        preferred_element_type=jnp.float32,
    )
    for item in range(items):
        for part in range(parts):
            out[item, part] = waves[part * rows : (part + 1) * rows, item * width : (item + 1) * width]


def set_in_kernel(rows, count, updated, middle, near, tail, straight, turned, updated_out, middle_out, matrix):
    slot = lax.broadcasted_iota(jnp.int32, straight.shape, 1) % rows
    node = jnp.where(slot < rows - HALO, slot, slot - rows).astype(jnp.float32)
    place = lax.axis_index("gx").astype(jnp.float32)
    angle = node * place * (2.0 * np.pi / (rows * count))
    matrix[...] = straight[...] * jnp.cos(angle) + turned[...] * jnp.sin(angle)
    for k, (ref, out) in enumerate(((updated, updated_out), (middle, middle_out))):
        for n in range(ref.shape[0]):
            at = k * ref.shape[0] + n
            out[n, HALO:-HALO, :] = ref[n, HALO:-HALO, :]
            out[n, :HALO, :] = near[at, :HALO, :]
            out[n, -HALO:, :] = tail[at * HALO : (at + 1) * HALO, :]


def exchange(value):
    peers = lax.axis_size("gx")
    rows, width = value.shape
    shaped = value.reshape(peers, 1, rows // peers * width)
    return lax.all_to_all(shaped, "gx", split_axis=0, concat_axis=0, tiled=True).reshape(rows, width)


def exchange_gy(value):
    return lax.all_to_all(value, "gy", split_axis=0, concat_axis=0, tiled=True)


def pass_on(value, axis, step):
    peers = lax.axis_size(axis)
    return lax.ppermute(value, axis, [(i, (i + step) % peers) for i in range(peers)])


def f32(*shape):
    return jax.ShapeDtypeStruct(shape, jnp.float32)


def on_device(displacement, previous, moduli, density, bins, omega, phase):
    groups = lax.axis_size("gx")
    rows, width = density.shape[1:]
    items = bins.shape[0] * bins.shape[1]
    block = (rows, width)
    arrays = [a.reshape((-1,) + block) for a in (displacement, previous, moduli, density, bins)]
    planes = sum(a.shape[0] for a in arrays) - BINS
    packed = -(-planes * rows // width) * width
    peers = lax.axis_size("gy")
    vmem = pl.BlockSpec(memory_space=pltpu.VMEM)
    hbm = pl.BlockSpec(memory_space=pltpu.HBM)
    params = pltpu.CompilerParams(vmem_limit_bytes=48 * 1024 * 1024)
    wide = 2 * width

    sides, whole = pl.pallas_call(
        pack_columns_kernel,
        out_shape=(
            pltpu.VMEM((peers, HALO, packed), jnp.float32),
            pltpu.VMEM((planes,) + block, jnp.float32),
        ),
        in_specs=[hbm] * 4,
        out_specs=(vmem,) * 2,
        scratch_shapes=[pltpu.SemaphoreType.DMA((4,))],
        compiler_params=pltpu.CompilerParams(vmem_limit_bytes=60 * 1024 * 1024),
    )(*arrays[:4])
    beside = exchange_gy(sides)
    edge = pl.pallas_call(
        pack_rows_kernel,
        out_shape=f32(planes + BINS // 2 + 2, EDGE, width),
        in_specs=[vmem] * 3,
        out_specs=vmem,
        compiler_params=params,
    )(whole, arrays[4], beside)
    edge, omega, phase = lax.optimization_barrier((edge, omega, phase))
    steps = np.arange(1, 3, dtype=np.float32)
    angles = (phase[None, :] + steps[:, None] * omega[None, :]).reshape(-1)
    angles = jnp.broadcast_to(angles[:, None], (angles.shape[0], width))
    behind = pass_on(edge, "gx", 1)
    updated, middle, head, waves = pl.pallas_call(
        own_rows_kernel,
        out_shape=(f32(9, *block), f32(9, *block), f32(planes, EDGE, wide), f32(EDGE, width)),
        in_specs=[vmem] * 3,
        out_specs=(vmem,) * 4,
        scratch_shapes=[
            pltpu.VMEM((planes, rows, wide), jnp.float32),
            pltpu.VMEM((3, 11, rows, wide), jnp.float32),
            pltpu.VMEM((packed, width), jnp.float32),
            pltpu.VMEM((9, rows, wide), jnp.float32),
        ],
        compiler_params=params,
        cost_estimate=pl.CostEstimate(flops=50_000_000, bytes_accessed=2_000_000, transcendentals=0),
    )(angles, whole, beside)
    near, tail, operand = pl.pallas_call(
        joint_rows_kernel,
        out_shape=(f32(18, EDGE, width), f32(18 * HALO, width), f32(3 * groups, width)),
        in_specs=[vmem] * 6,
        out_specs=(vmem,) * 3,
        scratch_shapes=[
            pltpu.VMEM((planes, 2 * EDGE, wide), jnp.float32),
            pltpu.VMEM((3, 11, 2 * EDGE, wide), jnp.float32),
            pltpu.VMEM((9, 2 * EDGE, wide), jnp.float32),
        ],
        compiler_params=params,
    )(waves, updated, middle, head, behind, arrays[4])

    stacked = np.concatenate(fourier_tables(groups), axis=0)
    high = stacked.astype(ml_dtypes.bfloat16)
    rest = (stacked - high.astype(np.float64)).astype(ml_dtypes.bfloat16)
    table = jnp.asarray(np.concatenate([high, high, rest], axis=1))
    sections, tail = pl.pallas_call(
        first_transform_kernel,
        out_shape=(f32(3 * groups, width), f32(*tail.shape)),
        in_specs=[vmem] * 3,
        out_specs=(vmem,) * 2,
        compiler_params=params,
    )(exchange(operand), table, tail)
    scale = (groups * rows) ** -0.5
    c, s = (t * scale for t in fourier_tables(rows))
    straight = jnp.asarray(np.block([[c, s], [-s, c]]), jnp.float32)
    turned = jnp.asarray(np.block([[-s, c], [-c, -s]]), jnp.float32)
    updated, middle, matrix = pl.pallas_call(
        functools.partial(set_in_kernel, rows, groups),
        out_shape=(f32(9, *block), f32(9, *block), f32(2 * rows, 2 * rows)),
        in_specs=[vmem] * 6,
        out_specs=(vmem,) * 3,
        compiler_params=params,
        cost_estimate=pl.CostEstimate(flops=1_000_000, bytes_accessed=1_200_000, transcendentals=0),
    )(updated, middle, near, pass_on(tail, "gx", -1), straight, turned)
    spectrum = pl.pallas_call(
        second_transform_kernel,
        out_shape=f32(items, 2, *block),
        in_specs=[vmem] * 2,
        out_specs=vmem,
        compiler_params=params,
    )(exchange(sections), matrix)
    return (
        updated.reshape(displacement.shape),
        middle.reshape(displacement.shape),
        spectrum.reshape(bins.shape),
    )


def solution(mesh):
    placed = (
        P(None, None, "gx", "gy"),
        P(None, None, "gx", "gy"),
        P(None, None, "gx", "gy"),
        P(None, "gx", "gy"),
        P(None, None, None, "gx", "gy"),
        P(),
        P(),
    )
    return jax.shard_map(
        on_device,
        mesh=mesh,
        in_specs=placed,
        out_specs=(
            P(None, None, "gx", "gy"),
            P(None, None, "gx", "gy"),
            P(None, None, None, "gx", "gy"),
        ),
        check_vma=False,
    )
```

```python
import functools

import jax
import jax.numpy as jnp
import ml_dtypes
import numpy as np
from jax import lax
from jax.experimental import pallas as pl
from jax.experimental.pallas import tpu as pltpu
from jax.sharding import PartitionSpec as P

time_step = 0.03
HALO = 4
EDGE = 8
BINS = 12


def edge_columns(width):
    side = lax.broadcasted_iota(jnp.int32, (EDGE, width), 0)
    lane = lax.broadcasted_iota(jnp.int32, (EDGE, width), 1)
    return (lane == jnp.where(side < HALO, side, side + width - EDGE)).astype(jnp.float32).astype(jnp.bfloat16)


def fourier_tables(length):
    index = np.arange(length)
    angle = 2.0 * np.pi * (index[:, None] * index[None, :] % length) / length
    return np.cos(angle), np.sin(angle)


def halves(value):
    high = value.astype(jnp.bfloat16)
    return high, (value - high.astype(jnp.float32)).astype(jnp.bfloat16)


def pick_columns(rows):
    width = rows.shape[1]
    turned = [rows[at : at + width].T for at in range(0, rows.shape[0], width)]
    return jnp.concatenate([jnp.concatenate([t[:HALO], t[-HALO:]], axis=0) for t in turned], axis=1)


def row_tiles(whole):
    planes, rows, width = whole.shape
    return jnp.concatenate(
        [whole[:, at : at + EDGE].reshape(planes * EDGE, width) for at in range(0, rows, EDGE)], axis=0
    )


def pack_columns_kernel(disp, prev, moduli, density, out, whole, sems):
    copies = []
    start = 0
    for ref in (disp, prev, moduli, density):
        for i in range(ref.shape[0]):
            copies.append(pltpu.make_async_copy(ref.at[i], whole.at[start], sems.at[start]))
            start += 1
    for copy in copies:
        copy.start()
    for copy in copies:
        copy.wait()
    peers, _, total = out.shape
    rows = row_tiles(whole[...])
    fill = jnp.zeros((total - rows.shape[0], rows.shape[1]), jnp.float32)
    packed = pick_columns(jnp.concatenate([rows, fill], axis=0))
    me = lax.axis_index("gy")
    for step in range(peers):
        slot = lax.rem(me + step, peers)
        if step in (1, peers - 1):
            out[slot] = packed[HALO:] if step == 1 else packed[:HALO]
        else:
            out[slot] = jnp.zeros(out.shape[1:], jnp.float32)


def both_sides(beside):
    peers = beside.shape[0]
    me = lax.axis_index("gy")
    return jnp.concatenate([beside[lax.rem(me + 1, peers)], beside[lax.rem(me + peers - 1, peers)]], axis=0)


def place_columns(both, width):
    chosen = edge_columns(width)
    return lax.dot_general(
        jnp.concatenate(halves(both), axis=0),
        jnp.concatenate([chosen, chosen], axis=0),
        (((0,), (0,)), ((), ())),
        preferred_element_type=jnp.float32,
    )


def pack_rows_kernel(whole, bins, beside, out):
    start, rows, width = whole.shape
    for n in range(start):
        out[n] = whole[n, -EDGE:, :]
    for n in range(BINS):
        at = n % 2 * HALO
        out[start + n // 2, at : at + HALO, :] = bins[n, -HALO:, :]
    both = both_sides(beside)
    first = start * (rows - EDGE)
    base = first // width * width
    corner = pltpu.roll(both[:, base : base + 2 * width], 2 * width - (first - base), 1)
    out[start + BINS // 2] = corner[:, :width]
    out[start + BINS // 2 + 1] = corner[:, width:]


def shift(value, amount, axis):
    return pltpu.roll(value, (-amount) % value.shape[axis], axis)


def slopes(value, axis, even):
    ahead, ahead2 = shift(value, 1, axis), shift(value, 2, axis)
    back, back2 = shift(value, -1, axis), shift(value, -2, axis)
    right = jnp.where(even, 4.0 * ahead - 3.0 * value - ahead2, ahead - back)
    left = 3.0 * value - 4.0 * back + back2
    return right, left, jnp.where(even, right + left, right)


def spread(right, left, axis, even):
    ahead = jnp.where(even, -4.0 * left, -right)
    back = jnp.where(even, 4.0 * right, right)
    ahead = ahead + shift(jnp.where(even, left, 0.0), 1, axis)
    back = back - shift(jnp.where(even, right, 0.0), -1, axis)
    own = jnp.where(even, 3.0 * (left - right), 0.0)
    return own + shift(ahead, 1, axis) + shift(back, -1, axis)


def spread_z(layers):
    a, b, c = layers
    return c - b - 3.0 * a, 4.0 * (a - c), b - a + 3.0 * c


def two_steps(field, coef, mid, keep_middle, keep_updated):
    _, tall, wide = field.shape
    width = wide // 2

    def tiled(tile, shape=(tall, wide)):
        line = jnp.concatenate([tile] * (shape[1] // tile.shape[1]), axis=1)
        return jnp.concatenate([line] * (shape[0] // tile.shape[0]), axis=0)

    tile_x, tile_y = (lax.broadcasted_iota(jnp.int32, (8, 128), axis) % 2 for axis in range(2))
    near_x, near_y = tiled(tile_x), tiled(tile_y)
    two_x, two_y = 2.0 - near_x.astype(jnp.float32), 2.0 - near_y.astype(jnp.float32)
    weight = (1.0 / 3.0 + near_x.astype(jnp.float32)) * (1.0 / 3.0 + near_y.astype(jnp.float32)) / 8.0
    lane = lax.broadcasted_iota(jnp.int32, (tall, wide), 1)
    unused = (lane >= width + HALO) & (lane < wide - HALO)
    for layer in range(3):
        weight_z = 4.0 / 3.0 if layer == 1 else 1.0 / 3.0
        here = weight * weight_z
        lam = field[18 + layer] * here
        mu = field[21 + layer] * here
        mu_x, mu_y = mu * two_x, mu * two_y
        mu_xy = mu_x * two_y
        lam_x, lam_y = lam * two_x, lam * two_y
        mass = jnp.where(unused, 1.0, field[24 + layer]) * (here * two_x * two_y)
        for n, value in enumerate(
            (lam, lam_x, lam_y, lam_x + 2.0 * mu_x, lam_y + 2.0 * mu_y, lam_x * two_y + 2.0 * mu_xy,
             mu, mu_x, mu_y, mu_xy, time_step * time_step / mass)
        ):
            coef[layer, n] = value

    def advance(source, older, store, own):
        out_width = width if own else wide
        even_x, even_y = near_x == 0, near_y == 0
        even_xs = even_x[:, :out_width]

        def for_x(value):
            return value[:, :out_width]

        def along_x(right, left):
            return spread(right, left, 0, even_xs)

        def along_y(right, left):
            return spread(right, left, 1, even_y)[:, :out_width]

        forces = [[None] * 3 for _ in range(3)]
        z_terms = [[None] * 3 for _ in range(3)]
        for layer in range(3):
            value = [source(c * 3 + layer) for c in range(3)]
            grad_z = []
            for c in range(3):
                a, b, d = (source(c * 3 + n) for n in range(3))
                if layer == 0:
                    grad_z.append(4.0 * b - 3.0 * a - d)
                elif layer == 1:
                    grad_z.append(d - a)
                else:
                    grad_z.append(a - 4.0 * b + 3.0 * d)
            lam, lam_x, lam_y, stiff_x, stiff_y, stiff_z, mu, mu_x, mu_y, mu_xy = (
                coef[layer, n] for n in range(10)
            )
            rx, lx, sx = zip(*(slopes(v, 0, even_x) for v in value))
            ry, ly, sy = zip(*(slopes(v, 1, even_y) for v in value))
            common = for_x(lam_y * grad_z[2] + lam * sy[1])
            scale = for_x(stiff_y)
            force_x = along_x(scale * for_x(rx[0]) + common, scale * for_x(lx[0]) + common)
            common = for_x(mu * sy[0])
            scale = for_x(mu_y)
            force_y = along_x(scale * for_x(rx[1]) + common, scale * for_x(lx[1]) + common)
            common = for_x(grad_z[0])
            force_z = along_x(scale * (for_x(rx[2]) + common), scale * (for_x(lx[2]) + common))
            common = (lam_x * grad_z[2] + lam * sx[0])
            scale = (stiff_x)
            force_y += along_y(scale * (ry[1]) + common, scale * (ly[1]) + common)
            common = (mu * sx[1])
            scale = (mu_x)
            force_x += along_y(scale * (ry[0]) + common, scale * (ly[0]) + common)
            common = (grad_z[1])
            force_z += along_y(scale * ((ry[2]) + common), scale * ((ly[2]) + common))
            for c, value in enumerate((force_x, force_y, force_z)):
                forces[c][layer] = value
            z_terms[0][layer] = for_x(mu_xy * grad_z[0] + mu_y * sx[2])
            z_terms[1][layer] = for_x(mu_xy * grad_z[1] + mu_x * sy[2])
            z_terms[2][layer] = for_x(lam_y * sx[0] + lam_x * sy[1] + stiff_z * grad_z[2])
        for c in range(3):
            along_z = spread_z(z_terms[c])
            for layer in range(3):
                n = c * 3 + layer
                total = (forces[c][layer] + along_z[layer]) * for_x(coef[layer, 10])
                store(n, 2.0 * for_x(source(n)) - for_x(older(n)) - total)

    advance(lambda n: field[n], lambda n: field[9 + n], keep_middle, False)
    advance(lambda n: mid[n], lambda n: field[n], keep_updated, True)


def add_bins(operand, waves, item, old, tops, first, rows):
    b = item // 3
    one, two = tops
    count, width = one.shape
    half = width // 2
    real = old[0] + waves[b : b + 1] * one + waves[2 + b : 3 + b] * two
    imag = old[1] - waves[4 + b : 5 + b] * one - waves[6 + b : 7 + b] * two
    if item < 4:
        at = 3 * (item * rows + first)
        operand[pl.ds(at, count, stride=3), :] = real
        operand[pl.ds(at + 1, count, stride=3), :] = imag
    else:
        low = lax.broadcasted_iota(jnp.int32, (count, width), 1) < half
        at = 3 * ((item - 4) * rows + first) + 2
        operand[pl.ds(at, count, stride=3), :] = jnp.where(low, real, pltpu.roll(imag, half, 1))
        operand[pl.ds(at + 6 * rows, count, stride=3), :] = jnp.where(low, pltpu.roll(real, half, 1), imag)


def own_rows_kernel(
    angles, whole, bins, beside, updated, middle, head, waves, operand, field, coef, strip, mid,
):
    planes, rows, width = whole.shape
    waves[: angles.shape[0], :] = jnp.cos(angles[...])
    waves[angles.shape[0] :, :] = jnp.sin(angles[...])
    strip[...] = place_columns(both_sides(beside), width)
    for n in range(planes):
        field[n, :, :width] = whole[n]
        for tile in range(rows // EDGE):
            at = (tile * planes + n) * EDGE
            field[n, tile * EDGE : (tile + 1) * EDGE, width:] = strip[at : at + EDGE, :]
        head[n] = field[n, :EDGE, :]

    def keep_middle(n, value):
        mid[n] = value
        middle[n] = value[:, :width]

    def keep_updated(n, value):
        updated[n] = value

    two_steps(field, coef, mid, keep_middle, keep_updated)
    inner = slice(EDGE, rows - EDGE)
    for item in range(BINS // 2):
        top = item % 3 * 3 + 2
        old = (bins[2 * item, inner], bins[2 * item + 1, inner])
        add_bins(operand, waves, item, old, (middle[top, inner], updated[top, inner]), EDGE, rows)


def joint_rows_kernel(
    waves, updated, middle, head, behind, bins, begun, near, tail, operand, field, coef, mid,
):
    rows, width = updated.shape[1], updated.shape[2]
    planes = field.shape[0]
    corner = jnp.concatenate([behind[planes + BINS // 2], behind[planes + BINS // 2 + 1]], axis=1)
    strip = place_columns(corner, width)
    for n in range(planes):
        field[n, :EDGE, :] = head[n]
        field[n, EDGE:, :width] = behind[n]
        field[n, EDGE:, width:] = strip[n * EDGE : (n + 1) * EDGE]
    is_near = lax.broadcasted_iota(jnp.int32, (EDGE, width), 0) < HALO
    tops = {}

    def keep(k, whole, n, value):
        near[k * 9 + n] = value[:EDGE]
        at = (k * 9 + n) * HALO
        tail[at : at + HALO, :] = value[EDGE + HALO :]
        if n % 3 == 2:
            first = jnp.where(is_near, value[:EDGE], whole[n, :EDGE, :])
            last = jnp.where(is_near, whole[n, rows - EDGE :, :], value[EDGE:])
            tops.setdefault(n // 3, []).append((first, last))

    def keep_middle(n, value):
        mid[n] = value
        keep(1, middle, n, value[:, :width])

    def keep_updated(n, value):
        keep(0, updated, n, value)

    two_steps(field, coef, mid, keep_middle, keep_updated)

    operand[...] = begun[...]
    for item in range(BINS // 2):
        rest = behind[planes + item]
        starts, ends = zip(*tops[item % 3])
        old = (bins[2 * item, :EDGE], bins[2 * item + 1, :EDGE])
        add_bins(operand, waves, item, old, starts, 0, rows)
        old = tuple(
            jnp.where(is_near, bins[n, rows - EDGE :], other)
            for n, other in ((2 * item, pltpu.roll(rest, HALO, 0)), (2 * item + 1, rest))
        )
        add_bins(operand, waves, item, old, ends, rows - EDGE, rows)


def first_transform_kernel(received, table, tail, out, tail_out):
    tail_out[...] = tail[...]
    count, width = received.shape[0] // 3, received.shape[1]
    joined = jnp.concatenate([received[pl.ds(n, count, stride=3), :] for n in range(3)], axis=1)
    high, rest = halves(joined)
    both = jnp.dot(
        table[...], jnp.concatenate([high, rest, high], axis=0), preferred_element_type=jnp.float32
    )
    by_cos, by_sin = both[:count], both[count:]
    out[pl.ds(0, count, stride=3), :] = by_cos[:, :width] + by_sin[:, width : 2 * width]
    out[pl.ds(1, count, stride=3), :] = by_cos[:, width : 2 * width] - by_sin[:, :width]
    turned = pltpu.roll(by_sin[:, 2 * width :], width // 2, 1)
    low = lax.broadcasted_iota(jnp.int32, turned.shape, 1) < width // 2
    out[pl.ds(2, count, stride=3), :] = by_cos[:, 2 * width :] + jnp.where(low, turned, -turned)


def second_transform_kernel(received, matrix, out):
    items, parts, rows, width = out.shape
    half = width // 2
    count = received.shape[0] // 3
    low = lax.broadcasted_iota(jnp.int32, (rows, width), 1) < half
    real, imag = [], []
    for item in range(items):
        if item < 4:
            real.append(received[pl.ds(3 * item * rows, rows, stride=3), :])
            imag.append(received[pl.ds(3 * item * rows + 1, rows, stride=3), :])
        else:
            at = 3 * (item - 4) * rows + 2
            one = received[pl.ds(at, rows, stride=3), :]
            two = received[pl.ds(at + 6 * rows, rows, stride=3), :]
            real.append(jnp.where(low, one, pltpu.roll(two, half, 1)))
            imag.append(jnp.where(low, pltpu.roll(one, half, 1), two))
    joined = jnp.concatenate([jnp.concatenate(real, axis=1), jnp.concatenate(imag, axis=1)], axis=0)
    left, left_rest = halves(matrix[...])
    high, rest = halves(joined)
    waves = jnp.dot(
        jnp.concatenate([left, left, left_rest], axis=1),
        jnp.concatenate([high, rest, high], axis=0),
        preferred_element_type=jnp.float32,
    )
    for item in range(items):
        for part in range(parts):
            out[item, part] = waves[part * rows : (part + 1) * rows, item * width : (item + 1) * width]


def set_in_kernel(rows, count, updated, middle, near, tail, straight, turned, updated_out, middle_out, matrix):
    slot = lax.broadcasted_iota(jnp.int32, straight.shape, 1) % rows
    node = jnp.where(slot < rows - HALO, slot, slot - rows).astype(jnp.float32)
    place = lax.axis_index("gx").astype(jnp.float32)
    angle = node * place * (2.0 * np.pi / (rows * count))
    matrix[...] = straight[...] * jnp.cos(angle) + turned[...] * jnp.sin(angle)
    for k, (ref, out) in enumerate(((updated, updated_out), (middle, middle_out))):
        for n in range(ref.shape[0]):
            at = k * ref.shape[0] + n
            out[n, HALO:-HALO, :] = ref[n, HALO:-HALO, :]
            out[n, :HALO, :] = near[at, :HALO, :]
            out[n, -HALO:, :] = tail[at * HALO : (at + 1) * HALO, :]


def exchange(value):
    peers = lax.axis_size("gx")
    rows, width = value.shape
    shaped = value.reshape(peers, 1, rows // peers * width)
    return lax.all_to_all(shaped, "gx", split_axis=0, concat_axis=0, tiled=True).reshape(rows, width)


def exchange_gy(value):
    return lax.all_to_all(value, "gy", split_axis=0, concat_axis=0, tiled=True)


def pass_on(value, axis, step):
    peers = lax.axis_size(axis)
    return lax.ppermute(value, axis, [(i, (i + step) % peers) for i in range(peers)])


def f32(*shape):
    return jax.ShapeDtypeStruct(shape, jnp.float32)


def on_device(displacement, previous, moduli, density, bins, omega, phase):
    groups = lax.axis_size("gx")
    rows, width = density.shape[1:]
    items = bins.shape[0] * bins.shape[1]
    block = (rows, width)
    arrays = [a.reshape((-1,) + block) for a in (displacement, previous, moduli, density, bins)]
    planes = sum(a.shape[0] for a in arrays) - BINS
    packed = -(-planes * rows // width) * width
    peers = lax.axis_size("gy")
    vmem = pl.BlockSpec(memory_space=pltpu.VMEM)
    hbm = pl.BlockSpec(memory_space=pltpu.HBM)
    params = pltpu.CompilerParams(vmem_limit_bytes=48 * 1024 * 1024)
    wide = 2 * width

    sides, whole = pl.pallas_call(
        pack_columns_kernel,
        out_shape=(
            pltpu.VMEM((peers, HALO, packed), jnp.float32),
            pltpu.VMEM((planes,) + block, jnp.float32),
        ),
        in_specs=[hbm] * 4,
        out_specs=(vmem,) * 2,
        scratch_shapes=[pltpu.SemaphoreType.DMA((planes,))],
        compiler_params=pltpu.CompilerParams(vmem_limit_bytes=60 * 1024 * 1024),
    )(*arrays[:4])
    beside = exchange_gy(sides)
    edge = pl.pallas_call(
        pack_rows_kernel,
        out_shape=f32(planes + BINS // 2 + 2, EDGE, width),
        in_specs=[vmem] * 3,
        out_specs=vmem,
        compiler_params=params,
    )(whole, arrays[4], beside)
    edge, omega, phase = lax.optimization_barrier((edge, omega, phase))
    steps = np.arange(1, 3, dtype=np.float32)
    angles = (phase[None, :] + steps[:, None] * omega[None, :]).reshape(-1)
    angles = jnp.broadcast_to(angles[:, None], (angles.shape[0], width))
    behind = pass_on(edge, "gx", 1)
    updated, middle, head, waves, begun = pl.pallas_call(
        own_rows_kernel,
        out_shape=(f32(9, *block), f32(9, *block), f32(planes, EDGE, wide), f32(EDGE, width), f32(3 * groups, width)),
        in_specs=[vmem] * 4,
        out_specs=(vmem,) * 5,
        scratch_shapes=[
            pltpu.VMEM((planes, rows, wide), jnp.float32),
            pltpu.VMEM((3, 11, rows, wide), jnp.float32),
            pltpu.VMEM((packed, width), jnp.float32),
            pltpu.VMEM((9, rows, wide), jnp.float32),
        ],
        compiler_params=params,
        cost_estimate=pl.CostEstimate(flops=50_000_000, bytes_accessed=2_000_000, transcendentals=0),
    )(angles, whole, arrays[4], beside)
    near, tail, operand = pl.pallas_call(
        joint_rows_kernel,
        out_shape=(f32(18, EDGE, width), f32(18 * HALO, width), f32(3 * groups, width)),
        in_specs=[vmem] * 7,
        out_specs=(vmem,) * 3,
        scratch_shapes=[
            pltpu.VMEM((planes, 2 * EDGE, wide), jnp.float32),
            pltpu.VMEM((3, 11, 2 * EDGE, wide), jnp.float32),
            pltpu.VMEM((9, 2 * EDGE, wide), jnp.float32),
        ],
        compiler_params=params,
    )(waves, updated, middle, head, behind, arrays[4], begun)

    stacked = np.concatenate(fourier_tables(groups), axis=0)
    high = stacked.astype(ml_dtypes.bfloat16)
    rest = (stacked - high.astype(np.float64)).astype(ml_dtypes.bfloat16)
    table = jnp.asarray(np.concatenate([high, high, rest], axis=1))
    sections, tail = pl.pallas_call(
        first_transform_kernel,
        out_shape=(f32(3 * groups, width), f32(*tail.shape)),
        in_specs=[vmem] * 3,
        out_specs=(vmem,) * 2,
        compiler_params=params,
    )(exchange(operand), table, tail)
    scale = (groups * rows) ** -0.5
    c, s = (t * scale for t in fourier_tables(rows))
    straight = jnp.asarray(np.block([[c, s], [-s, c]]), jnp.float32)
    turned = jnp.asarray(np.block([[-s, c], [-c, -s]]), jnp.float32)
    updated, middle, matrix = pl.pallas_call(
        functools.partial(set_in_kernel, rows, groups),
        out_shape=(f32(9, *block), f32(9, *block), f32(2 * rows, 2 * rows)),
        in_specs=[vmem] * 6,
        out_specs=(vmem,) * 3,
        compiler_params=params,
        cost_estimate=pl.CostEstimate(flops=1_000_000, bytes_accessed=1_200_000, transcendentals=0),
    )(updated, middle, near, pass_on(tail, "gx", -1), straight, turned)
    spectrum = pl.pallas_call(
        second_transform_kernel,
        out_shape=f32(items, 2, *block),
        in_specs=[vmem] * 2,
        out_specs=vmem,
        compiler_params=params,
    )(exchange(sections), matrix)
    return (
        updated.reshape(displacement.shape),
        middle.reshape(displacement.shape),
        spectrum.reshape(bins.shape),
    )


def solution(mesh):
    placed = (
        P(None, None, "gx", "gy"),
        P(None, None, "gx", "gy"),
        P(None, None, "gx", "gy"),
        P(None, "gx", "gy"),
        P(None, None, None, "gx", "gy"),
        P(),
        P(),
    )
    return jax.shard_map(
        on_device,
        mesh=mesh,
        in_specs=placed,
        out_specs=(
            P(None, None, "gx", "gy"),
            P(None, None, "gx", "gy"),
            P(None, None, None, "gx", "gy"),
        ),
        check_vma=False,
    )
```

```python
import functools

import jax
import jax.numpy as jnp
import ml_dtypes
import numpy as np
from jax import lax
from jax.experimental import pallas as pl
from jax.experimental.pallas import tpu as pltpu
from jax.sharding import PartitionSpec as P

time_step = 0.03
HALO = 4
EDGE = 8
BINS = 12


def edge_columns(width):
    side = lax.broadcasted_iota(jnp.int32, (EDGE, width), 0)
    lane = lax.broadcasted_iota(jnp.int32, (EDGE, width), 1)
    return (lane == jnp.where(side < HALO, side, side + width - EDGE)).astype(jnp.float32).astype(jnp.bfloat16)


def fourier_tables(length):
    index = np.arange(length)
    angle = 2.0 * np.pi * (index[:, None] * index[None, :] % length) / length
    return np.cos(angle), np.sin(angle)


def halves(value):
    high = value.astype(jnp.bfloat16)
    return high, (value - high.astype(jnp.float32)).astype(jnp.bfloat16)


def pick_columns(rows):
    width = rows.shape[1]
    turned = [rows[at : at + width].T for at in range(0, rows.shape[0], width)]
    return jnp.concatenate([jnp.concatenate([t[:HALO], t[-HALO:]], axis=0) for t in turned], axis=1)


def row_tiles(whole):
    planes, rows, width = whole.shape
    return jnp.concatenate(
        [whole[:, at : at + EDGE].reshape(planes * EDGE, width) for at in range(0, rows, EDGE)], axis=0
    )


def pack_columns_kernel(disp, prev, moduli, density, out, whole, sems):
    copies = []
    start = 0
    for n, ref in enumerate((disp, prev, moduli, density)):
        copies.append(pltpu.make_async_copy(ref, whole.at[pl.ds(start, ref.shape[0])], sems.at[n]))
        start += ref.shape[0]
    for copy in copies:
        copy.start()
    for copy in copies:
        copy.wait()
    peers, _, total = out.shape
    rows = row_tiles(whole[...])
    fill = jnp.zeros((total - rows.shape[0], rows.shape[1]), jnp.float32)
    packed = pick_columns(jnp.concatenate([rows, fill], axis=0))
    me = lax.axis_index("gy")
    for step in range(peers):
        slot = lax.rem(me + step, peers)
        if step in (1, peers - 1):
            out[slot] = packed[HALO:] if step == 1 else packed[:HALO]
        else:
            out[slot] = jnp.zeros(out.shape[1:], jnp.float32)


def both_sides(beside):
    peers = beside.shape[0]
    me = lax.axis_index("gy")
    return jnp.concatenate([beside[lax.rem(me + 1, peers)], beside[lax.rem(me + peers - 1, peers)]], axis=0)


def place_columns(both, width):
    chosen = edge_columns(width)
    return lax.dot_general(
        jnp.concatenate(halves(both), axis=0),
        jnp.concatenate([chosen, chosen], axis=0),
        (((0,), (0,)), ((), ())),
        preferred_element_type=jnp.float32,
    )


def pack_rows_kernel(whole, bins, beside, out):
    start, rows, width = whole.shape
    for n in range(start):
        out[n] = whole[n, -EDGE:, :]
    for n in range(BINS):
        at = n % 2 * HALO
        out[start + n // 2, at : at + HALO, :] = bins[n, -HALO:, :]
    both = both_sides(beside)
    first = start * (rows - EDGE)
    base = first // width * width
    corner = pltpu.roll(both[:, base : base + 2 * width], 2 * width - (first - base), 1)
    out[start + BINS // 2] = corner[:, :width]
    out[start + BINS // 2 + 1] = corner[:, width:]


def shift(value, amount, axis):
    return pltpu.roll(value, (-amount) % value.shape[axis], axis)


def slopes(value, axis, even):
    ahead, ahead2 = shift(value, 1, axis), shift(value, 2, axis)
    back, back2 = shift(value, -1, axis), shift(value, -2, axis)
    right = jnp.where(even, 4.0 * ahead - 3.0 * value - ahead2, ahead - back)
    left = 3.0 * value - 4.0 * back + back2
    return right, left, jnp.where(even, right + left, right)


def spread(right, left, axis, even):
    ahead = jnp.where(even, -4.0 * left, -right)
    back = jnp.where(even, 4.0 * right, right)
    ahead = ahead + shift(jnp.where(even, left, 0.0), 1, axis)
    back = back - shift(jnp.where(even, right, 0.0), -1, axis)
    own = jnp.where(even, 3.0 * (left - right), 0.0)
    return own + shift(ahead, 1, axis) + shift(back, -1, axis)


def spread_z(layers):
    a, b, c = layers
    return c - b - 3.0 * a, 4.0 * (a - c), b - a + 3.0 * c


def two_steps(field, coef, mid, keep_middle, keep_updated):
    _, tall, wide = field.shape
    width = wide // 2

    def tiled(tile, shape=(tall, wide)):
        line = jnp.concatenate([tile] * (shape[1] // tile.shape[1]), axis=1)
        return jnp.concatenate([line] * (shape[0] // tile.shape[0]), axis=0)

    tile_x, tile_y = (lax.broadcasted_iota(jnp.int32, (8, 128), axis) % 2 for axis in range(2))
    near_x, near_y = tiled(tile_x), tiled(tile_y)
    two_x, two_y = 2.0 - near_x.astype(jnp.float32), 2.0 - near_y.astype(jnp.float32)
    weight = (1.0 / 3.0 + near_x.astype(jnp.float32)) * (1.0 / 3.0 + near_y.astype(jnp.float32)) / 8.0
    lane = lax.broadcasted_iota(jnp.int32, (tall, wide), 1)
    unused = (lane >= width + HALO) & (lane < wide - HALO)
    for layer in range(3):
        weight_z = 4.0 / 3.0 if layer == 1 else 1.0 / 3.0
        here = weight * weight_z
        lam = field[18 + layer] * here
        mu = field[21 + layer] * here
        mu_x, mu_y = mu * two_x, mu * two_y
        mu_xy = mu_x * two_y
        lam_x, lam_y = lam * two_x, lam * two_y
        mass = jnp.where(unused, 1.0, field[24 + layer]) * (here * two_x * two_y)
        for n, value in enumerate(
            (lam, lam_x, lam_y, lam_x + 2.0 * mu_x, lam_y + 2.0 * mu_y, lam_x * two_y + 2.0 * mu_xy,
             mu, mu_x, mu_y, mu_xy, time_step * time_step / mass)
        ):
            coef[layer, n] = value

    def advance(source, older, store, own):
        out_width = width if own else wide
        even_x, even_y = near_x == 0, near_y == 0
        even_xs = even_x[:, :out_width]

        def for_x(value):
            return value[:, :out_width]

        def along_x(right, left):
            return spread(right, left, 0, even_xs)

        def along_y(right, left):
            return spread(right, left, 1, even_y)[:, :out_width]

        forces = [[None] * 3 for _ in range(3)]
        z_terms = [[None] * 3 for _ in range(3)]
        for layer in range(3):
            value = [source(c * 3 + layer) for c in range(3)]
            grad_z = []
            for c in range(3):
                a, b, d = (source(c * 3 + n) for n in range(3))
                if layer == 0:
                    grad_z.append(4.0 * b - 3.0 * a - d)
                elif layer == 1:
                    grad_z.append(d - a)
                else:
                    grad_z.append(a - 4.0 * b + 3.0 * d)
            lam, lam_x, lam_y, stiff_x, stiff_y, stiff_z, mu, mu_x, mu_y, mu_xy = (
                coef[layer, n] for n in range(10)
            )
            rx, lx, sx = zip(*(slopes(v, 0, even_x) for v in value))
            ry, ly, sy = zip(*(slopes(v, 1, even_y) for v in value))
            common = for_x(lam_y * grad_z[2] + lam * sy[1])
            scale = for_x(stiff_y)
            force_x = along_x(scale * for_x(rx[0]) + common, scale * for_x(lx[0]) + common)
            common = for_x(mu * sy[0])
            scale = for_x(mu_y)
            force_y = along_x(scale * for_x(rx[1]) + common, scale * for_x(lx[1]) + common)
            common = for_x(grad_z[0])
            force_z = along_x(scale * (for_x(rx[2]) + common), scale * (for_x(lx[2]) + common))
            common = (lam_x * grad_z[2] + lam * sx[0])
            scale = (stiff_x)
            force_y += along_y(scale * (ry[1]) + common, scale * (ly[1]) + common)
            common = (mu * sx[1])
            scale = (mu_x)
            force_x += along_y(scale * (ry[0]) + common, scale * (ly[0]) + common)
            common = (grad_z[1])
            force_z += along_y(scale * ((ry[2]) + common), scale * ((ly[2]) + common))
            for c, value in enumerate((force_x, force_y, force_z)):
                forces[c][layer] = value
            z_terms[0][layer] = for_x(mu_xy * grad_z[0] + mu_y * sx[2])
            z_terms[1][layer] = for_x(mu_xy * grad_z[1] + mu_x * sy[2])
            z_terms[2][layer] = for_x(lam_y * sx[0] + lam_x * sy[1] + stiff_z * grad_z[2])
        for c in range(3):
            along_z = spread_z(z_terms[c])
            for layer in range(3):
                n = c * 3 + layer
                total = (forces[c][layer] + along_z[layer]) * for_x(coef[layer, 10])
                store(n, 2.0 * for_x(source(n)) - for_x(older(n)) - total)

    advance(lambda n: field[n], lambda n: field[9 + n], keep_middle, False)
    advance(lambda n: mid[n], lambda n: field[n], keep_updated, True)


def add_bins(operand, waves, item, old, tops, first, rows):
    b = item // 3
    one, two = tops
    count, width = one.shape
    half = width // 2
    real = old[0] + waves[b : b + 1] * one + waves[2 + b : 3 + b] * two
    imag = old[1] - waves[4 + b : 5 + b] * one - waves[6 + b : 7 + b] * two
    if item < 4:
        at = 3 * (item * rows + first)
        operand[pl.ds(at, count, stride=3), :] = real
        operand[pl.ds(at + 1, count, stride=3), :] = imag
    else:
        low = lax.broadcasted_iota(jnp.int32, (count, width), 1) < half
        at = 3 * ((item - 4) * rows + first) + 2
        operand[pl.ds(at, count, stride=3), :] = jnp.where(low, real, pltpu.roll(imag, half, 1))
        operand[pl.ds(at + 6 * rows, count, stride=3), :] = jnp.where(low, pltpu.roll(real, half, 1), imag)


def own_rows_kernel(
    angles, whole, bins, beside, updated, middle, head, waves, operand, field, coef, strip, mid,
):
    planes, rows, width = whole.shape
    waves[: angles.shape[0], :] = jnp.cos(angles[...])
    waves[angles.shape[0] :, :] = jnp.sin(angles[...])
    strip[...] = place_columns(both_sides(beside), width)
    for n in range(planes):
        field[n, :, :width] = whole[n]
        for tile in range(rows // EDGE):
            at = (tile * planes + n) * EDGE
            field[n, tile * EDGE : (tile + 1) * EDGE, width:] = strip[at : at + EDGE, :]
        head[n] = field[n, :EDGE, :]

    def keep_middle(n, value):
        mid[n] = value
        middle[n] = value[:, :width]

    def keep_updated(n, value):
        updated[n] = value

    two_steps(field, coef, mid, keep_middle, keep_updated)
    inner = slice(EDGE, rows - EDGE)
    for item in range(BINS // 2):
        top = item % 3 * 3 + 2
        old = (bins[2 * item, inner], bins[2 * item + 1, inner])
        add_bins(operand, waves, item, old, (middle[top, inner], updated[top, inner]), EDGE, rows)


def joint_rows_kernel(
    waves, updated, middle, head, behind, bins, begun, near, tail, operand, field, coef, mid,
):
    rows, width = updated.shape[1], updated.shape[2]
    planes = field.shape[0]
    corner = jnp.concatenate([behind[planes + BINS // 2], behind[planes + BINS // 2 + 1]], axis=1)
    strip = place_columns(corner, width)
    for n in range(planes):
        field[n, :EDGE, :] = head[n]
        field[n, EDGE:, :width] = behind[n]
        field[n, EDGE:, width:] = strip[n * EDGE : (n + 1) * EDGE]
    is_near = lax.broadcasted_iota(jnp.int32, (EDGE, width), 0) < HALO
    tops = {}

    def keep(k, whole, n, value):
        near[k * 9 + n] = value[:EDGE]
        at = (k * 9 + n) * HALO
        tail[at : at + HALO, :] = value[EDGE + HALO :]
        if n % 3 == 2:
            first = jnp.where(is_near, value[:EDGE], whole[n, :EDGE, :])
            last = jnp.where(is_near, whole[n, rows - EDGE :, :], value[EDGE:])
            tops.setdefault(n // 3, []).append((first, last))

    def keep_middle(n, value):
        mid[n] = value
        keep(1, middle, n, value[:, :width])

    def keep_updated(n, value):
        keep(0, updated, n, value)

    two_steps(field, coef, mid, keep_middle, keep_updated)

    operand[...] = begun[...]
    for item in range(BINS // 2):
        rest = behind[planes + item]
        starts, ends = zip(*tops[item % 3])
        old = (bins[2 * item, :EDGE], bins[2 * item + 1, :EDGE])
        add_bins(operand, waves, item, old, starts, 0, rows)
        old = tuple(
            jnp.where(is_near, bins[n, rows - EDGE :], other)
            for n, other in ((2 * item, pltpu.roll(rest, HALO, 0)), (2 * item + 1, rest))
        )
        add_bins(operand, waves, item, old, ends, rows - EDGE, rows)


def first_transform_kernel(received, table, tail, out, tail_out):
    tail_out[...] = tail[...]
    count, width = received.shape[0] // 3, received.shape[1]
    joined = jnp.concatenate([received[pl.ds(n, count, stride=3), :] for n in range(3)], axis=1)
    high, rest = halves(joined)
    both = jnp.dot(
        table[...], jnp.concatenate([high, rest, high], axis=0), preferred_element_type=jnp.float32
    )
    by_cos, by_sin = both[:count], both[count:]
    out[pl.ds(0, count, stride=3), :] = by_cos[:, :width] + by_sin[:, width : 2 * width]
    out[pl.ds(1, count, stride=3), :] = by_cos[:, width : 2 * width] - by_sin[:, :width]
    turned = pltpu.roll(by_sin[:, 2 * width :], width // 2, 1)
    low = lax.broadcasted_iota(jnp.int32, turned.shape, 1) < width // 2
    out[pl.ds(2, count, stride=3), :] = by_cos[:, 2 * width :] + jnp.where(low, turned, -turned)


def second_transform_kernel(received, matrix, out):
    items, parts, rows, width = out.shape
    half = width // 2
    count = received.shape[0] // 3
    low = lax.broadcasted_iota(jnp.int32, (rows, width), 1) < half
    real, imag = [], []
    for item in range(items):
        if item < 4:
            real.append(received[pl.ds(3 * item * rows, rows, stride=3), :])
            imag.append(received[pl.ds(3 * item * rows + 1, rows, stride=3), :])
        else:
            at = 3 * (item - 4) * rows + 2
            one = received[pl.ds(at, rows, stride=3), :]
            two = received[pl.ds(at + 6 * rows, rows, stride=3), :]
            real.append(jnp.where(low, one, pltpu.roll(two, half, 1)))
            imag.append(jnp.where(low, pltpu.roll(one, half, 1), two))
    joined = jnp.concatenate([jnp.concatenate(real, axis=1), jnp.concatenate(imag, axis=1)], axis=0)
    left, left_rest = halves(matrix[...])
    high, rest = halves(joined)
    waves = jnp.dot(
        jnp.concatenate([left, left, left_rest], axis=1),
        jnp.concatenate([high, rest, high], axis=0),
        preferred_element_type=jnp.float32,
    )
    for item in range(items):
        for part in range(parts):
            out[item, part] = waves[part * rows : (part + 1) * rows, item * width : (item + 1) * width]


def set_in_kernel(rows, count, updated, middle, near, tail, straight, turned, updated_out, middle_out, matrix):
    slot = lax.broadcasted_iota(jnp.int32, straight.shape, 1) % rows
    node = jnp.where(slot < rows - HALO, slot, slot - rows).astype(jnp.float32)
    place = lax.axis_index("gx").astype(jnp.float32)
    angle = node * place * (2.0 * np.pi / (rows * count))
    matrix[...] = straight[...] * jnp.cos(angle) + turned[...] * jnp.sin(angle)
    for k, (ref, out) in enumerate(((updated, updated_out), (middle, middle_out))):
        for n in range(ref.shape[0]):
            at = k * ref.shape[0] + n
            out[n, HALO:-HALO, :] = ref[n, HALO:-HALO, :]
            out[n, :HALO, :] = near[at, :HALO, :]
            out[n, -HALO:, :] = tail[at * HALO : (at + 1) * HALO, :]


def exchange(value):
    peers = lax.axis_size("gx")
    rows, width = value.shape
    shaped = value.reshape(peers, 1, rows // peers * width)
    return lax.all_to_all(shaped, "gx", split_axis=0, concat_axis=0, tiled=True).reshape(rows, width)


def exchange_gy(value):
    return lax.all_to_all(value, "gy", split_axis=0, concat_axis=0, tiled=True)


def pass_on(value, axis, step):
    peers = lax.axis_size(axis)
    return lax.ppermute(value, axis, [(i, (i + step) % peers) for i in range(peers)])


def f32(*shape):
    return jax.ShapeDtypeStruct(shape, jnp.float32)


def on_device(displacement, previous, moduli, density, bins, omega, phase):
    groups = lax.axis_size("gx")
    rows, width = density.shape[1:]
    items = bins.shape[0] * bins.shape[1]
    block = (rows, width)
    arrays = [a.reshape((-1,) + block) for a in (displacement, previous, moduli, density, bins)]
    planes = sum(a.shape[0] for a in arrays) - BINS
    packed = -(-planes * rows // width) * width
    peers = lax.axis_size("gy")
    vmem = pl.BlockSpec(memory_space=pltpu.VMEM)
    hbm = pl.BlockSpec(memory_space=pltpu.HBM)
    params = pltpu.CompilerParams(vmem_limit_bytes=48 * 1024 * 1024)
    wide = 2 * width

    sides, whole = pl.pallas_call(
        pack_columns_kernel,
        out_shape=(
            pltpu.VMEM((peers, HALO, packed), jnp.float32),
            pltpu.VMEM((planes,) + block, jnp.float32),
        ),
        in_specs=[hbm] * 4,
        out_specs=(vmem,) * 2,
        scratch_shapes=[pltpu.SemaphoreType.DMA((4,))],
        compiler_params=pltpu.CompilerParams(vmem_limit_bytes=60 * 1024 * 1024),
    )(*arrays[:4])
    beside = exchange_gy(sides)
    edge = pl.pallas_call(
        pack_rows_kernel,
        out_shape=f32(planes + BINS // 2 + 2, EDGE, width),
        in_specs=[vmem] * 3,
        out_specs=vmem,
        compiler_params=params,
    )(whole, arrays[4], beside)
    edge, omega, phase = lax.optimization_barrier((edge, omega, phase))
    steps = np.arange(1, 3, dtype=np.float32)
    angles = (phase[None, :] + steps[:, None] * omega[None, :]).reshape(-1)
    angles = jnp.broadcast_to(angles[:, None], (angles.shape[0], width))
    behind = pass_on(edge, "gx", 1)
    updated, middle, head, waves, begun = pl.pallas_call(
        own_rows_kernel,
        out_shape=(f32(9, *block), f32(9, *block), f32(planes, EDGE, wide), f32(EDGE, width), f32(3 * groups, width)),
        in_specs=[vmem] * 4,
        out_specs=(vmem,) * 5,
        scratch_shapes=[
            pltpu.VMEM((planes, rows, wide), jnp.float32),
            pltpu.VMEM((3, 11, rows, wide), jnp.float32),
            pltpu.VMEM((packed, width), jnp.float32),
            pltpu.VMEM((9, rows, wide), jnp.float32),
        ],
        compiler_params=params,
        cost_estimate=pl.CostEstimate(flops=50_000_000, bytes_accessed=2_000_000, transcendentals=0),
    )(angles, whole, arrays[4], beside)
    near, tail, operand = pl.pallas_call(
        joint_rows_kernel,
        out_shape=(f32(18, EDGE, width), f32(18 * HALO, width), f32(3 * groups, width)),
        in_specs=[vmem] * 7,
        out_specs=(vmem,) * 3,
        scratch_shapes=[
            pltpu.VMEM((planes, 2 * EDGE, wide), jnp.float32),
            pltpu.VMEM((3, 11, 2 * EDGE, wide), jnp.float32),
            pltpu.VMEM((9, 2 * EDGE, wide), jnp.float32),
        ],
        compiler_params=params,
    )(waves, updated, middle, head, behind, arrays[4], begun)

    stacked = np.concatenate(fourier_tables(groups), axis=0)
    high = stacked.astype(ml_dtypes.bfloat16)
    rest = (stacked - high.astype(np.float64)).astype(ml_dtypes.bfloat16)
    table = jnp.asarray(np.concatenate([high, high, rest], axis=1))
    sections, tail = pl.pallas_call(
        first_transform_kernel,
        out_shape=(f32(3 * groups, width), f32(*tail.shape)),
        in_specs=[vmem] * 3,
        out_specs=(vmem,) * 2,
        compiler_params=params,
    )(exchange(operand), table, tail)
    scale = (groups * rows) ** -0.5
    c, s = (t * scale for t in fourier_tables(rows))
    straight = jnp.asarray(np.block([[c, s], [-s, c]]), jnp.float32)
    turned = jnp.asarray(np.block([[-s, c], [-c, -s]]), jnp.float32)
    updated, middle, matrix = pl.pallas_call(
        functools.partial(set_in_kernel, rows, groups),
        out_shape=(f32(9, *block), f32(9, *block), f32(2 * rows, 2 * rows)),
        in_specs=[vmem] * 6,
        out_specs=(vmem,) * 3,
        compiler_params=params,
        cost_estimate=pl.CostEstimate(flops=1_000_000, bytes_accessed=1_200_000, transcendentals=0),
    )(updated, middle, near, pass_on(tail, "gx", -1), straight, turned)
    spectrum = pl.pallas_call(
        second_transform_kernel,
        out_shape=f32(items, 2, *block),
        in_specs=[vmem] * 2,
        out_specs=vmem,
        compiler_params=params,
    )(exchange(sections), matrix)
    return (
        updated.reshape(displacement.shape),
        middle.reshape(displacement.shape),
        spectrum.reshape(bins.shape),
    )


def solution(mesh):
    placed = (
        P(None, None, "gx", "gy"),
        P(None, None, "gx", "gy"),
        P(None, None, "gx", "gy"),
        P(None, "gx", "gy"),
        P(None, None, None, "gx", "gy"),
        P(),
        P(),
    )
    return jax.shard_map(
        on_device,
        mesh=mesh,
        in_specs=placed,
        out_specs=(
            P(None, None, "gx", "gy"),
            P(None, None, "gx", "gy"),
            P(None, None, None, "gx", "gy"),
        ),
        check_vma=False,
    )
```
